32 devices in a mesh: rows: 8 (over z, x), blk: 4 (over y, core).
Axes of the slice: x: 2, y: 2, z: 4, core: 2. Of those that a mesh axis runs over, the one named last changes fastest.
Arguments:
- tokens: bfloat16 [64, 512, 768], P('rows', 'blk'), may hold values from -6 to 6
- lengths: int32 [64, 8], P('rows'), may hold values from 1 to 385, 512 in all within a row
- input_weight: bfloat16 [768, 2304], replicated, may hold values from -0.21875 to 0.21875
- query_bias: float32 [768], replicated, may hold values from -3 to 3
- value_bias: float32 [768], replicated, may hold values from -3 to 3
- output_weight: bfloat16 [768, 768], replicated, may hold values from -1.75 to 1.75
- output_bias: float32 [768], replicated, may hold values from -3 to 3
- first_gain: float32 [768], replicated, may hold values from 0.1 to 1.9
- first_shift: float32 [768], replicated, may hold values from -3 to 3
- up_weight: bfloat16 [768, 3072], replicated, may hold values from -0.21875 to 0.21875
- up_bias: float32 [3072], replicated, may hold values from -3 to 3
- down_weight: bfloat16 [3072, 768], replicated, may hold values from -0.109375 to 0.109375
- down_bias: float32 [768], replicated, may hold values from -3 to 3
- second_gain: float32 [768], replicated, may hold values from 0.1 to 1.9
- second_shift: float32 [768], replicated, may hold values from -3 to 3
- out_grad: bfloat16 [64, 512, 768], P('rows', 'blk'), may hold values from -6 to 6
- pool_grad: bfloat16 [64, 8, 768], P('rows'), may hold values from -96 to 96
Outputs:
- hidden_out: bfloat16 [64, 512, 768], P('rows', 'blk')
- pooled: float32 [64, 8, 768], P('rows')
- tokens_grad: float32 [64, 512, 768], P('rows', 'blk')
- input_weight_grad: float32 [768, 2304], replicated
- query_bias_grad: float32 [768], replicated
- value_bias_grad: float32 [768], replicated
- output_weight_grad: float32 [768, 768], replicated
- output_bias_grad: float32 [768], replicated
- first_gain_grad: float32 [768], replicated
- first_shift_grad: float32 [768], replicated
- up_weight_grad: float32 [768, 3072], replicated
- up_bias_grad: float32 [3072], replicated
- down_weight_grad: float32 [3072, 768], replicated
- down_bias_grad: float32 [768], replicated
- second_gain_grad: float32 [768], replicated
- second_shift_grad: float32 [768], replicated
The draws below stay inside these ranges and needn't reach their ends.
Inputs may be any that keep to these rules, and one draw needn't show every extreme that they name: Each row's lengths sum to 512.
All inputs are finite; a program needn't handle non-finite values.
Results may differ from the reference program's by a relative error of at most 0.01.
Values may be sent and summed in bfloat16 or wider, within the bound.
No kernel may reach another device: no remote copies, remote signals or barrier semaphores. Data moves between devices by JAX's collectives and lax.ppermute only.
A program may use at most 256 MiB of HBM per device.

```python
import math
import jax
import jax.numpy as jnp
import numpy as np
from jax import lax

D = 768
H = 12
DH = 64
FF = 3072
SEQUENCE_LENGTH = 512
NSEG = 8
SEQS = 64
LONGEST = 385


def level_of(key, extent, cuts, least, top_value):
    factor_of = 1.0
    for axis_at, shards_of in cuts:
        heights = jax.random.uniform(jax.random.fold_in(jax.random.fold_in(key, 6), axis_at), (shards_of,), jnp.float32, least / len(cuts), top_value / len(cuts))
        factor_of = factor_of * jnp.repeat(jnp.exp(heights), extent[axis_at] // shards_of).reshape((-1,) + (1,) * (len(extent) - 1 - axis_at))
    return factor_of


def profile(number_of, total, most, skew):
    loads = [(1 << 20) // math.isqrt(grade ** skew) + 1 for grade in range(2, number_of + 1)]
    spare, holding = total - most - (number_of - 1), [1] * (number_of - 1)
    while spare > 0:
        movable = [i for i in range(number_of - 1) if holding[i] < most]
        pool, left = sum([loads[i] for i in movable]), spare
        for i in movable:
            extra = min(most - holding[i], max(1, left * loads[i] // pool), spare)
            holding[i] = holding[i] + extra
            spare = spare - extra
    return np.array([most] + holding)


def ragged_sizes(key, count, total, limit, skew):
    if count == 2:
        one = jax.random.randint(key, (), max(1, total - limit), min(limit, total - 1) + 1)
        return jnp.stack([one, total - one])
    sizes = jnp.asarray(profile(count, total, limit, skew), jnp.int32)
    twos = (count - 1) // 2
    giver, sink = sizes[1:1 + 2 * twos:2], sizes[2:2 + 2 * twos:2]
    room = jnp.minimum(giver - 1, limit - sink)
    shifted = jax.random.randint(jax.random.fold_in(key, 1), (twos,), 0, 1 << 20) % (room + 1)
    sizes = sizes.at[1:1 + 2 * twos:2].set(giver - shifted).at[2:2 + 2 * twos:2].set(sink + shifted)
    return sizes[jax.random.permutation(jax.random.fold_in(key, 2), count)]


def normal_values(own_key, shape, scale, limit, shards=(), kind=jnp.bfloat16):
    drawn = scale * jax.random.normal(own_key, shape, jnp.float32)
    if shards:
        drawn = drawn * level_of(own_key, shape, shards, -0.22, 0.18)
    return jnp.clip(drawn, -limit, limit).astype(kind)


def setup_inputs(seed: int = 0) -> dict:
    key_list = jax.random.split(jax.random.key(seed), 18)
    return {
        "tokens": normal_values(key_list[0], (SEQS, SEQUENCE_LENGTH, D), 1.0, 6.0, ((0, 8), (1, 4))),
        "lengths": jax.vmap(lambda own: ragged_sizes(own, NSEG, SEQUENCE_LENGTH, LONGEST, 0))(jax.random.split(key_list[1], SEQS)).reshape((SEQS, NSEG)).astype(jnp.int32),
        "input_weight": normal_values(key_list[2], (D, 3 * D), D ** -0.5, 0.21875),
        "query_bias": normal_values(key_list[3], (D,), 0.5, 3.0, (), jnp.float32),
        "value_bias": normal_values(key_list[4], (D,), 0.5, 3.0, (), jnp.float32),
        "output_weight": normal_values(key_list[5], (D, D), (D // 64) ** -0.5, 1.75),
        "output_bias": normal_values(key_list[6], (D,), 0.5, 3.0, (), jnp.float32),
        "first_gain": jnp.clip(1.0 + 0.18 * jax.random.normal(key_list[7], (D,), jnp.float32), 0.1, 1.9),
        "first_shift": normal_values(key_list[8], (D,), 0.5, 3.0, (), jnp.float32),
        "up_weight": normal_values(key_list[9], (D, FF), D ** -0.5, 0.21875),
        "up_bias": normal_values(key_list[10], (FF,), 0.5, 3.0, (), jnp.float32),
        "down_weight": normal_values(key_list[11], (FF, D), FF ** -0.5, 0.109375),
        "down_bias": normal_values(key_list[12], (D,), 0.5, 3.0, (), jnp.float32),
        "second_gain": jnp.clip(1.0 + 0.18 * jax.random.normal(key_list[13], (D,), jnp.float32), 0.1, 1.9),
        "second_shift": normal_values(key_list[14], (D,), 0.5, 3.0, (), jnp.float32),
        "out_grad": normal_values(key_list[15], (SEQS, SEQUENCE_LENGTH, D), 1.0, 6.0, ((0, 8), (1, 4))),
        "pool_grad": normal_values(key_list[16], (SEQS, NSEG, D), (SEQUENCE_LENGTH // (4 * NSEG)), 96.0, ((0, 8),)),
    }


@jax.custom_vjp
def low(v):
    return lax.optimization_barrier(v.astype(jnp.bfloat16)).astype(jnp.float32)

@jax.custom_vjp
def low_back(v):
    return v

def low_keep(v):
    return (low(v), None)

def low_pass(kept, grad):
    return (grad,)

def back_keep(v):
    return (v, None)

def back_low(kept, grad):
    return (low(grad),)
low.defvjp(low_keep, low_pass)
low_back.defvjp(back_keep, back_low)
FINEST_PRECISION = lax.Precision.HIGHEST
NORM_EPS = 1e-12
MASKED = -1000000000.0

def layer_norm(hidden, gain, shift):
    center = hidden - lax.optimization_barrier(jnp.mean(hidden, axis=-1, keepdims=True))
    spread = lax.optimization_barrier(jnp.mean(center * center, axis=-1, keepdims=True))
    return center * lax.rsqrt(spread + NORM_EPS) * gain + shift

def segment_of(lengths, start, count):
    ends = jnp.cumsum(lengths, axis=-1).astype(jnp.int32)
    places = start + jnp.arange(count, dtype=jnp.int32)
    return lax.optimization_barrier(jnp.sum((places[None, :, None] >= ends[:, None, :]).astype(jnp.int32), axis=-1)).astype(jnp.int32)

def layer(params, inputs, labels):
    input_weight, query_bias, value_bias, output_weight, output_bias, first_gain, first_shift, up_weight, up_bias, down_weight, down_bias, second_gain, second_shift = params
    group, length = (inputs.shape[0], inputs.shape[1])
    bias = jnp.concatenate([query_bias, jnp.zeros_like(query_bias), value_bias])
    packed = low(low_back(jnp.einsum('gld,de->gle', inputs, input_weight, precision=FINEST_PRECISION) + bias))
    queries = packed[..., :D].reshape(group, length, H, DH)
    key_heads = packed[..., D:2 * D].reshape(group, length, H, DH)
    value_heads = packed[..., 2 * D:].reshape(group, length, H, DH)
    scores = low_back(jnp.einsum('gqhe,gkhe->ghqk', queries, key_heads, precision=FINEST_PRECISION) * DH ** (-0.5))
    same = labels[:, None, :, None] == labels[:, None, None, :]
    scores = jnp.where(same, scores, MASKED)
    top = lax.optimization_barrier(jnp.max(scores, axis=-1, keepdims=True))
    weights = jnp.exp(scores - top)
    weights = weights / lax.optimization_barrier(jnp.sum(weights, axis=-1, keepdims=True))
    mixed = jnp.einsum('ghqk,gkhe->gqhe', low(weights), value_heads, precision=FINEST_PRECISION)
    mixed = low(low_back(mixed.reshape(group, length, D)))
    branch = low_back(jnp.einsum('gld,de->gle', mixed, output_weight, precision=FINEST_PRECISION) + output_bias)
    first = layer_norm(inputs + branch, first_gain, first_shift)
    inner = low_back(jnp.einsum('gld,df->glf', low(first), up_weight, precision=FINEST_PRECISION) + up_bias)
    active = low(jax.nn.gelu(inner, approximate=False))
    outer = low_back(jnp.einsum('glf,fd->gld', active, down_weight, precision=FINEST_PRECISION) + down_bias)
    return layer_norm(first + outer, second_gain, second_shift)

def pooled_of(layer_result, labels, lengths):
    segment_indicator = (labels[..., None] == jnp.arange(NSEG, dtype=jnp.int32)).astype(jnp.float32)
    segment_totals = jnp.einsum('mew,met->mwt', segment_indicator, layer_result, precision=FINEST_PRECISION)
    return segment_totals / lengths.astype(jnp.float32)[..., None]

def reference(tokens, lengths, input_weight, query_bias, value_bias, output_weight, output_bias, first_gain, first_shift, up_weight, up_bias, down_weight, down_bias, second_gain, second_shift, out_grad, pool_grad):
    params = tuple((item.astype(jnp.float32) for item in (input_weight, query_bias, value_bias, output_weight, output_bias, first_gain, first_shift, up_weight, up_bias, down_weight, down_bias, second_gain, second_shift)))
    group = 8 if SEQS % 8 == 0 else 1
    count = SEQS // group
    labels = segment_of(lengths, 0, SEQUENCE_LENGTH)

    def grouped(array):
        return array.reshape((count, group) + array.shape[1:])

    def one_group(carry, item):
        inputs, labels_here, lengths_here, result_grad, pooled_grad = item

        def forward(weights, values_in):
            layer_result = layer(weights, values_in, labels_here)
            return (layer_result, pooled_of(layer_result, labels_here, lengths_here))
        (layer_result, pooled), pull = jax.vjp(forward, params, inputs)
        grad_params, grad_inputs = pull((result_grad, pooled_grad))
        carry = tuple((total + part for total, part in zip(carry, grad_params)))
        return (carry, (layer_result.astype(jnp.bfloat16), pooled, grad_inputs))
    zeros = tuple((jnp.zeros(item.shape, jnp.float32) for item in params))
    grads, (outputs, pooled, grad_tokens) = lax.scan(one_group, zeros, (grouped(tokens.astype(jnp.float32)), grouped(labels), grouped(lengths), grouped(out_grad.astype(jnp.float32)), grouped(pool_grad.astype(jnp.float32))))
    return (outputs.reshape(SEQS, SEQUENCE_LENGTH, D), pooled.reshape(SEQS, NSEG, D), grad_tokens.reshape(SEQS, SEQUENCE_LENGTH, D), grads[0], grads[1], grads[2], grads[3], grads[4], grads[5], grads[6], grads[7], grads[8], grads[9], grads[10], grads[11], grads[12])
```

```python
import functools
import jax
import jax.numpy as jnp
from jax import lax
from jax.experimental import pallas as pl
from jax.experimental.pallas import tpu as pltpu
from jax.sharding import PartitionSpec as P

D = 768
H = 12
DH = 64
FF = 3072
NSEG = 8
PAIR = 2 * DH
NORM_EPS = 1e-12
BIG = 1e9
BF = jnp.bfloat16
F32 = jnp.float32
CHUNK = 512
VMEM_LIMIT = 60 * 1024 * 1024


def nn(a, b):
    return lax.dot_general(a, b, (((1,), (0,)), ((), ())), preferred_element_type=F32)


def nt(a, b):
    return lax.dot_general(a, b, (((1,), (1,)), ((), ())), preferred_element_type=F32)


def tn(a, b):
    return lax.dot_general(a, b, (((0,), (0,)), ((), ())), preferred_element_type=F32)


def col_sum(a):
    return jnp.sum(a, axis=0, keepdims=True)


def norm_parts(hidden):
    center = hidden - jnp.mean(hidden, axis=-1, keepdims=True)
    spread = jnp.mean(center * center, axis=-1, keepdims=True)
    inverse = lax.rsqrt(spread + NORM_EPS)
    return center * inverse, inverse


def norm_back(grad, gain, unit, inverse):
    scaled = grad * gain
    along = jnp.mean(scaled * unit, axis=-1, keepdims=True)
    return inverse * (scaled - jnp.mean(scaled, axis=-1, keepdims=True) - unit * along)


def segments(lengths_ref, row, shape, nblk, me):
    local = lax.broadcasted_iota(jnp.int32, shape, 0)
    block = shape[0] // nblk
    places = ((local // block) ^ me) * block + local % block
    end = jnp.int32(0)
    labels = jnp.zeros(shape, jnp.int32)
    for c in range(NSEG):
        end = end + lengths_ref[row, c]
        labels = labels + (places >= end).astype(jnp.int32)
    return labels


def on_blk():
    return lax.axis_index("blk")


def head_masks(length):
    lane = lax.broadcasted_iota(jnp.int32, (length, PAIR), 1)
    return lane < DH, lane >= DH


def attention_kernel(
    lengths_ref, tokens_ref, w_in_ref, bias_ref, w_out_ref, out_bias_ref,
    packed_ref, mixed_ref, first_in_ref, nblk, where, qblock=512,
):
    length = tokens_ref.shape[1]
    row = pl.program_id(0)
    x = tokens_ref[0]
    for c in range(3):
        cols = pl.ds(c * D, D)
        packed_ref[0, :, cols] = (nn(x, w_in_ref[:, cols]) + bias_ref[:, cols]).astype(BF)
    labels = segments(lengths_ref, row, (length, PAIR), nblk, where())
    lane = lax.broadcasted_iota(jnp.int32, (length, PAIR), 1)
    hit = labels == lane
    here = jnp.where(hit, 1.0, 0.0).astype(BF)
    away = jnp.where(hit, 0.0, -BIG).astype(BF)
    masks = head_masks(qblock)
    for j in range(H // 2):
        k = packed_ref[0, :, pl.ds(D + j * PAIR, PAIR)]
        v = packed_ref[0, :, pl.ds(2 * D + j * PAIR, PAIR)]
        k_aug = jnp.concatenate([k, away], axis=1)
        for t in range(length // qblock):
            rows = pl.ds(t * qblock, qblock)
            q = packed_ref[0, rows, pl.ds(j * PAIR, PAIR)] * jnp.asarray(DH**-0.5, BF)
            outs = []
            for h in range(2):
                qh = jnp.where(masks[h], q, jnp.zeros_like(q))
                s = nt(jnp.concatenate([qh, here[t * qblock : (t + 1) * qblock]], axis=1), k_aug)
                e = jnp.exp(s - jnp.max(s, axis=1, keepdims=True))
                total = jnp.sum(e, axis=1, keepdims=True)
                outs.append(nn(e.astype(BF), v) / total)
            mixed_ref[0, rows, pl.ds(j * PAIR, PAIR)] = jnp.where(masks[0], outs[0], outs[1]).astype(BF)
    branch = nn(mixed_ref[0], w_out_ref[...]) + out_bias_ref[...]
    first_in_ref[0] = x.astype(F32) + branch


def whole(shape):
    return pl.BlockSpec(shape, lambda *_: (0,) * len(shape), pipeline_mode=pl.Buffered(1))


def per_row(*shape):
    return pl.BlockSpec((1,) + shape, lambda r: (r,) + (0,) * len(shape))


SMEM = pl.BlockSpec(memory_space=pltpu.SMEM)


def attention_forward(lengths, tokens, w_in, bias, w_out, out_bias, nblk, where=on_blk, qblock=512):
    rows, length, _ = tokens.shape
    return pl.pallas_call(
        functools.partial(attention_kernel, nblk=nblk, where=where, qblock=qblock),
        grid=(rows,),
        in_specs=[SMEM, per_row(length, D), whole((D, 3 * D)), whole((1, 3 * D)), whole((D, D)), whole((1, D))],
        out_specs=[per_row(length, 3 * D), per_row(length, D), per_row(length, D)],
        out_shape=[
            jax.ShapeDtypeStruct((rows, length, 3 * D), BF),
            jax.ShapeDtypeStruct((rows, length, D), BF),
            jax.ShapeDtypeStruct((rows, length, D), F32),
        ],
        compiler_params=pltpu.CompilerParams(vmem_limit_bytes=VMEM_LIMIT),
        name="attention_forward",
    )(lengths, tokens, w_in, bias, w_out, out_bias)


def gelu_both(x):
    cdf = 0.5 + 0.5 * lax.erf(x * (0.5**0.5))
    density = jnp.exp(x * x * -0.5) * 0.3989422804014327
    return x * cdf, cdf + x * density


def feed_forward_kernel(
    lengths_ref, first_in_ref, w_up_ref, up_bias_ref, w_down_ref, down_bias_ref,
    g1_ref, b1_ref, g2_ref, b2_ref, out_grad_ref, pool_grad_ref,
    hidden_ref, pooled_ref, slope_ref, grad_second_ref, down_grad_ref, vec_ref,
    active_ref, outer_ref, nblk, where,
):
    r = pl.program_id(0)
    nrows = pl.num_programs(0)
    length = first_in_ref.shape[1]
    row = r
    unit, _ = norm_parts(first_in_ref[0])
    first = unit * g1_ref[...] + b1_ref[...]
    low = first.astype(BF)
    here_rows = pl.ds(pl.multiple_of(r * length, length), length)
    acc = first + down_bias_ref[...]
    for c in range(FF // CHUNK):
        cols = pl.ds(c * CHUNK, CHUNK)
        inner = nn(low, w_up_ref[:, cols]) + up_bias_ref[:, cols]
        act, slope = gelu_both(inner)
        act = act.astype(BF)
        active_ref[here_rows, cols] = act
        slope_ref[0, :, cols] = slope.astype(BF)
        acc = acc + nn(act, w_down_ref[cols, :])
    unit, inverse = norm_parts(acc)
    result = unit * g2_ref[...] + b2_ref[...]
    hidden_ref[0] = result.astype(BF)
    lane = lax.broadcasted_iota(jnp.int32, (length, PAIR), 1)
    hit = segments(lengths_ref, row, (length, PAIR), nblk, where()) == lane
    here = jnp.where(hit, 1.0, 0.0).astype(BF)
    high = result.astype(BF)
    rest = (result - high.astype(F32)).astype(BF)
    sums = (tn(here, high) + tn(here, rest))[:NSEG]
    sub = lax.broadcasted_iota(jnp.int32, (NSEG, 1), 0)
    count = jnp.zeros((NSEG, 1), F32)
    for c in range(NSEG):
        count = jnp.where(sub == c, lengths_ref[row, c].astype(F32), count)
    pooled_ref[0] = sums / count
    share = pool_grad_ref[0].astype(F32) / count
    share_high = share.astype(BF)
    share_rest = (share - share_high.astype(F32)).astype(BF)
    pad = jnp.zeros((PAIR - NSEG, D), BF)
    spread = nn(here, jnp.concatenate([share_high, pad], axis=0)) + nn(here, jnp.concatenate([share_rest, pad], axis=0))
    grad = out_grad_ref[0].astype(F32) + spread
    grad_second = norm_back(grad, g2_ref[...], unit, inverse)
    grad_second_ref[0] = grad_second
    outer = grad_second.astype(BF)
    outer_ref[here_rows, :] = outer
    sums = jnp.concatenate(
        [col_sum(grad * unit), col_sum(grad), col_sum(outer.astype(F32)), jnp.zeros((5, D), F32)], axis=0
    )

    @pl.when(r == 0)
    def _():
        vec_ref[...] = sums

    @pl.when(r != 0)
    def _():
        vec_ref[...] += sums

    @pl.when(r == nrows - 1)
    def _():
        for c in range(FF // CHUNK):
            cols = pl.ds(c * CHUNK, CHUNK)
            down_grad_ref[cols, :] = tn(active_ref[:, cols], outer_ref[...]).astype(BF)


def feed_forward(lengths, first_in, w_up, up_bias, w_down, down_bias, g1, b1, g2, b2, out_grad, pool_grad, nblk, where=on_blk):
    rows, length, _ = first_in.shape
    vec = whole((1, D))
    return pl.pallas_call(
        functools.partial(feed_forward_kernel, nblk=nblk, where=where),
        grid=(rows,),
        in_specs=[SMEM, per_row(length, D), whole((D, FF)), whole((1, FF)), whole((FF, D)), vec, vec, vec, vec, vec,
                  per_row(length, D), per_row(NSEG, D)],
        out_specs=[per_row(length, D), per_row(NSEG, D), per_row(length, FF), per_row(length, D), whole((FF, D)), whole((8, D))],
        out_shape=[
            jax.ShapeDtypeStruct((rows, length, D), BF),
            jax.ShapeDtypeStruct((rows, NSEG, D), F32),
            jax.ShapeDtypeStruct((rows, length, FF), BF),
            jax.ShapeDtypeStruct((rows, length, D), F32),
            jax.ShapeDtypeStruct((FF, D), BF),
            jax.ShapeDtypeStruct((8, D), F32),
        ],
        scratch_shapes=[pltpu.VMEM((rows * length, FF), BF), pltpu.VMEM((rows * length, D), BF)],
        compiler_params=pltpu.CompilerParams(vmem_limit_bytes=VMEM_LIMIT),
        name="feed_forward",
    )(lengths, first_in, w_up, up_bias, w_down, down_bias, g1, b1, g2, b2, out_grad, pool_grad)


def feed_back_kernel(
    first_in_ref, slope_ref, grad_second_ref, mixed_ref, w_up_ref, w_down_ref, w_out_ref, g1_ref, b1_ref,
    grad_first_in_ref, grad_mixed_ref, up_grad_ref, output_grad_ref, vec_ref, up_bias_ref,
    low_ref, inner_ref, branch_ref, mix_ref,
):
    r = pl.program_id(0)
    nrows = pl.num_programs(0)
    length = first_in_ref.shape[1]
    here_rows = pl.ds(pl.multiple_of(r * length, length), length)
    grad_second = grad_second_ref[0]
    outer = grad_second.astype(BF)
    acc = grad_second

    @pl.when(r == 0)
    def _():
        vec_ref[...] = jnp.zeros_like(vec_ref)
        up_bias_ref[...] = jnp.zeros_like(up_bias_ref)

    for c in range(FF // CHUNK):
        cols = pl.ds(c * CHUNK, CHUNK)
        grad_active = nt(outer, w_down_ref[cols, :])
        inner = (grad_active * slope_ref[0, :, cols].astype(F32)).astype(BF)
        inner_ref[here_rows, cols] = inner
        up_bias_ref[:, cols] += col_sum(inner.astype(F32))
        acc = acc + nt(inner, w_up_ref[:, cols])
    unit, inverse = norm_parts(first_in_ref[0])
    low_ref[here_rows, :] = (unit * g1_ref[...] + b1_ref[...]).astype(BF)
    grad_first_in = norm_back(acc, g1_ref[...], unit, inverse)
    grad_first_in_ref[0] = grad_first_in
    branch = grad_first_in.astype(BF)
    branch_ref[here_rows, :] = branch
    mix_ref[here_rows, :] = mixed_ref[0]
    vec_ref[...] += jnp.concatenate(
        [col_sum(acc * unit), col_sum(acc), col_sum(branch.astype(F32)), jnp.zeros((5, D), F32)], axis=0
    )
    grad_mixed_ref[0] = nt(branch, w_out_ref[...]).astype(BF)

    @pl.when(r == nrows - 1)
    def _():
        for c in range(FF // CHUNK):
            cols = pl.ds(c * CHUNK, CHUNK)
            up_grad_ref[:, cols] = tn(low_ref[...], inner_ref[:, cols]).astype(BF)
        output_grad_ref[...] = tn(mix_ref[...], branch_ref[...]).astype(BF)


def feed_back(first_in, slope, grad_second, mixed, w_up, w_down, w_out, g1, b1):
    rows, length, _ = first_in.shape
    return pl.pallas_call(
        feed_back_kernel,
        grid=(rows,),
        in_specs=[per_row(length, D), per_row(length, FF), per_row(length, D), per_row(length, D),
                  whole((D, FF)), whole((FF, D)), whole((D, D)), whole((1, D)), whole((1, D))],
        out_specs=[per_row(length, D), per_row(length, D), whole((D, FF)), whole((D, D)), whole((8, D)), whole((1, FF))],
        out_shape=[
            jax.ShapeDtypeStruct((rows, length, D), F32),
            jax.ShapeDtypeStruct((rows, length, D), BF),
            jax.ShapeDtypeStruct((D, FF), BF),
            jax.ShapeDtypeStruct((D, D), BF),
            jax.ShapeDtypeStruct((8, D), F32),
            jax.ShapeDtypeStruct((1, FF), F32),
        ],
        scratch_shapes=[pltpu.VMEM((rows * length, D), BF), pltpu.VMEM((rows * length, FF), BF),
                        pltpu.VMEM((rows * length, D), BF), pltpu.VMEM((rows * length, D), BF)],
        compiler_params=pltpu.CompilerParams(vmem_limit_bytes=VMEM_LIMIT),
        name="feed_back",
    )(first_in, slope, grad_second, mixed, w_up, w_down, w_out, g1, b1)


def attention_back_kernel(
    lengths_ref, tokens_ref, packed_ref, grad_mixed_ref, grad_first_in_ref, w_in_ref,
    tokens_grad_ref, input_grad_ref, vec_ref, x_ref, grad_packed_ref, nblk, where,
):
    r = pl.program_id(0)
    nrows = pl.num_programs(0)
    length = tokens_ref.shape[1]
    row = r
    here_rows = pl.ds(pl.multiple_of(r * length, length), length)
    x_ref[here_rows, :] = tokens_ref[0]
    labels = segments(lengths_ref, row, (length, PAIR), nblk, where())
    lane = lax.broadcasted_iota(jnp.int32, (length, PAIR), 1)
    hit = labels == lane
    here = jnp.where(hit, 1.0, 0.0).astype(BF)
    away = jnp.where(hit, 0.0, -BIG).astype(BF)
    masks = head_masks(length)
    scale = DH**-0.5
    for j in range(H // 2):
        q = packed_ref[0, :, pl.ds(j * PAIR, PAIR)] * jnp.asarray(scale, BF)
        k = packed_ref[0, :, pl.ds(D + j * PAIR, PAIR)]
        v = packed_ref[0, :, pl.ds(2 * D + j * PAIR, PAIR)]
        gm = grad_mixed_ref[0, :, pl.ds(j * PAIR, PAIR)]
        k_aug = jnp.concatenate([k, away], axis=1)
        gq = gk = gv = None
        for h in range(2):
            zero = jnp.zeros_like(q)
            qh = jnp.where(masks[h], q, zero)
            kh = jnp.where(masks[h], k, zero)
            gmh = jnp.where(masks[h], gm, zero)
            s = nt(k_aug, jnp.concatenate([qh, here], axis=1))
            e = jnp.exp(s - jnp.max(s, axis=0, keepdims=True))
            p = e * (1.0 / jnp.sum(e, axis=0, keepdims=True))
            gp = nt(v, gmh)
            delta = jnp.sum(gp * p, axis=0, keepdims=True)
            gs = (p * (gp - delta)).astype(BF)
            gvh = nn(p.astype(BF), gmh)
            gkh = nn(gs, qh)
            gqh = tn(gs, kh)
            gq, gk, gv = (gqh, gkh, gvh) if h == 0 else (gq + gqh, gk + gkh, gv + gvh)
        grad_packed_ref[here_rows, pl.ds(j * PAIR, PAIR)] = (gq * scale).astype(BF)
        grad_packed_ref[here_rows, pl.ds(D + j * PAIR, PAIR)] = gk.astype(BF)
        grad_packed_ref[here_rows, pl.ds(2 * D + j * PAIR, PAIR)] = gv.astype(BF)
    gpk = grad_packed_ref[here_rows, :]
    tokens_grad_ref[0] = (grad_first_in_ref[0] + nt(gpk, w_in_ref[...])).astype(tokens_grad_ref.dtype)
    sums = jnp.concatenate(
        [col_sum(gpk[:, :D].astype(F32)), col_sum(gpk[:, 2 * D :].astype(F32)), jnp.zeros((6, D), F32)], axis=0
    )

    @pl.when(r == 0)
    def _():
        vec_ref[...] = sums

    @pl.when(r != 0)
    def _():
        vec_ref[...] += sums

    @pl.when(r == nrows - 1)
    def _():
        for c in range(3):
            cols = pl.ds(c * D, D)
            input_grad_ref[:, cols] = tn(x_ref[...], grad_packed_ref[:, cols]).astype(BF)


def attention_back(lengths, tokens, packed, grad_mixed, grad_first_in, w_in, nblk, where=on_blk):
    rows, length, _ = tokens.shape
    return pl.pallas_call(
        functools.partial(attention_back_kernel, nblk=nblk, where=where),
        grid=(rows,),
        in_specs=[SMEM, per_row(length, D), per_row(length, 3 * D), per_row(length, D), per_row(length, D), whole((D, 3 * D))],
        out_specs=[per_row(length, D), whole((D, 3 * D)), whole((8, D))],
        out_shape=[
            jax.ShapeDtypeStruct((rows, length, D), BF),
            jax.ShapeDtypeStruct((D, 3 * D), BF),
            jax.ShapeDtypeStruct((8, D), F32),
        ],
        scratch_shapes=[pltpu.VMEM((rows * length, D), BF), pltpu.VMEM((rows * length, 3 * D), BF)],
        compiler_params=pltpu.CompilerParams(vmem_limit_bytes=VMEM_LIMIT),
        name="attention_back",
    )(lengths, tokens, packed, grad_mixed, grad_first_in, w_in)


def pieces_of(array, me, nblk):
    rows = array.shape[0] // nblk
    return [lax.dynamic_slice_in_dim(array, (me ^ k) * rows, rows, axis=0) for k in range(nblk)]


def swap(pieces, nblk):
    return [pieces[0]] + [
        lax.ppermute(pieces[k], "blk", [(i, i ^ k) for i in range(nblk)]) for k in range(1, nblk)
    ]


def placed(pieces, me, nblk):
    rows = pieces[0].shape[0]
    out = jnp.zeros((rows * nblk,) + pieces[0].shape[1:], pieces[0].dtype)
    for k in range(nblk):
        out = lax.dynamic_update_slice_in_dim(out, pieces[k], (me ^ k) * rows, axis=0)
    return out


def to_rows(array, me, nblk):
    return jnp.concatenate(swap(pieces_of(array, me, nblk), nblk), axis=1)


def to_blocks(array, me, nblk):
    block = array.shape[1] // nblk
    return placed(swap([array[:, k * block : (k + 1) * block] for k in range(nblk)], nblk), me, nblk)


def on_device(
    tokens,
    lengths,
    input_weight,
    query_bias,
    value_bias,
    output_weight,
    output_bias,
    first_gain,
    first_shift,
    up_weight,
    up_bias,
    down_weight,
    down_bias,
    second_gain,
    second_shift,
    out_grad,
    pool_grad,
):
    batch, block, _ = tokens.shape
    nblk = lax.axis_size("blk")
    me = lax.axis_index("blk")
    rows = batch // nblk
    row = lambda v: v.reshape(1, -1)
    bias = row(jnp.concatenate([query_bias, jnp.zeros_like(query_bias), value_bias]))
    x = to_rows(tokens, me, nblk)
    out_grad = to_rows(out_grad, me, nblk)
    own_lengths = lax.dynamic_slice_in_dim(lengths, me * rows, rows, axis=0)
    own_pool = lax.dynamic_slice_in_dim(pool_grad, me * rows, rows, axis=0)
    packed, mixed, first_in = attention_forward(
        own_lengths, x, input_weight, bias, output_weight, row(output_bias), nblk
    )
    hidden, pooled, slope, grad_second, down_grad, vec2 = feed_forward(
        own_lengths, first_in, up_weight, row(up_bias), down_weight, row(down_bias), row(first_gain),
        row(first_shift), row(second_gain), row(second_shift), out_grad, own_pool, nblk,
    )
    grad_first_in, grad_mixed, up_grad, output_grad, vec1, up_bias_grad = feed_back(
        first_in, slope, grad_second, mixed, up_weight, down_weight, output_weight, row(first_gain),
        row(first_shift),
    )
    tokens_grad, input_grad, vec0 = attention_back(
        own_lengths, x, packed, grad_mixed, grad_first_in, input_weight, nblk
    )
    axes = ("rows", "blk")
    total = lambda a: lax.psum(a, axes).astype(F32)
    vecs = lax.psum(jnp.concatenate([vec0[:2], vec1[:3], vec2[:3], up_bias_grad.reshape(-1, D)], axis=0), axes)
    return (
        to_blocks(hidden, me, nblk),
        lax.all_gather(pooled, "blk", axis=0, tiled=True),
        to_blocks(tokens_grad, me, nblk).astype(F32),
        total(input_grad),
        vecs[0],
        vecs[1],
        total(output_grad),
        vecs[4],
        vecs[2],
        vecs[3],
        total(up_grad),
        vecs[8:].reshape(-1),
        total(down_grad),
        vecs[7],
        vecs[5],
        vecs[6],
    )


def solution(mesh):
    whole_rows = P("rows", "blk", None)
    rest = (P(),) * 13
    return jax.shard_map(
        on_device,
        mesh=mesh,
        in_specs=(whole_rows, P("rows", None)) + rest + (whole_rows, P("rows", None, None)),
        out_specs=(whole_rows, P("rows", None, None), whole_rows) + rest,
        check_vma=False,
    )
```

```python
import functools
import jax
import jax.numpy as jnp
from jax import lax
from jax.experimental import pallas as pl
from jax.experimental.pallas import tpu as pltpu
from jax.sharding import PartitionSpec as P

D = 768
H = 12
DH = 64
FF = 3072
NSEG = 8
PAIR = 2 * DH
NORM_EPS = 1e-12
BIG = 1e9
BF = jnp.bfloat16
F32 = jnp.float32
CHUNK = 512
VMEM_LIMIT = 60 * 1024 * 1024


def nn(a, b):
    return lax.dot_general(a, b, (((1,), (0,)), ((), ())), preferred_element_type=F32)


def nt(a, b):
    return lax.dot_general(a, b, (((1,), (1,)), ((), ())), preferred_element_type=F32)


def tn(a, b):
    return lax.dot_general(a, b, (((0,), (0,)), ((), ())), preferred_element_type=F32)


def col_sum(a):
    return jnp.sum(a, axis=0, keepdims=True)


def norm_parts(hidden):
    center = hidden - jnp.mean(hidden, axis=-1, keepdims=True)
    spread = jnp.mean(center * center, axis=-1, keepdims=True)
    inverse = lax.rsqrt(spread + NORM_EPS)
    return center * inverse, inverse


def norm_back(grad, gain, unit, inverse):
    scaled = grad * gain
    along = jnp.mean(scaled * unit, axis=-1, keepdims=True)
    return inverse * (scaled - jnp.mean(scaled, axis=-1, keepdims=True) - unit * along)


def segments(lengths_ref, row, length, count, nblk, me, first=0):
    shape = (count, PAIR)
    local = lax.broadcasted_iota(jnp.int32, shape, 0) + first
    block = length // nblk
    places = ((local // block) ^ me) * block + local % block
    end = jnp.int32(0)
    labels = jnp.zeros(shape, jnp.int32)
    for c in range(NSEG):
        end = end + lengths_ref[row, c]
        labels = labels + (places >= end).astype(jnp.int32)
    return labels == lax.broadcasted_iota(jnp.int32, shape, 1)


def head_masks(length):
    lane = lax.broadcasted_iota(jnp.int32, (length, PAIR), 1)
    return lane < DH, lane >= DH


PLACE = {"y": 0, "x": 1, "a": 2, "b": 3}
BLOCKS = 16
DOWN_ORDER = ("xyab", "yxab", 3)
UP_ORDER = ("xyab", "yxab", 3)
HEAD_ORDER = ("xyab", "yxab", 3)
TAIL = "duhrtdurvudrvurvdrv1durv2u34r5r6"


def own_place():
    blk = lax.axis_index("blk")
    rows = lax.axis_index("rows")
    return blk & 1, ((rows & 7) << 1) | ((blk >> 1) & 1), blk


def slot_in(order, halved, block, here):
    slot = 0
    for t, bit in enumerate(order):
        at = block ^ here if t < halved else block
        slot = slot | (((at >> PLACE[bit]) & 1) << (3 - t))
    return slot


def slot_of(orders, core, block, here):
    return jnp.where(
        core == 0, slot_in(orders[0], orders[2], block, here), slot_in(orders[1], orders[2], block, here)
    )


def hand_out(slots_ref, send_ref, keep_ref, sems):
    half = BLOCKS // 2
    copies = [
        pltpu.make_async_copy(slots_ref.at[pl.ds(half, half)], send_ref, sems.at[0]),
        pltpu.make_async_copy(slots_ref.at[pl.ds(0, half)], keep_ref, sems.at[1]),
    ]
    for c in copies:
        c.start()
    for c in copies:
        c.wait()


def whole(shape):
    return pl.BlockSpec(shape, lambda *_: (0,) * len(shape), pipeline_mode=pl.Buffered(1))


def per_row(*shape):
    return pl.BlockSpec((1,) + shape, lambda r: (r,) + (0,) * len(shape))


def flat(*shape):
    return pl.BlockSpec(shape, lambda r: (r,) + (0,) * (len(shape) - 1))


SMEM = pl.BlockSpec(memory_space=pltpu.SMEM)
ANY = pl.BlockSpec(memory_space=pl.ANY)


def slots(rows, cols):
    half = (ANY, (BLOCKS // 2, rows, cols), BF)
    return [half, half], [pltpu.VMEM((BLOCKS, rows, cols), BF), pltpu.SemaphoreType.DMA((2,))]


def shape_of(shape, dtype):
    return jax.ShapeDtypeStruct(shape, dtype)


def call(kernel, name, grid, in_specs, outs, scratch=(), flops=0, nbytes=0, aliases=None):
    return pl.pallas_call(
        kernel,
        grid=grid,
        in_specs=in_specs,
        out_specs=[o[0] for o in outs],
        out_shape=[shape_of(o[1], o[2]) for o in outs],
        scratch_shapes=scratch,
        input_output_aliases=aliases or {},
        compiler_params=pltpu.CompilerParams(vmem_limit_bytes=VMEM_LIMIT),
        cost_estimate=pl.CostEstimate(flops=int(flops), bytes_accessed=int(nbytes), transcendentals=0),
        name=name,
    )


def attention_kernel(lengths_ref, *refs, nblk, place):
    pieces = refs[:nblk]
    w_in_ref, bias_ref, w_out_ref, out_bias_ref, x_ref, packed_ref, mixed_ref, first_in_ref = refs[nblk:]
    block = pieces[0].shape[1]
    length = block * nblk
    for i in range(nblk):
        x_ref[pl.ds(i * block, block), :] = pieces[i][0]
    x = x_ref[...]
    for c in range(3):
        cols = pl.ds(c * D, D)
        packed_ref[0, :, cols] = (nn(x, w_in_ref[:, cols]) + bias_ref[:, cols]).astype(BF)
    hit = segments(lengths_ref, pl.program_id(0), length, length, nblk, place()[2])
    here = jnp.where(hit, 1.0, 0.0).astype(BF)
    away = jnp.where(hit, 0.0, -BIG).astype(BF)
    masks = head_masks(length)
    for j in range(H // 2):
        q = packed_ref[0, :, pl.ds(j * PAIR, PAIR)] * jnp.asarray(DH**-0.5, BF)
        k = packed_ref[0, :, pl.ds(D + j * PAIR, PAIR)]
        v = packed_ref[0, :, pl.ds(2 * D + j * PAIR, PAIR)]
        k_aug = jnp.concatenate([k, away], axis=1)
        outs = []
        for h in range(2):
            qh = jnp.where(masks[h], q, jnp.zeros_like(q))
            s = nt(jnp.concatenate([qh, here], axis=1), k_aug)
            e = jnp.exp(s - jnp.max(s, axis=1, keepdims=True))
            total = jnp.sum(e, axis=1, keepdims=True)
            outs.append(nn(e.astype(BF), v) / total)
        mixed_ref[:, pl.ds(j * PAIR, PAIR)] = jnp.where(masks[0], outs[0], outs[1]).astype(BF)
    branch = nn(mixed_ref[...], w_out_ref[...]) + out_bias_ref[...]
    first_in_ref[...] = x.astype(F32) + branch


def attention_forward(lengths, pieces, w_in, bias, w_out, out_bias, place=own_place):
    nblk = len(pieces)
    rows, block, _ = pieces[0].shape
    length = block * nblk
    return call(
        functools.partial(attention_kernel, nblk=nblk, place=place),
        "attention_forward",
        (rows,),
        [SMEM] + [per_row(block, D)] * nblk + [whole((D, 3 * D)), whole((1, 3 * D)), whole((D, D)), whole((1, D))],
        [
            (flat(length, D), (rows * length, D), BF),
            (per_row(length, 3 * D), (rows, length, 3 * D), BF),
            (flat(length, D), (rows * length, D), BF),
            (flat(length, D), (rows * length, D), F32),
        ],
        flops=18e9,
    )(lengths, *pieces, w_in, bias, w_out, out_bias)


def gelu_both(x):
    cdf = 0.5 + 0.5 * lax.erf(x * (0.5**0.5))
    density = jnp.exp(x * x * -0.5) * 0.3989422804014327
    return x * cdf, cdf + x * density


def feed_kernel(lengths_ref, first_in_ref, pool_grad_ref, *refs, nblk, place):
    grad_pieces = refs[:nblk]
    (w_up_ref, up_bias_ref, w_down_ref, down_bias_ref, w_out_ref, g1_ref, b1_ref, g2_ref, b2_ref) = refs[nblk : nblk + 9]
    hidden = refs[nblk + 9 : 2 * nblk + 9]
    (low_ref, active_own_ref, active_other_ref, inner_own_ref, inner_other_ref, grad_first_in_ref, grad_mixed_ref,
     branch_own_ref, branch_other_ref, vec_ref, up_sums_ref,
     active_ref, slope_ref, inner_ref, branch_ref, pooled_ref) = refs[2 * nblk + 9 :]
    step = pl.program_id(0)
    r, part = step // 2, step % 2
    count = first_in_ref.shape[0]
    block = hidden[0].shape[1] - 2 * NSEG
    length = block * nblk
    some = nblk // 2
    half = FF // 2
    core, _, blk = place()
    own = pl.ds(pl.multiple_of(core * half, 128), half)
    other = pl.ds(pl.multiple_of((core ^ 1) * half, 128), half)

    unit1, inverse1 = norm_parts(first_in_ref[...])
    first = unit1 * g1_ref[...] + b1_ref[...]
    low = first.astype(BF)
    low_ref[...] = low
    acc = first + down_bias_ref[...]
    for c in range(FF // CHUNK):
        cols = pl.ds(c * CHUNK, CHUNK)
        inner = nn(low, w_up_ref[:, cols]) + up_bias_ref[:, cols]
        act, slope = gelu_both(inner)
        act = act.astype(BF)
        active_ref[:, cols] = act
        slope_ref[:, cols] = slope.astype(BF)
        acc = acc + nn(act, w_down_ref[cols, :])
    active_own_ref[...] = active_ref[:, own]
    active_other_ref[:, :half] = active_ref[:, other]
    unit, inverse = norm_parts(acc)
    result = unit * g2_ref[...] + b2_ref[...]
    high = result.astype(BF)
    here = jnp.where(segments(lengths_ref, r, length, count, nblk, blk, part * count), 1.0, 0.0).astype(BF)
    rest = (result - high.astype(F32)).astype(BF)
    sums = (tn(here, high) + tn(here, rest))[:NSEG]
    sub = lax.broadcasted_iota(jnp.int32, (NSEG, 1), 0)
    counts = jnp.zeros((NSEG, 1), F32)
    for c in range(NSEG):
        counts = jnp.where(sub == c, lengths_ref[r, c].astype(F32), counts)

    @pl.when(part == 0)
    def _():
        pooled_ref[...] = sums
        for i in range(some):
            hidden[i][0, :block, :] = high[i * block : (i + 1) * block]

    @pl.when(part == 1)
    def _():
        pooled = (pooled_ref[...] + sums) / counts
        pooled_high = pooled.astype(BF)
        both = jnp.concatenate([pooled_high.astype(F32), pooled - pooled_high.astype(F32)], axis=0).astype(BF)
        for i in range(some):
            hidden[some + i][0, :block, :] = high[i * block : (i + 1) * block]
        for i in range(nblk):
            hidden[i][0, block:, :] = both

    share = pool_grad_ref[0].astype(F32) / counts
    share_high = share.astype(BF)
    share_rest = (share - share_high.astype(F32)).astype(BF)
    pad = jnp.zeros((PAIR - NSEG, D), BF)
    spread = nn(here, jnp.concatenate([share_high, pad], axis=0)) + nn(here, jnp.concatenate([share_rest, pad], axis=0))
    given = jnp.where(
        part == 0,
        jnp.concatenate([g[0] for g in grad_pieces[:some]], axis=0).astype(F32),
        jnp.concatenate([g[0] for g in grad_pieces[some:]], axis=0).astype(F32),
    )
    grad = given + spread
    acc = norm_back(grad, g2_ref[...], unit, inverse)
    outer = acc.astype(BF)
    active_other_ref[:, half:] = outer
    sums2 = [col_sum(grad * unit), col_sum(grad), col_sum(outer.astype(F32))]
    bias_sums = []
    for c in range(FF // CHUNK):
        cols = pl.ds(c * CHUNK, CHUNK)
        inner = (nt(outer, w_down_ref[cols, :]) * slope_ref[:, cols].astype(F32)).astype(BF)
        inner_ref[:, cols] = inner
        bias_sums.append(col_sum(inner.astype(F32)))
        acc = acc + nt(inner, w_up_ref[:, cols])
    inner_own_ref[...] = inner_ref[:, own]
    inner_other_ref[...] = inner_ref[:, other]
    grad_first_in = norm_back(acc, g1_ref[...], unit1, inverse1)
    grad_first_in_ref[...] = grad_first_in
    branch = grad_first_in.astype(BF)
    branch_ref[...] = branch
    for ref, flip in ((branch_own_ref, 0), (branch_other_ref, 1)):
        ref[...] = branch_ref[:, pl.ds(pl.multiple_of((core ^ flip) * (D // 2), 128), D // 2)]
    grad_mixed_ref[...] = nt(branch, w_out_ref[...]).astype(BF)
    sums1 = [col_sum(acc * unit1), col_sum(acc), col_sum(branch.astype(F32))]
    vec = jnp.concatenate(sums1 + sums2 + [jnp.zeros((2, D), F32)], axis=0)
    up_sums = jnp.concatenate([jnp.concatenate(bias_sums, axis=1), jnp.zeros((7, FF), F32)], axis=0)

    @pl.when(step == 0)
    def _():
        vec_ref[...] = vec
        up_sums_ref[...] = up_sums

    @pl.when(step != 0)
    def _():
        vec_ref[...] += vec
        up_sums_ref[...] += up_sums


def feed(lengths, first_in, pool_grad, grads, w_up, up_bias, w_down, down_bias, w_out, g1, b1, g2, b2, place=own_place):
    nblk = len(grads)
    rows, block, _ = grads[0].shape
    total = first_in.shape[0]
    tile = block * nblk // 2
    vec = whole((1, D))

    def row(*shape):
        return pl.BlockSpec((1,) + shape, lambda i: (i // 2,) + (0,) * len(shape))

    def out(cols, dtype=BF):
        return flat(tile, cols), (total, cols), dtype

    half = FF // 2
    return call(
        functools.partial(feed_kernel, nblk=nblk, place=place),
        "feed",
        (total // tile,),
        [SMEM, flat(tile, D), row(NSEG, D)] + [row(block, D)] * nblk
        + [whole((D, FF)), whole((1, FF)), whole((FF, D)), vec, whole((D, D)), vec, vec, vec, vec],
        [(row(block + 2 * NSEG, D), (rows, block + 2 * NSEG, D), BF)] * nblk
        + [out(D), out(half), out(half + D), out(half), out(half), out(D, F32), out(D), out(D // 2), out(D // 2),
           (whole((8, D)), (8, D), F32), (whole((8, FF)), (8, FF), F32)],
        scratch=[pltpu.VMEM((tile, FF), BF)] * 3 + [pltpu.VMEM((tile, D), BF), pltpu.VMEM((NSEG, D), F32)],
        flops=40e9,
    )(lengths, first_in, pool_grad, *grads, w_up, up_bias, w_down, down_bias, w_out, g1, b1, g2, b2)


def down_kernel(
    active_ref, outer_ref, came_active_ref, came_outer_ref, send_ref, keep_ref, slots_ref, sems, place, orders
):
    step = pl.program_id(0)
    core, here_block, _ = place()
    rows = slots_ref.shape[1]
    here = active_ref.shape[1] // rows
    tile = (tn(active_ref[...], outer_ref[...]) + tn(came_active_ref[...], came_outer_ref[...])).astype(BF)
    for i in range(here):
        slots_ref[slot_of(orders, core, step * here + i, here_block)] = tile[i * rows : (i + 1) * rows]

    @pl.when(step == pl.num_programs(0) - 1)
    def _():
        hand_out(slots_ref, send_ref, keep_ref, sems)


def down_gradient(active, mine, came, orders, place=own_place):
    total, half = active.shape
    outs, scratch = slots(half // BLOCKS, D)
    wide = 384
    part = pl.BlockSpec((total, wide), lambda j: (0, j))
    outer = pl.BlockSpec((total, D), lambda j: (0, half // D), pipeline_mode=pl.Buffered(1))
    return call(
        functools.partial(down_kernel, place=place, orders=orders),
        "down_gradient",
        (half // wide,),
        [part, outer, part, outer],
        outs,
        scratch=scratch,
        flops=6e9,
    )(active, mine, came, came)


def up_kernel(low_ref, inner_ref, came_low_ref, came_inner_ref, send_ref, keep_ref, slots_ref, sems, place, orders):
    step = pl.program_id(0)
    core, here_block, _ = place()
    rows = slots_ref.shape[1]
    wide = inner_ref.shape[1]
    tile = (tn(low_ref[...], inner_ref[...]) + tn(came_low_ref[...], came_inner_ref[...])).astype(BF)
    cols = pl.ds(pl.multiple_of(step * wide, 128), wide)
    for i in range(BLOCKS):
        slots_ref[slot_of(orders, core, i, here_block), :, cols] = tile[i * rows : (i + 1) * rows]

    @pl.when(step == pl.num_programs(0) - 1)
    def _():
        hand_out(slots_ref, send_ref, keep_ref, sems)


def up_gradient(low, inner, came_low, came_inner, orders, place=own_place):
    total, half = inner.shape
    outs, scratch = slots(D // BLOCKS, half)
    wide = 512
    part = pl.BlockSpec((total, wide), lambda j: (0, j))
    return call(
        functools.partial(up_kernel, place=place, orders=orders),
        "up_gradient",
        (half // wide,),
        [whole((total, D)), part, whole((total, D)), part],
        outs,
        scratch=scratch,
        flops=6e9,
    )(low, inner, came_low, came_inner)


def attention_back_kernel(lengths_ref, *refs, nblk, place):
    q_ref, k_ref, v_ref, gm_ref, grads_ref, other_ref, vec_ref = refs
    r = pl.program_id(0)
    core, _, blk = place()
    length = q_ref.shape[1]
    wide = 3 * PAIR
    hit = segments(lengths_ref, r, length, length, nblk, blk)
    here = jnp.where(hit, 1.0, 0.0).astype(BF)
    away = jnp.where(hit, 0.0, -BIG).astype(BF)
    masks = head_masks(length)
    scale = DH**-0.5
    for j in range(2):
        lanes = slice(j * PAIR, (j + 1) * PAIR)
        q = q_ref[0, :, lanes] * jnp.asarray(scale, BF)
        k = k_ref[0, :, lanes]
        v = v_ref[0, :, lanes]
        gm = gm_ref[:, lanes]
        k_aug = jnp.concatenate([k, away], axis=1)
        zero = jnp.zeros_like(q)
        gq = gk = gv = 0.0
        for h in range(2):
            qh = jnp.where(masks[h], q, zero)
            kh = jnp.where(masks[h], k, zero)
            gmh = jnp.where(masks[h], gm, zero)
            s = nt(k_aug, jnp.concatenate([qh, here], axis=1))
            e = jnp.exp(s - jnp.max(s, axis=0, keepdims=True))
            p = e * (1.0 / jnp.sum(e, axis=0, keepdims=True))
            gp = nt(v, gmh)
            delta = jnp.sum(gp * p, axis=0, keepdims=True)
            gs = (p * (gp - delta)).astype(BF)
            gv = gv + nn(p.astype(BF), gmh)
            gk = gk + nn(gs, qh)
            gq = gq + tn(gs, kh)
        grads = jnp.concatenate([(gq * scale).astype(BF), gk.astype(BF), gv.astype(BF)], axis=1)
        at = pl.ds(j * wide, wide)
        grads_ref[:, at] = grads
        sums = jnp.concatenate([col_sum(grads.astype(F32)), jnp.zeros((7, wide), F32)], axis=0)

        @pl.when(r == 0)
        def _():
            vec_ref[:, at] = sums

        @pl.when(r != 0)
        def _():
            vec_ref[:, at] += sums

    other_ref[...] = grads_ref[:, pl.ds(pl.multiple_of((core ^ 1) * wide, 128), wide)]


def attention_back(lengths, packed, grad_mixed, nblk, group, place=own_place):
    rows, length, _ = packed.shape
    total = rows * length

    def pairs(section):
        return pl.BlockSpec((1, length, 2 * PAIR), lambda r: (r, 0, section * (H // 4) + group))

    return call(
        functools.partial(attention_back_kernel, nblk=nblk, place=place),
        "attention_back",
        (rows,),
        [SMEM, pairs(0), pairs(1), pairs(2), pl.BlockSpec((length, 2 * PAIR), lambda r: (r, group))],
        [(flat(length, D), (total, D), BF), (flat(length, D // 2), (total, D // 2), BF), (whole((8, D)), (8, D), F32)],
        flops=12e9,
    )(lengths, packed, packed, packed, grad_mixed)


def head_gradient_kernel(*refs, count, place, orders):
    lefts, rights, came_rights = refs[:4], refs[4 : 4 + count], refs[4 + count : 4 + 2 * count]
    send_ref, keep_ref = refs[4 + 2 * count : 6 + 2 * count]
    held, right_held, slots_ref, sems, left_sems, right_sems = refs[6 + 2 * count :]
    core, here_block, _ = place()
    wide = D // 2
    left_loads = [pltpu.make_async_copy(ref, held.at[n], left_sems.at[n]) for n, ref in enumerate(lefts)]
    right_loads = []
    for n, ref in enumerate(rights):
        lanes = pl.ds(pl.multiple_of(core * wide, 128), wide) if ref.shape[1] == D else pl.ds(0, wide)
        right_loads.append(pltpu.make_async_copy(ref.at[:, lanes], right_held.at[n, 0], right_sems.at[2 * n]))
        right_loads.append(pltpu.make_async_copy(came_rights[n], right_held.at[n, 1], right_sems.at[2 * n + 1]))
    order = left_loads[:2] + right_loads[:2] + left_loads[2:] + right_loads[2:]
    for load in order:
        load.start()
    rows = D // BLOCKS
    for n in range(count):
        if n < 2:
            left_loads[2 * n].wait()
            left_loads[2 * n + 1].wait()
        right_loads[2 * n].wait()
        right_loads[2 * n + 1].wait()
        at = 0 if n == 0 else 2
        tile = (tn(held[at], right_held[n, 0]) + tn(held[at + 1], right_held[n, 1])).astype(BF)
        for i in range(BLOCKS):
            slot = slot_of(orders, core, i, here_block)
            slots_ref[slot, :, n * wide : (n + 1) * wide] = tile[i * rows : (i + 1) * rows]
    hand_out(slots_ref, send_ref, keep_ref, sems)


def head_gradient(lefts, rights, came_rights, orders, place=own_place):
    total = lefts[0].shape[0]
    count = len(rights)
    wide = D // 2
    outs, scratch = slots(D // BLOCKS, count * wide)
    return call(
        functools.partial(head_gradient_kernel, count=count, place=place, orders=orders),
        "head_gradient",
        (1,),
        [ANY] * (4 + 2 * count),
        outs,
        scratch=[pltpu.VMEM((4, total, D), BF), pltpu.VMEM((count, 2, total, wide), BF)] + scratch
        + [pltpu.SemaphoreType.DMA((4,)), pltpu.SemaphoreType.DMA((2 * count,))],
        flops=6e9,
    )(*lefts, *rights, *came_rights)


def tokens_grad_kernel(*refs, groups, nblk):
    grads = refs[:groups]
    grad_first_in_ref, w_in_ref = refs[groups : groups + 2]
    outs = refs[groups + 2 : groups + 2 + nblk]
    all_ref = refs[-1]
    length = grad_first_in_ref.shape[0]
    block = length // nblk
    for g in range(groups):
        for j in range(2):
            for section in range(3):
                at = section * D + (2 * g + j) * PAIR
                start = (3 * j + section) * PAIR
                all_ref[:, at : at + PAIR] = grads[g][:, start : start + PAIR]
    total = (grad_first_in_ref[...] + nt(all_ref[...], w_in_ref[...])).astype(BF)
    for i in range(nblk):
        outs[i][0] = total[i * block : (i + 1) * block]


def tokens_gradient(grads, grad_first_in, w_in, nblk, rows):
    length = grad_first_in.shape[0] // rows
    block = length // nblk
    return call(
        functools.partial(tokens_grad_kernel, groups=len(grads), nblk=nblk),
        "tokens_gradient",
        (rows,),
        [flat(length, D)] * len(grads) + [flat(length, D), whole((D, 3 * D))],
        [(per_row(block, D), (rows, block, D), BF)] * nblk,
        scratch=[pltpu.VMEM((length, 3 * D), BF)],
        flops=5e9,
    )(*grads, grad_first_in, w_in)


def place_hidden_kernel(*refs, nblk, rows, block, place):
    pieces, (hidden_ref, pooled_ref) = refs[:nblk], refs[nblk:]
    blk = place()[2]
    for i in range(nblk):
        for r in range(rows):
            at = (blk ^ i) * rows + r
            hidden_ref[pl.ds(at, 1)] = pieces[i][pl.ds(r, 1), :block, :]
            tail = pieces[i][r, block:, :].astype(F32)
            pooled_ref[pl.ds(at, 1)] = (tail[:NSEG] + tail[NSEG:]).reshape(1, NSEG, D)


def place_hidden(pieces, place=own_place):
    nblk = len(pieces)
    rows, block, _ = pieces[0].shape
    block -= 2 * NSEG
    return call(
        functools.partial(place_hidden_kernel, nblk=nblk, rows=rows, block=block, place=place),
        "place_hidden",
        (1,),
        [whole((rows, block + 2 * NSEG, D))] * nblk,
        [(whole((rows * nblk, block, D)), (rows * nblk, block, D), BF), (whole((rows * nblk, NSEG, D)), (rows * nblk, NSEG, D), F32)],
        flops=1e9,
    )(*pieces)


def place_tokens_kernel(*refs, nblk, rows, place):
    pieces, out_ref = refs[:nblk], refs[nblk]
    blk = place()[2]
    for i in range(nblk):
        for r in range(rows):
            out_ref[pl.ds((blk ^ i) * rows + r, 1)] = pieces[i][pl.ds(r, 1)].astype(F32)


def place_tokens(pieces, place=own_place):
    nblk = len(pieces)
    rows, block, _ = pieces[0].shape
    return call(
        functools.partial(place_tokens_kernel, nblk=nblk, rows=rows, place=place),
        "place_tokens",
        (1,),
        [whole((rows, block, D))] * nblk,
        [(whole((rows * nblk, block, D)), (rows * nblk, block, D), F32)],
        flops=1e9,
    )(*pieces)[0]


def unpack_kernel(half_ref, *refs, flip, place, orders):
    out_ref = refs[-1]
    core, here_block, _ = place()
    rows = half_ref.shape[1]
    count = out_ref.shape[0] // rows
    for i in range(count):
        slot = slot_of(orders, core ^ flip, pl.program_id(0) * count + i, here_block)
        out_ref[i * rows : (i + 1) * rows, :] = half_ref[slot].astype(F32)


def unpack_feed(half, by_rows, flip, before, orders, place=own_place):
    _, rows, cols = half.shape
    parts = 4
    core = lambda: place()[0] ^ flip
    tall = rows * BLOCKS
    shape, index = (
        ((2 * tall, cols), lambda q: (core() * parts + q, 0)) if by_rows else ((tall, 2 * cols), lambda q: (q, core()))
    )
    extra = [] if before is None else [before]
    return call(
        functools.partial(unpack_kernel, flip=flip, place=place, orders=orders),
        "unpack_feed",
        (parts,),
        [whole(half.shape)] + [ANY] * len(extra),
        [(pl.BlockSpec((tall // parts, cols), index), shape, F32)],
        aliases={1: 0} if extra else None,
        flops=2e9,
    )(half, *extra)[0]


def unpack_heads_kernel(half_ref, *refs, flip, place, orders):
    output_ref, input_ref = refs[-2:]
    core, here_block, _ = place()
    rows = D // BLOCKS
    step = pl.program_id(0)

    def fill(out_ref):
        cols = pl.ds(pl.multiple_of(step * PAIR, 128), PAIR)
        for i in range(BLOCKS):
            slot = slot_of(orders, core ^ flip, i, here_block)
            out_ref[i * rows : (i + 1) * rows, :] = half_ref[slot, :, cols].astype(F32)

    @pl.when(step < 3)
    def _():
        fill(output_ref)

    @pl.when(step >= 3)
    def _():
        fill(input_ref)


def unpack_heads(half, flip, before, orders, place=own_place):
    core = lambda: place()[0] ^ flip

    def input_index(j):
        k = jnp.maximum(j - 3, 0)
        return 0, (k % 3) * (H // 2) + 2 * (k // 3) + core()

    extra = [] if before is None else list(before)
    return call(
        functools.partial(unpack_heads_kernel, flip=flip, place=place, orders=orders),
        "unpack_heads",
        (half.shape[2] // PAIR,),
        [whole(half.shape)] + [ANY] * len(extra),
        [
            (pl.BlockSpec((D, PAIR), lambda j: (0, core() * 3 + jnp.minimum(j, 2))), (D, D), F32),
            (pl.BlockSpec((D, PAIR), input_index), (D, 3 * D), F32),
        ],
        aliases={1: 0, 2: 1} if extra else None,
        flops=2e9,
    )(half, *extra)


def exchange(array, bits):
    nblk, nrows = lax.axis_size("blk"), lax.axis_size("rows")
    moves = {"c": (0, 1), "y": (0, 2), "x": (1, 0), "a": (2, 0), "b": (4, 0)}
    pairs = []
    for i in range(nblk * nrows):
        row, blk = divmod(i, nblk)
        bit = bits[blk & 1]
        by_row, by_blk = moves[bit] if isinstance(bit, str) else (bit, 0)
        pairs.append((i, (row ^ by_row) * nblk + (blk ^ by_blk)))
    return lax.ppermute(array, ("rows", "blk"), pairs)


def added(left, right):
    return (left.astype(F32) + right.astype(F32)).astype(BF)


class Sum:
    def __init__(self, send, keep, orders):
        self.keep = keep
        extra = []
        bit = 8
        while bit < lax.axis_size("rows"):
            extra.append(bit)
            bit *= 2
        bits = [(orders[0][t], orders[1][t]) for t in range(4)]
        halves, wholes = bits[: orders[2]], bits[orders[2] :]
        self.plan = [("half", h) for h in halves] + [("all", w) for w in wholes] + [("all", (e, e)) for e in extra]
        self.plan += [("join", h) for h in reversed(halves)] + [("end", ("c", "c"))]
        self.moving = exchange(send, self.plan[0][1])
        self.stage = 0

    def busy(self):
        return self.stage < len(self.plan)

    def step(self, marks=()):
        if not self.busy():
            return []
        kind = self.plan[self.stage][0]
        (came,) = after([self.moving], marks)
        self.stage += 1
        if kind == "end":
            self.other = came
            return [self.other]
        if kind == "half":
            if self.plan[self.stage][0] == "half":
                n = self.keep.shape[0] // 2
                send, self.keep = added(self.keep[n:], came[n:]), added(self.keep[:n], came[:n])
            else:
                send = self.now = added(self.keep, came)
        elif kind == "all":
            send = self.now = added(self.now, came)
        else:
            send = self.now = jnp.concatenate([self.now, came], axis=0)
        self.moving = exchange(send, self.plan[self.stage][1])
        return [send]

    def last(self):
        return self.stage == len(self.plan) - 1


class Vectors:
    def __init__(self, value):
        self.value = value
        bit = 8
        self.left = ["c", "y", "x", "a", "b"]
        while bit < lax.axis_size("rows"):
            self.left.append(bit)
            bit *= 2

    def step(self, marks=()):
        if self.left:
            bit = self.left.pop(0)
            (here,) = after([self.value], marks)
            self.value = here + exchange(here, (bit, bit))
        return [self.value]

    def finish(self):
        while self.left:
            self.step()
        return self.value


def after(arrays, *marks):
    marks = [m for mark in marks for m in mark]
    return list(lax.optimization_barrier(tuple(arrays) + tuple(marks))[: len(arrays)])


def pieces_of(array, me, nblk):
    rows = array.shape[0] // nblk
    return [lax.dynamic_slice_in_dim(array, (me ^ k) * rows, rows, axis=0) for k in range(nblk)]


def swap(pieces):
    nblk = len(pieces)
    return [pieces[0]] + [
        lax.ppermute(pieces[k], "blk", [(i, i ^ k) for i in range(nblk)]) for k in range(1, nblk)
    ]


def on_device(
    tokens,
    lengths,
    input_weight,
    query_bias,
    value_bias,
    output_weight,
    output_bias,
    first_gain,
    first_shift,
    up_weight,
    up_bias,
    down_weight,
    down_bias,
    second_gain,
    second_shift,
    out_grad,
    pool_grad,
):
    nblk = lax.axis_size("blk")
    me = lax.axis_index("blk")
    rows = tokens.shape[0] // nblk
    row = lambda v: v.reshape(1, -1)
    g1, b1 = row(first_gain), row(first_shift)
    bias = row(jnp.concatenate([query_bias, jnp.zeros_like(query_bias), value_bias]))
    own_lengths = lax.dynamic_slice_in_dim(lengths, me * rows, rows, axis=0)
    own_pool = lax.dynamic_slice_in_dim(pool_grad, me * rows, rows, axis=0)
    pieces = swap(pieces_of(tokens, me, nblk))
    grads = swap(pieces_of(out_grad, me, nblk))
    twin = lambda a: exchange(a, ("c", "c"))
    x, packed, mixed, first_in = attention_forward(
        own_lengths, pieces, input_weight, bias, output_weight, row(output_bias)
    )
    came_x, came_mixed = twin(x), twin(mixed)
    *hidden, low, active, active_outer, inner, inner_other, grad_first_in, grad_mixed, branch, branch_other, vec1, ups = feed(
        own_lengths, first_in, own_pool, grads, up_weight, row(up_bias), down_weight, row(down_bias), output_weight,
        g1, b1, row(second_gain), row(second_shift),
    )
    came_active = twin(active_outer)
    came_low, came_inner, came_branch = twin(low), twin(inner_other), twin(branch_other)
    hidden = swap(hidden)

    def attention(group, marks):
        grad_packed, other, sums = attention_back(own_lengths, packed, after([grad_mixed], marks)[0], nblk, group)
        return grad_packed, twin(other), sums[0].reshape(2, 3, PAIR)

    gp0, came0, vec_a = attention(0, [])
    active, came_active = after([active, came_active], [gp0])
    send, keep = down_gradient(active, active_outer, came_active, DOWN_ORDER)
    down = Sum(send, keep, DOWN_ORDER)
    (inner,) = after([inner], [keep])
    send, keep = up_gradient(low, inner, came_low, came_inner, UP_ORDER)
    up = Sum(send, keep, UP_ORDER)
    gp1, came1, vec_b = attention(1, [keep] + hidden)
    m = down.step([gp1])
    gp2, came2, vec_c = attention(2, m)
    m = up.step(down.step([gp2]))
    (mixed,) = after([mixed], m)
    send, keep = head_gradient(
        [mixed, came_mixed, x, came_x], [branch, gp0, gp1, gp2], [came_branch, came0, came1, came2], HEAD_ORDER
    )
    heads = Sum(send, keep, HEAD_ORDER)
    m = up.step(down.step([keep]))
    sections = jnp.concatenate([vec_a, vec_b, vec_c], axis=0)
    vecs = Vectors(
        jnp.concatenate(
            [sections[:, 0].reshape(1, D), sections[:, 2].reshape(1, D), vec1[:6], ups[0].reshape(-1, D)], axis=0
        )
    )
    gp0, gp1, gp2, vecs.value = after([gp0, gp1, gp2, vecs.value], m)
    tokens_pieces = tokens_gradient([gp0, gp1, gp2], grad_first_in, input_weight, nblk, rows)
    tokens_grad = swap(tokens_pieces)
    m = tokens_pieces[:1]
    sums = {"d": down, "u": up, "r": heads, "v": vecs}
    held = {"down": None, "up": None, "heads": None}
    for action in TAIL:
        if action in sums:
            m = sums[action].step(m)
        elif action == "h":
            hidden_out, pooled = place_hidden(after(hidden, m))
            m = [hidden_out]
        elif action == "t":
            tokens_out = place_tokens(after(tokens_grad, m))
            m = [tokens_out]
        else:
            which, flip = divmod(int(action) - 1, 2)
            total = (down, up, heads)[which]
            while not total.last() and total.busy() or (flip and total.busy()):
                m = total.step(m)
            (half,) = after([total.other if flip else total.now], m)
            if which == 0:
                held["down"] = unpack_feed(half, True, flip, held["down"], DOWN_ORDER)
                m = [held["down"]]
            elif which == 1:
                held["up"] = unpack_feed(half, False, flip, held["up"], UP_ORDER)
                m = [held["up"]]
            else:
                held["heads"] = unpack_heads(half, flip, held["heads"], HEAD_ORDER)
                m = held["heads"]
    down_grad, up_grad, (output_grad, input_grad) = held["down"], held["up"], held["heads"]
    vecs = vecs.finish()
    return (
        hidden_out,
        pooled,
        tokens_out,
        input_grad,
        vecs[0],
        vecs[1],
        output_grad,
        vecs[4],
        vecs[2],
        vecs[3],
        up_grad,
        vecs[8:12].reshape(-1),
        down_grad,
        vecs[7],
        vecs[5],
        vecs[6],
    )


def solution(mesh):
    whole_rows = P("rows", "blk", None)
    rest = (P(),) * 13
    return jax.shard_map(
        on_device,
        mesh=mesh,
        in_specs=(whole_rows, P("rows", None)) + rest + (whole_rows, P("rows", None, None)),
        out_specs=(whole_rows, P("rows", None, None), whole_rows) + rest,
        check_vma=False,
    )
```

```python
import functools
import jax
import jax.numpy as jnp
from jax import lax
from jax.experimental import pallas as pl
from jax.experimental.pallas import tpu as pltpu
from jax.sharding import PartitionSpec as P

D = 768
H = 12
DH = 64
FF = 3072
NSEG = 8
PAIR = 2 * DH
NORM_EPS = 1e-12
BIG = 1e9
BF = jnp.bfloat16
F32 = jnp.float32
CHUNK = 768
VMEM_LIMIT = 60 * 1024 * 1024


def nn(a, b):
    return lax.dot_general(a, b, (((1,), (0,)), ((), ())), preferred_element_type=F32)


def nt(a, b):
    return lax.dot_general(a, b, (((1,), (1,)), ((), ())), preferred_element_type=F32)


def tn(a, b):
    return lax.dot_general(a, b, (((0,), (0,)), ((), ())), preferred_element_type=F32)


def col_sum(a):
    return jnp.sum(a, axis=0, keepdims=True)


def norm_parts(hidden):
    center = hidden - jnp.mean(hidden, axis=-1, keepdims=True)
    spread = jnp.mean(center * center, axis=-1, keepdims=True)
    inverse = lax.rsqrt(spread + NORM_EPS)
    return center * inverse, inverse


def norm_back(grad, gain, unit, inverse):
    scaled = grad * gain
    along = jnp.mean(scaled * unit, axis=-1, keepdims=True)
    return inverse * (scaled - jnp.mean(scaled, axis=-1, keepdims=True) - unit * along)


def segments(lengths_ref, row, length, count, nblk, me, first=0):
    shape = (count, PAIR)
    local = lax.broadcasted_iota(jnp.int32, shape, 0) + first
    block = length // nblk
    places = ((local // block) ^ me) * block + local % block
    end = jnp.int32(0)
    labels = jnp.zeros(shape, jnp.int32)
    for c in range(NSEG):
        end = end + lengths_ref[row, c]
        labels = labels + (places >= end).astype(jnp.int32)
    return labels == lax.broadcasted_iota(jnp.int32, shape, 1)


def head_masks(length):
    lane = lax.broadcasted_iota(jnp.int32, (length, PAIR), 1)
    return lane < DH, lane >= DH


PLACE = {"y": 0, "x": 1, "a": 2, "b": 3}
BLOCKS = 16
DOWN_ORDER = ("xyab", "yxab", 3)
UP_ORDER = ("xyab", "yxab", 3)
HEAD_ORDER = ("xyab", "yxab", 3)
TAIL = "duhrsdurwvudvrutvrvdrv1durv2u34vr5r6"


def own_place():
    blk = lax.axis_index("blk")
    rows = lax.axis_index("rows")
    return blk & 1, ((rows & 7) << 1) | ((blk >> 1) & 1), blk


def slot_in(order, halved, block, here):
    slot = 0
    for t, bit in enumerate(order):
        at = block ^ here if t < halved else block
        slot = slot | (((at >> PLACE[bit]) & 1) << (3 - t))
    return slot


def slot_of(orders, core, block, here):
    return jnp.where(
        core == 0, slot_in(orders[0], orders[2], block, here), slot_in(orders[1], orders[2], block, here)
    )


def hand_out(slots_ref, send_ref, keep_ref, sems):
    half = BLOCKS // 2
    copies = [
        pltpu.make_async_copy(slots_ref.at[pl.ds(half, half)], send_ref, sems.at[0]),
        pltpu.make_async_copy(slots_ref.at[pl.ds(0, half)], keep_ref, sems.at[1]),
    ]
    for c in copies:
        c.start()
    for c in copies:
        c.wait()


def whole(shape):
    return pl.BlockSpec(shape, lambda *_: (0,) * len(shape), pipeline_mode=pl.Buffered(1))


def per_row(*shape):
    return pl.BlockSpec((1,) + shape, lambda r: (r,) + (0,) * len(shape))


def flat(*shape):
    return pl.BlockSpec(shape, lambda r: (r,) + (0,) * (len(shape) - 1))


SMEM = pl.BlockSpec(memory_space=pltpu.SMEM)
ANY = pl.BlockSpec(memory_space=pl.ANY)


def slots(rows, cols):
    half = (ANY, (BLOCKS // 2, rows, cols), BF)
    return [half, half], [pltpu.VMEM((BLOCKS, rows, cols), BF), pltpu.SemaphoreType.DMA((2,))]


def shape_of(shape, dtype):
    return jax.ShapeDtypeStruct(shape, dtype)


def call(kernel, name, grid, in_specs, outs, scratch=(), flops=0, nbytes=0, aliases=None):
    return pl.pallas_call(
        kernel,
        grid=grid,
        in_specs=in_specs,
        out_specs=[o[0] for o in outs],
        out_shape=[shape_of(o[1], o[2]) for o in outs],
        scratch_shapes=scratch,
        input_output_aliases=aliases or {},
        compiler_params=pltpu.CompilerParams(vmem_limit_bytes=VMEM_LIMIT),
        cost_estimate=pl.CostEstimate(flops=int(flops), bytes_accessed=int(nbytes), transcendentals=0),
        name=name,
    )


def attention_kernel(lengths_ref, *refs, nblk, place, row):
    pieces = refs[:nblk]
    w_in_ref, bias_ref, w_out_ref, out_bias_ref = refs[nblk : nblk + 4]
    both_ref, packed_ref, first_in_ref = refs[-3:]
    block = pieces[0].shape[1]
    length = block * nblk
    for i in range(nblk):
        both_ref[pl.ds(i * block, block), :D] = pieces[i][0]
    x = both_ref[:, :D]
    for c in range(3):
        cols = pl.ds(c * D, D)
        packed_ref[0, :, cols] = (nn(x, w_in_ref[:, cols]) + bias_ref[:, cols]).astype(BF)
    hit = segments(lengths_ref, row, length, length, nblk, place()[2])
    here = jnp.where(hit, 1.0, 0.0).astype(BF)
    away = jnp.where(hit, 0.0, -BIG).astype(BF)
    masks = head_masks(length)
    for j in range(H // 2):
        q = packed_ref[0, :, pl.ds(j * PAIR, PAIR)] * jnp.asarray(DH**-0.5, BF)
        k = packed_ref[0, :, pl.ds(D + j * PAIR, PAIR)]
        v = packed_ref[0, :, pl.ds(2 * D + j * PAIR, PAIR)]
        k_aug = jnp.concatenate([k, away], axis=1)
        zero = jnp.zeros_like(q)
        weights, totals = [], []
        for h in range(2):
            s = nt(jnp.concatenate([jnp.where(masks[h], q, zero), here], axis=1), k_aug)
            e = jnp.exp(s - jnp.max(s, axis=1, keepdims=True))
            totals.append(jnp.sum(e, axis=1, keepdims=True))
            weights.append(e.astype(BF))
        values = jnp.concatenate([jnp.where(m, v, zero) for m in masks], axis=0)
        out = nn(jnp.concatenate(weights, axis=1), values) / jnp.where(masks[0], totals[0], totals[1])
        both_ref[:, pl.ds(D + j * PAIR, PAIR)] = out.astype(BF)
    branch = nn(both_ref[:, D:], w_out_ref[...]) + out_bias_ref[...]
    first_in_ref[...] = x.astype(F32) + branch


def attention_forward(lengths, pieces, w_in, bias, w_out, out_bias, rows, row, before, place=own_place):
    nblk = len(pieces)
    block = pieces[0].shape[1]
    length = block * nblk
    extra = list(before)
    return call(
        functools.partial(attention_kernel, nblk=nblk, place=place, row=row),
        "attention_forward",
        (1,),
        [SMEM] + [per_row(block, D)] * nblk + [whole((D, 3 * D)), whole((1, 3 * D)), whole((D, D)), whole((1, D))]
        + [ANY] * len(extra),
        [
            (pl.BlockSpec((length, 2 * D), lambda r: (row, 0)), (rows * length, 2 * D), BF),
            (pl.BlockSpec((1, length, 3 * D), lambda r: (row, 0, 0)), (rows, length, 3 * D), BF),
            (pl.BlockSpec((length, D), lambda r: (row, 0)), (rows * length, D), F32),
        ],
        aliases={nblk + 5 + n: n for n in range(len(extra))},
        flops=9e9,
    )(lengths, *pieces, w_in, bias, w_out, out_bias, *extra)


def gelu_both(x):
    cdf = 0.5 + 0.5 * lax.erf(x * (0.5**0.5))
    density = jnp.exp(x * x * -0.5) * 0.3989422804014327
    return x * cdf, cdf + x * density


def feed_kernel(lengths_ref, first_in_ref, pool_grad_ref, *refs, nblk, place):
    grad_pieces = refs[:nblk]
    (w_up_ref, up_bias_ref, w_down_ref, down_bias_ref, w_out_ref, g1_ref, b1_ref, g2_ref, b2_ref) = refs[nblk : nblk + 9]
    hidden = refs[nblk + 9 : 2 * nblk + 9]
    (active_own_ref, active_other_ref, inner_own_ref, other_ref, low_own_ref, grad_first_in_ref, grad_mixed_ref,
     branch_own_ref, vec_ref, up_sums_ref, slope_ref, branch_ref, pooled_ref) = refs[2 * nblk + 9 :]
    step = pl.program_id(0)
    r, part = step // 2, step % 2
    count = first_in_ref.shape[0]
    block = hidden[0].shape[1] - 2 * NSEG
    length = block * nblk
    some = nblk // 2
    half = FF // 2
    core, _, blk = place()
    chunks = [(flip, c) for flip in (1, 0) for c in range(half // CHUNK)]

    def units(flip, c):
        return pl.ds(pl.multiple_of((core ^ flip) * half + c * CHUNK, 128), CHUNK)


    unit1, inverse1 = norm_parts(first_in_ref[...])
    first = unit1 * g1_ref[...] + b1_ref[...]
    low = first.astype(BF)
    low_own_ref[...] = low
    other_ref[:, half : half + D] = low
    acc = first + down_bias_ref[...]
    for flip, c in chunks:
        cols, at = units(flip, c), pl.ds(c * CHUNK, CHUNK)
        inner = nn(low, w_up_ref[:, cols]) + up_bias_ref[:, cols]
        act, slope = gelu_both(inner)
        act = act.astype(BF)
        (active_other_ref if flip else active_own_ref)[:, at] = act
        slope_ref[flip, :, at] = slope.astype(BF)
        acc = acc + nn(act, w_down_ref[cols, :])
    unit, inverse = norm_parts(acc)
    result = unit * g2_ref[...] + b2_ref[...]
    high = result.astype(BF)
    here = jnp.where(segments(lengths_ref, r, length, count, nblk, blk, part * count), 1.0, 0.0).astype(BF)
    rest = (result - high.astype(F32)).astype(BF)
    sums = (tn(here, high) + tn(here, rest))[:NSEG]
    sub = lax.broadcasted_iota(jnp.int32, (NSEG, 1), 0)
    counts = jnp.zeros((NSEG, 1), F32)
    for c in range(NSEG):
        counts = jnp.where(sub == c, lengths_ref[r, c].astype(F32), counts)

    @pl.when(part == 0)
    def _():
        pooled_ref[...] = sums
        for i in range(some):
            hidden[i][0, :block, :] = high[i * block : (i + 1) * block]

    @pl.when(part == 1)
    def _():
        pooled = (pooled_ref[...] + sums) / counts
        pooled_high = pooled.astype(BF)
        both = jnp.concatenate([pooled_high.astype(F32), pooled - pooled_high.astype(F32)], axis=0).astype(BF)
        for i in range(some):
            hidden[some + i][0, :block, :] = high[i * block : (i + 1) * block]
        for i in range(nblk):
            hidden[i][0, block:, :] = both

    share = pool_grad_ref[0].astype(F32) / counts
    share_high = share.astype(BF)
    share_rest = (share - share_high.astype(F32)).astype(BF)
    pad = jnp.zeros((PAIR - NSEG, D), BF)
    spread = nn(here, jnp.concatenate([share_high, pad], axis=0)) + nn(here, jnp.concatenate([share_rest, pad], axis=0))
    given = jnp.where(
        part == 0,
        jnp.concatenate([g[0] for g in grad_pieces[:some]], axis=0).astype(F32),
        jnp.concatenate([g[0] for g in grad_pieces[some:]], axis=0).astype(F32),
    )
    grad = given + spread
    acc = norm_back(grad, g2_ref[...], unit, inverse)
    outer = acc.astype(BF)
    active_other_ref[:, half:] = outer
    sums2 = [col_sum(grad * unit), col_sum(grad), col_sum(outer.astype(F32))]
    @pl.when(step == 0)
    def _():
        up_sums_ref[...] = jnp.zeros_like(up_sums_ref)

    for flip, c in chunks:
        cols, at = units(flip, c), pl.ds(c * CHUNK, CHUNK)
        inner = (nt(outer, w_down_ref[cols, :]) * slope_ref[flip, :, at].astype(F32)).astype(BF)
        (other_ref if flip else inner_own_ref)[:, at] = inner
        up_sums_ref[:1, cols] += col_sum(inner.astype(F32))
        acc = acc + nt(inner, w_up_ref[:, cols])
    grad_first_in = norm_back(acc, g1_ref[...], unit1, inverse1)
    grad_first_in_ref[...] = grad_first_in
    branch = grad_first_in.astype(BF)
    branch_ref[...] = branch
    branch_own_ref[...] = branch_ref[:, pl.ds(pl.multiple_of(core * (D // 2), 128), D // 2)]
    other_ref[:, half + D :] = branch_ref[:, pl.ds(pl.multiple_of((core ^ 1) * (D // 2), 128), D // 2)]
    grad_mixed_ref[...] = nt(branch, w_out_ref[...]).astype(BF)
    sums1 = [col_sum(acc * unit1), col_sum(acc), col_sum(branch.astype(F32))]
    vec = jnp.concatenate(sums1 + sums2 + [jnp.zeros((2, D), F32)], axis=0)

    @pl.when(step == 0)
    def _():
        vec_ref[...] = vec

    @pl.when(step != 0)
    def _():
        vec_ref[...] += vec


def feed(lengths, first_in, pool_grad, grads, w_up, up_bias, w_down, down_bias, w_out, g1, b1, g2, b2, place=own_place):
    nblk = len(grads)
    rows, block, _ = grads[0].shape
    total = first_in.shape[0]
    tile = block * nblk // 2
    vec = whole((1, D))

    def row(*shape):
        return pl.BlockSpec((1,) + shape, lambda i: (i // 2,) + (0,) * len(shape))

    def out(cols, dtype=BF):
        return flat(tile, cols), (total, cols), dtype

    half = FF // 2
    return call(
        functools.partial(feed_kernel, nblk=nblk, place=place),
        "feed",
        (total // tile,),
        [SMEM, flat(tile, D), row(NSEG, D)] + [row(block, D)] * nblk
        + [whole((D, FF)), whole((1, FF)), whole((FF, D)), vec, whole((D, D)), vec, vec, vec, vec],
        [(row(block + 2 * NSEG, D), (rows, block + 2 * NSEG, D), BF)] * nblk
        + [out(half), out(half + D), out(half), out(half + D + D // 2), out(D), out(D, F32), out(D), out(D // 2),
           (whole((8, D)), (8, D), F32), (whole((8, FF)), (8, FF), F32)],
        scratch=[pltpu.VMEM((2, tile, half), BF), pltpu.VMEM((tile, D), BF), pltpu.VMEM((NSEG, D), F32)],
        flops=40e9,
    )(lengths, first_in, pool_grad, *grads, w_up, up_bias, w_down, down_bias, w_out, g1, b1, g2, b2)


def down_kernel(
    active_ref, outer_ref, came_active_ref, came_outer_ref, send_ref, keep_ref, slots_ref, sems, place, orders
):
    step = pl.program_id(0)
    core, here_block, _ = place()
    rows = slots_ref.shape[1]
    here = active_ref.shape[1] // rows
    tile = (tn(active_ref[...], outer_ref[...]) + tn(came_active_ref[...], came_outer_ref[...])).astype(BF)
    for i in range(here):
        slots_ref[slot_of(orders, core, step * here + i, here_block)] = tile[i * rows : (i + 1) * rows]

    @pl.when(step == pl.num_programs(0) - 1)
    def _():
        hand_out(slots_ref, send_ref, keep_ref, sems)


def down_gradient(active, mine, came, orders, place=own_place):
    total, half = active.shape
    outs, scratch = slots(half // BLOCKS, D)
    wide = 384
    part = pl.BlockSpec((total, wide), lambda j: (0, j))
    outer = pl.BlockSpec((total, D), lambda j: (0, half // D), pipeline_mode=pl.Buffered(1))
    return call(
        functools.partial(down_kernel, place=place, orders=orders),
        "down_gradient",
        (half // wide,),
        [part, outer, part, outer],
        outs,
        scratch=scratch,
        flops=6e9,
    )(active, mine, came, came)


def up_kernel(low_ref, inner_ref, came_low_ref, came_inner_ref, send_ref, keep_ref, slots_ref, sems, place, orders):
    step = pl.program_id(0)
    core, here_block, _ = place()
    rows = slots_ref.shape[1]
    wide = inner_ref.shape[1]
    tile = (tn(low_ref[...], inner_ref[...]) + tn(came_low_ref[...], came_inner_ref[...])).astype(BF)
    cols = pl.ds(pl.multiple_of(step * wide, 128), wide)
    for i in range(BLOCKS):
        slots_ref[slot_of(orders, core, i, here_block), :, cols] = tile[i * rows : (i + 1) * rows]

    @pl.when(step == pl.num_programs(0) - 1)
    def _():
        hand_out(slots_ref, send_ref, keep_ref, sems)


def up_gradient(low, inner, came, orders, place=own_place):
    total, half = inner.shape
    outs, scratch = slots(D // BLOCKS, half)
    wide = 512
    part = pl.BlockSpec((total, wide), lambda j: (0, j))
    came_low = pl.BlockSpec((total, D), lambda j: (0, half // D), pipeline_mode=pl.Buffered(1))
    return call(
        functools.partial(up_kernel, place=place, orders=orders),
        "up_gradient",
        (half // wide,),
        [whole((total, D)), part, came_low, part],
        outs,
        scratch=scratch,
        flops=6e9,
    )(low, inner, came, came)


def attention_back_kernel(lengths_ref, *refs, nblk, place):
    q_ref, k_ref, v_ref, gm_ref, grads_ref, other_ref, vec_ref = refs
    r = pl.program_id(0)
    core, _, blk = place()
    length = q_ref.shape[1]
    wide = 3 * PAIR
    hit = segments(lengths_ref, r, length, length, nblk, blk)
    here = jnp.where(hit, 1.0, 0.0).astype(BF)
    away = jnp.where(hit, 0.0, -BIG).astype(BF)
    masks = head_masks(length)
    scale = DH**-0.5
    for j in range(2):
        lanes = slice(j * PAIR, (j + 1) * PAIR)
        q = q_ref[0, :, lanes] * jnp.asarray(scale, BF)
        k = k_ref[0, :, lanes]
        v = v_ref[0, :, lanes]
        gm = gm_ref[:, lanes]
        k_aug = jnp.concatenate([k, away], axis=1)
        zero = jnp.zeros_like(q)
        probs, slopes, queries, keys, mixes = [], [], [], [], []
        for h in range(2):
            qh = jnp.where(masks[h], q, zero)
            kh = jnp.where(masks[h], k, zero)
            gmh = jnp.where(masks[h], gm, zero)
            s = nt(k_aug, jnp.concatenate([qh, here], axis=1))
            e = jnp.exp(s - jnp.max(s, axis=0, keepdims=True))
            p = e * (1.0 / jnp.sum(e, axis=0, keepdims=True))
            gp = nt(v, gmh)
            delta = jnp.sum(gp * p, axis=0, keepdims=True)
            slopes.append((p * (gp - delta)).astype(BF))
            probs.append(p.astype(BF))
            queries.append(qh)
            keys.append(kh)
            mixes.append(gmh)
        both = jnp.concatenate(slopes, axis=1)
        gv = nn(jnp.concatenate(probs, axis=1), jnp.concatenate(mixes, axis=0))
        gk = nn(both, jnp.concatenate(queries, axis=0))
        gq = nn(jnp.concatenate([x.T for x in keys], axis=1), jnp.concatenate(slopes, axis=0)).T
        grads = jnp.concatenate([(gq * scale).astype(BF), gk.astype(BF), gv.astype(BF)], axis=1)
        at = pl.ds(j * wide, wide)
        grads_ref[:, at] = grads
        sums = jnp.concatenate([col_sum(grads.astype(F32)), jnp.zeros((7, wide), F32)], axis=0)

        @pl.when(r == 0)
        def _():
            vec_ref[:, at] = sums

        @pl.when(r != 0)
        def _():
            vec_ref[:, at] += sums

    other_ref[...] = grads_ref[:, pl.ds(pl.multiple_of((core ^ 1) * wide, 128), wide)]


def attention_back(lengths, packed, grad_mixed, nblk, group, place=own_place):
    rows, length, _ = packed.shape
    total = rows * length

    def pairs(section):
        return pl.BlockSpec((1, length, 2 * PAIR), lambda r: (r, 0, section * (H // 4) + group))

    return call(
        functools.partial(attention_back_kernel, nblk=nblk, place=place),
        "attention_back",
        (rows,),
        [SMEM, pairs(0), pairs(1), pairs(2), pl.BlockSpec((length, 2 * PAIR), lambda r: (r, group))],
        [(flat(length, D), (total, D), BF), (flat(length, D // 2), (total, D // 2), BF), (whole((8, D)), (8, D), F32)],
        flops=12e9,
    )(lengths, packed, packed, packed, grad_mixed)


def head_gradient_kernel(
    both_ref, came_both_ref, branch_ref, came_rest_ref, *refs, groups, place, orders
):
    rights, came_rights = refs[:groups], refs[groups : 2 * groups]
    send_ref, keep_ref, held, right_held, slots_ref, sems, left_sems, right_sems = refs[2 * groups :]
    core, here_block, _ = place()
    wide = D // 2
    own = pl.ds(pl.multiple_of(core * wide, 128), wide)
    tokens, mixed, tail = pl.ds(0, D), pl.ds(D, D), pl.ds(came_rest_ref.shape[1] - wide, wide)
    pairs = [(branch_ref, came_rest_ref.at[:, tail])] + [(a.at[:, own], b) for a, b in zip(rights, came_rights)]
    left_loads = [
        pltpu.make_async_copy(ref.at[:, lanes], held.at[n], left_sems.at[n])
        for n, (ref, lanes) in enumerate(
            ((both_ref, mixed), (came_both_ref, mixed), (both_ref, tokens), (came_both_ref, tokens))
        )
    ]
    right_loads = [
        pltpu.make_async_copy(ref, right_held.at[n, side], right_sems.at[2 * n + side])
        for n, pair in enumerate(pairs)
        for side, ref in enumerate(pair)
    ]
    for load in left_loads[:2] + right_loads[:2] + left_loads[2:] + right_loads[2:]:
        load.start()
    rows = D // BLOCKS
    for n in range(groups + 1):
        for load in (left_loads[2 * n : 2 * n + 2] if n < 2 else []) + right_loads[2 * n : 2 * n + 2]:
            load.wait()
        at = 0 if n == 0 else 2
        tile = (tn(held[at], right_held[n, 0]) + tn(held[at + 1], right_held[n, 1])).astype(BF)
        for i in range(BLOCKS):
            slot = slot_of(orders, core, i, here_block)
            slots_ref[slot, :, n * wide : (n + 1) * wide] = tile[i * rows : (i + 1) * rows]
    hand_out(slots_ref, send_ref, keep_ref, sems)


def head_gradient(both, came_both, branch, came_rest, grads, came_grads, orders, place=own_place):
    total = both.shape[0]
    groups = len(grads)
    wide = D // 2
    outs, scratch = slots(D // BLOCKS, (groups + 1) * wide)
    return call(
        functools.partial(head_gradient_kernel, groups=groups, place=place, orders=orders),
        "head_gradient",
        (1,),
        [ANY] * (4 + 2 * groups),
        outs,
        scratch=[pltpu.VMEM((4, total, D), BF), pltpu.VMEM((groups + 1, 2, total, wide), BF)] + scratch
        + [pltpu.SemaphoreType.DMA((4,)), pltpu.SemaphoreType.DMA((2 * groups + 2,))],
        flops=6e9,
    )(both, came_both, branch, came_rest, *grads, *came_grads)


def tokens_grad_kernel(*refs, groups, nblk):
    grads = refs[:groups]
    grad_first_in_ref, w_in_ref = refs[groups : groups + 2]
    outs = refs[groups + 2 : groups + 2 + nblk]
    all_ref = refs[-1]
    part = pl.program_id(0) % 2
    block = outs[0].shape[1]
    some = nblk // 2
    for g in range(groups):
        for j in range(2):
            for section in range(3):
                at = section * D + (2 * g + j) * PAIR
                start = (3 * j + section) * PAIR
                all_ref[:, at : at + PAIR] = grads[g][:, start : start + PAIR]
    total = (grad_first_in_ref[...] + nt(all_ref[...], w_in_ref[...])).astype(BF)
    for half in range(2):

        @pl.when(part == half)
        def _():
            for i in range(some):
                outs[half * some + i][0] = total[i * block : (i + 1) * block]


def tokens_gradient(grads, grad_first_in, w_in, nblk, rows):
    total = grad_first_in.shape[0]
    block = total // rows // nblk
    tile = total // rows // 2
    return call(
        functools.partial(tokens_grad_kernel, groups=len(grads), nblk=nblk),
        "tokens_gradient",
        (2 * rows,),
        [flat(tile, D)] * len(grads) + [flat(tile, D), whole((D, 3 * D))],
        [(pl.BlockSpec((1, block, D), lambda i: (i // 2, 0, 0)), (rows, block, D), BF)] * nblk,
        scratch=[pltpu.VMEM((tile, 3 * D), BF)],
        flops=5e9,
    )(*grads, grad_first_in, w_in)


def place_hidden_kernel(*refs, nblk, rows, block, place):
    pieces, (hidden_ref, pooled_ref) = refs[:nblk], refs[nblk:]
    blk = place()[2]
    for i in range(nblk):
        for r in range(rows):
            at = (blk ^ i) * rows + r
            hidden_ref[pl.ds(at, 1)] = pieces[i][pl.ds(r, 1), :block, :]
            tail = pieces[i][r, block:, :].astype(F32)
            pooled_ref[pl.ds(at, 1)] = (tail[:NSEG] + tail[NSEG:]).reshape(1, NSEG, D)


def place_hidden(pieces, place=own_place):
    nblk = len(pieces)
    rows, block, _ = pieces[0].shape
    block -= 2 * NSEG
    return call(
        functools.partial(place_hidden_kernel, nblk=nblk, rows=rows, block=block, place=place),
        "place_hidden",
        (1,),
        [whole((rows, block + 2 * NSEG, D))] * nblk,
        [(whole((rows * nblk, block, D)), (rows * nblk, block, D), BF), (whole((rows * nblk, NSEG, D)), (rows * nblk, NSEG, D), F32)],
        flops=1e9,
    )(*pieces)


def place_tokens_kernel(*refs, nblk, rows, place):
    pieces, out_ref = refs[:nblk], refs[nblk]
    blk = place()[2]
    for i in range(nblk):
        for r in range(rows):
            out_ref[pl.ds((blk ^ i) * rows + r, 1)] = pieces[i][pl.ds(r, 1)].astype(F32)


def place_tokens(pieces, place=own_place):
    nblk = len(pieces)
    rows, block, _ = pieces[0].shape
    return call(
        functools.partial(place_tokens_kernel, nblk=nblk, rows=rows, place=place),
        "place_tokens",
        (1,),
        [whole((rows, block, D))] * nblk,
        [(whole((rows * nblk, block, D)), (rows * nblk, block, D), F32)],
        flops=1e9,
    )(*pieces)[0]


def unpack_kernel(half_ref, *refs, flip, place, orders):
    out_ref = refs[-1]
    core, here_block, _ = place()
    rows = half_ref.shape[1]
    count = out_ref.shape[0] // rows
    for i in range(count):
        slot = slot_of(orders, core ^ flip, pl.program_id(0) * count + i, here_block)
        out_ref[i * rows : (i + 1) * rows, :] = half_ref[slot].astype(F32)


def unpack_feed(half, by_rows, flip, before, orders, place=own_place):
    _, rows, cols = half.shape
    parts = 4
    core = lambda: place()[0] ^ flip
    tall = rows * BLOCKS
    shape, index = (
        ((2 * tall, cols), lambda q: (core() * parts + q, 0)) if by_rows else ((tall, 2 * cols), lambda q: (q, core()))
    )
    extra = [] if before is None else [before]
    return call(
        functools.partial(unpack_kernel, flip=flip, place=place, orders=orders),
        "unpack_feed",
        (parts,),
        [whole(half.shape)] + [ANY] * len(extra),
        [(pl.BlockSpec((tall // parts, cols), index), shape, F32)],
        aliases={1: 0} if extra else None,
        flops=2e9,
    )(half, *extra)[0]


def unpack_heads_kernel(half_ref, *refs, flip, place, orders):
    output_ref, input_ref = refs[-2:]
    core, here_block, _ = place()
    rows = D // BLOCKS
    step = pl.program_id(0)

    def fill(out_ref):
        cols = pl.ds(pl.multiple_of(step * PAIR, 128), PAIR)
        for i in range(BLOCKS):
            slot = slot_of(orders, core ^ flip, i, here_block)
            out_ref[i * rows : (i + 1) * rows, :] = half_ref[slot, :, cols].astype(F32)

    @pl.when(step < 3)
    def _():
        fill(output_ref)

    @pl.when(step >= 3)
    def _():
        fill(input_ref)


def unpack_heads(half, flip, before, orders, place=own_place):
    core = lambda: place()[0] ^ flip

    def input_index(j):
        k = jnp.maximum(j - 3, 0)
        return 0, (k % 3) * (H // 2) + 2 * (k // 3) + core()

    extra = [] if before is None else list(before)
    return call(
        functools.partial(unpack_heads_kernel, flip=flip, place=place, orders=orders),
        "unpack_heads",
        (half.shape[2] // PAIR,),
        [whole(half.shape)] + [ANY] * len(extra),
        [
            (pl.BlockSpec((D, PAIR), lambda j: (0, core() * 3 + jnp.minimum(j, 2))), (D, D), F32),
            (pl.BlockSpec((D, PAIR), input_index), (D, 3 * D), F32),
        ],
        aliases={1: 0, 2: 1} if extra else None,
        flops=2e9,
    )(half, *extra)


def exchange(array, bits):
    nblk, nrows = lax.axis_size("blk"), lax.axis_size("rows")
    moves = {"c": (0, 1), "y": (0, 2), "x": (1, 0), "a": (2, 0), "b": (4, 0)}
    pairs = []
    for i in range(nblk * nrows):
        row, blk = divmod(i, nblk)
        bit = bits[blk & 1]
        by_row, by_blk = moves[bit] if isinstance(bit, str) else (bit, 0)
        pairs.append((i, (row ^ by_row) * nblk + (blk ^ by_blk)))
    return lax.ppermute(array, ("rows", "blk"), pairs)


def added(left, right):
    return (left.astype(F32) + right.astype(F32)).astype(BF)


class Sum:
    def __init__(self, send, keep, orders):
        self.keep = keep
        extra = []
        bit = 8
        while bit < lax.axis_size("rows"):
            extra.append(bit)
            bit *= 2
        bits = [(orders[0][t], orders[1][t]) for t in range(4)]
        halves, wholes = bits[: orders[2]], bits[orders[2] :]
        self.plan = [("half", h) for h in halves] + [("all", w) for w in wholes] + [("all", (e, e)) for e in extra]
        self.plan += [("join", h) for h in reversed(halves)] + [("end", ("c", "c"))]
        self.moving = exchange(send, self.plan[0][1])
        self.stage = 0

    def busy(self):
        return self.stage < len(self.plan)

    def step(self, marks=()):
        if not self.busy():
            return []
        kind = self.plan[self.stage][0]
        (came,) = after([self.moving], marks)
        self.stage += 1
        if kind == "end":
            self.other = came
            return [self.other]
        if kind == "half":
            if self.plan[self.stage][0] == "half":
                n = self.keep.shape[0] // 2
                send, self.keep = added(self.keep[n:], came[n:]), added(self.keep[:n], came[:n])
            else:
                send = self.now = added(self.keep, came)
        elif kind == "all":
            send = self.now = added(self.now, came)
        else:
            send = self.now = jnp.concatenate([self.now, came], axis=0)
        self.moving = exchange(send, self.plan[self.stage][1])
        return [send]

    def last(self):
        return self.stage == len(self.plan) - 1


class Vectors:
    def __init__(self, value):
        self.value = value
        bit = 8
        self.left = ["c", "y", "x", "a", "b"]
        while bit < lax.axis_size("rows"):
            self.left.append(bit)
            bit *= 2
        self.moving = None

    def step(self, marks=()):
        if self.moving is not None:
            (came,) = after([self.moving], marks)
            self.value = self.value + came
            self.moving = None
        elif marks:
            (self.value,) = after([self.value], marks)
        if self.left:
            bit = self.left.pop(0)
            self.moving = exchange(self.value, (bit, bit))
        return [self.value]

    def finish(self):
        while self.left or self.moving is not None:
            self.step()
        return self.value


def after(arrays, *marks):
    marks = [m for mark in marks for m in mark]
    return list(lax.optimization_barrier(tuple(arrays) + tuple(marks))[: len(arrays)])


def pieces_of(array, me, nblk, first=0, count=None):
    rows = array.shape[0] // nblk
    return [lax.dynamic_slice_in_dim(array, (me ^ k) * rows + first, count or rows, axis=0) for k in range(nblk)]


def swap(pieces):
    nblk = len(pieces)
    return [pieces[0]] + [
        lax.ppermute(pieces[k], "blk", [(i, i ^ k) for i in range(nblk)]) for k in range(1, nblk)
    ]


def on_device(
    tokens,
    lengths,
    input_weight,
    query_bias,
    value_bias,
    output_weight,
    output_bias,
    first_gain,
    first_shift,
    up_weight,
    up_bias,
    down_weight,
    down_bias,
    second_gain,
    second_shift,
    out_grad,
    pool_grad,
):
    nblk = lax.axis_size("blk")
    me = lax.axis_index("blk")
    rows = tokens.shape[0] // nblk
    row = lambda v: v.reshape(1, -1)
    g1, b1 = row(first_gain), row(first_shift)
    bias = row(jnp.concatenate([query_bias, jnp.zeros_like(query_bias), value_bias]))
    own_lengths = lax.dynamic_slice_in_dim(lengths, me * rows, rows, axis=0)
    own_pool = lax.dynamic_slice_in_dim(pool_grad, me * rows, rows, axis=0)
    pieces = []
    for r in range(rows):
        pieces.append(swap(after(pieces_of(tokens, me, nblk, r, 1), pieces[-1] if pieces else [])))
    grads = swap(after(pieces_of(out_grad, me, nblk), pieces[0]))
    twin = lambda a: exchange(a, ("c", "c"))
    made = ()
    for r in range(rows):
        made = attention_forward(
            own_lengths, pieces[r], input_weight, bias, output_weight, row(output_bias), rows, r, made
        )
    both, packed, first_in = made
    *hidden, active, active_outer, inner, inner_rest, low, grad_first_in, grad_mixed, branch, vec1, ups = feed(
        own_lengths, first_in, own_pool, grads, up_weight, row(up_bias), down_weight, row(down_bias), output_weight,
        g1, b1, row(second_gain), row(second_shift),
    )
    came_active, came_rest = twin(active_outer), twin(inner_rest)
    hidden = swap(hidden)

    def attention(group, marks):
        grad_packed, other, sums = attention_back(own_lengths, packed, after([grad_mixed], marks)[0], nblk, group)
        return grad_packed, other, sums[0].reshape(2, 3, PAIR)

    gp0, other0, vec_a = attention(0, [])
    active, came_active = after([active, came_active], [gp0])
    send, keep = down_gradient(active, active_outer, came_active, DOWN_ORDER)
    down = Sum(send, keep, DOWN_ORDER)
    (inner,) = after([inner], [keep] + hidden)
    send, keep = up_gradient(low, inner, came_rest, UP_ORDER)
    up = Sum(send, keep, UP_ORDER)
    came_both, came0 = [twin(a) for a in after([both, other0], [keep])]
    gp1, other1, vec_b = attention(1, [keep] + hidden)
    m = down.step([gp1])
    came1 = twin(other1)
    gp2, other2, vec_c = attention(2, m)
    came2 = twin(other2)
    m = up.step(down.step([gp2]))
    (both,) = after([both], m)
    send, keep = head_gradient(
        both, came_both, branch, came_rest, [gp0, gp1, gp2], [came0, came1, came2], HEAD_ORDER
    )
    heads = Sum(send, keep, HEAD_ORDER)
    m = up.step(down.step([keep]))
    sections = jnp.concatenate([vec_a, vec_b, vec_c], axis=0)
    vecs = Vectors(
        jnp.concatenate(
            [sections[:, 0].reshape(1, D), sections[:, 2].reshape(1, D), vec1[:6], ups[0].reshape(-1, D)], axis=0
        )
    )
    gp0, gp1, gp2, vecs.value = after([gp0, gp1, gp2, vecs.value], m)
    tokens_pieces = tokens_gradient([gp0, gp1, gp2], grad_first_in, input_weight, nblk, rows)
    m = tokens_pieces[:1]
    sums = {"d": down, "u": up, "r": heads, "v": vecs}
    held = {"down": None, "up": None, "heads": None}
    for action in TAIL:
        if action in sums:
            m = sums[action].step(m)
        elif action == "h":
            hidden_out, pooled = place_hidden(after(hidden, m))
            m = [hidden_out]
        elif action == "s":
            tokens_grad = after(tokens_pieces, m)
            halfway = twin(jnp.concatenate([tokens_grad[1], tokens_grad[3]], axis=0))
        elif action == "w":
            (halfway,) = after([halfway], m)
            far = jnp.concatenate([tokens_grad[2], halfway[rows:]], axis=0)
            m = [far]
            far = lax.ppermute(far, "blk", [(i, i ^ 2) for i in range(nblk)])
            tokens_grad = [tokens_grad[0], halfway[:rows], far[:rows], far[rows:]]
        elif action == "t":
            tokens_out = place_tokens(after(tokens_grad, m))
            m = [tokens_out]
        else:
            which, flip = divmod(int(action) - 1, 2)
            total = (down, up, heads)[which]
            while not total.last() and total.busy() or (flip and total.busy()):
                m = total.step(m)
            (half,) = after([total.other if flip else total.now], m)
            if which == 0:
                held["down"] = unpack_feed(half, True, flip, held["down"], DOWN_ORDER)
                m = [held["down"]]
            elif which == 1:
                held["up"] = unpack_feed(half, False, flip, held["up"], UP_ORDER)
                m = [held["up"]]
            else:
                held["heads"] = unpack_heads(half, flip, held["heads"], HEAD_ORDER)
                m = held["heads"]
    down_grad, up_grad, (output_grad, input_grad) = held["down"], held["up"], held["heads"]
    vecs = vecs.finish()
    return (
        hidden_out,
        pooled,
        tokens_out,
        input_grad,
        vecs[0],
        vecs[1],
        output_grad,
        vecs[4],
        vecs[2],
        vecs[3],
        up_grad,
        vecs[8:12].reshape(-1),
        down_grad,
        vecs[7],
        vecs[5],
        vecs[6],
    )


def solution(mesh):
    whole_rows = P("rows", "blk", None)
    rest = (P(),) * 13
    return jax.shard_map(
        on_device,
        mesh=mesh,
        in_specs=(whole_rows, P("rows", None)) + rest + (whole_rows, P("rows", None, None)),
        out_specs=(whole_rows, P("rows", None, None), whole_rows) + rest,
        check_vma=False,
    )
```

```python
import functools
import jax
import jax.numpy as jnp
from jax import lax
from jax.experimental import pallas as pl
from jax.experimental.pallas import tpu as pltpu
from jax.sharding import PartitionSpec as P

D = 768
H = 12
DH = 64
FF = 3072
NSEG = 8
PAIR = 2 * DH
NORM_EPS = 1e-12
BIG = 1e9
BF = jnp.bfloat16
F32 = jnp.float32
CHUNK = 768
VMEM_LIMIT = 60 * 1024 * 1024


def nn(a, b):
    return lax.dot_general(a, b, (((1,), (0,)), ((), ())), preferred_element_type=F32)


def nt(a, b):
    return lax.dot_general(a, b, (((1,), (1,)), ((), ())), preferred_element_type=F32)


def tn(a, b):
    return lax.dot_general(a, b, (((0,), (0,)), ((), ())), preferred_element_type=F32)


def col_sum(a):
    return jnp.sum(a, axis=0, keepdims=True)


def norm_parts(hidden):
    center = hidden - jnp.mean(hidden, axis=-1, keepdims=True)
    spread = jnp.mean(center * center, axis=-1, keepdims=True)
    inverse = lax.rsqrt(spread + NORM_EPS)
    return center * inverse, inverse


def norm_back(grad, gain, unit, inverse):
    scaled = grad * gain
    along = jnp.mean(scaled * unit, axis=-1, keepdims=True)
    return inverse * (scaled - jnp.mean(scaled, axis=-1, keepdims=True) - unit * along)


def segments(lengths_ref, row, length, count, nblk, me, first=0):
    shape = (count, PAIR)
    local = lax.broadcasted_iota(jnp.int32, shape, 0) + first
    block = length // nblk
    places = ((local // block) ^ me) * block + local % block
    end = jnp.int32(0)
    labels = jnp.zeros(shape, jnp.int32)
    for c in range(NSEG):
        end = end + lengths_ref[row, c]
        labels = labels + (places >= end).astype(jnp.int32)
    return labels == lax.broadcasted_iota(jnp.int32, shape, 1)


def head_masks(length):
    lane = lax.broadcasted_iota(jnp.int32, (length, PAIR), 1)
    return lane < DH, lane >= DH


PLACE = {"y": 0, "x": 1, "a": 2, "b": 3}
BLOCKS = 16
DOWN_ORDER = ("xyab", "yxab", 3)
UP_ORDER = ("xyab", "yxab", 3)
HEAD_ORDER = ("xyab", "yxab", 3)
TAIL = "duhrsdurwvudvrutvrvdrv1durv2u34vr5r6"


def own_place():
    blk = lax.axis_index("blk")
    rows = lax.axis_index("rows")
    return blk & 1, ((rows & 7) << 1) | ((blk >> 1) & 1), blk


def slot_in(order, halved, block, here):
    slot = 0
    for t, bit in enumerate(order):
        at = block ^ here if t < halved else block
        slot = slot | (((at >> PLACE[bit]) & 1) << (3 - t))
    return slot


def slot_of(orders, core, block, here):
    return jnp.where(
        core == 0, slot_in(orders[0], orders[2], block, here), slot_in(orders[1], orders[2], block, here)
    )


def hand_out(slots_ref, send_ref, keep_ref, sems):
    half = BLOCKS // 2
    copies = [
        pltpu.make_async_copy(slots_ref.at[pl.ds(half, half)], send_ref, sems.at[0]),
        pltpu.make_async_copy(slots_ref.at[pl.ds(0, half)], keep_ref, sems.at[1]),
    ]
    for c in copies:
        c.start()
    for c in copies:
        c.wait()


def whole(shape):
    return pl.BlockSpec(shape, lambda *_: (0,) * len(shape), pipeline_mode=pl.Buffered(1))


def per_row(*shape):
    return pl.BlockSpec((1,) + shape, lambda r: (r,) + (0,) * len(shape))


def flat(*shape):
    return pl.BlockSpec(shape, lambda r: (r,) + (0,) * (len(shape) - 1))


SMEM = pl.BlockSpec(memory_space=pltpu.SMEM)
ANY = pl.BlockSpec(memory_space=pl.ANY)


def slots(rows, cols):
    half = (ANY, (BLOCKS // 2, rows, cols), BF)
    return [half, half], [pltpu.VMEM((BLOCKS, rows, cols), BF), pltpu.SemaphoreType.DMA((2,))]


def shape_of(shape, dtype):
    return jax.ShapeDtypeStruct(shape, dtype)


def call(kernel, name, grid, in_specs, outs, scratch=(), flops=0, nbytes=0, aliases=None):
    return pl.pallas_call(
        kernel,
        grid=grid,
        in_specs=in_specs,
        out_specs=[o[0] for o in outs],
        out_shape=[shape_of(o[1], o[2]) for o in outs],
        scratch_shapes=scratch,
        input_output_aliases=aliases or {},
        compiler_params=pltpu.CompilerParams(vmem_limit_bytes=VMEM_LIMIT),
        cost_estimate=pl.CostEstimate(flops=int(flops), bytes_accessed=int(nbytes), transcendentals=0),
        name=name,
    )


def attention_kernel(lengths_ref, *refs, nblk, place, row):
    pieces = refs[:nblk]
    w_in_ref, bias_ref, w_out_ref, out_bias_ref = refs[nblk : nblk + 4]
    both_ref, packed_ref, first_in_ref = refs[-3:]
    block = pieces[0].shape[1]
    length = block * nblk
    for i in range(nblk):
        both_ref[pl.ds(i * block, block), :D] = pieces[i][0]
    x = both_ref[:, :D]
    for c in range(3):
        cols = pl.ds(c * D, D)
        packed_ref[0, :, cols] = (nn(x, w_in_ref[:, cols]) + bias_ref[:, cols]).astype(BF)
    hit = segments(lengths_ref, row, length, length, nblk, place()[2])
    here = jnp.where(hit, 1.0, 0.0).astype(BF)
    away = jnp.where(hit, 0.0, -BIG).astype(BF)
    masks = head_masks(length)
    for j in range(H // 2):
        q = packed_ref[0, :, pl.ds(j * PAIR, PAIR)] * jnp.asarray(DH**-0.5, BF)
        k = packed_ref[0, :, pl.ds(D + j * PAIR, PAIR)]
        v = packed_ref[0, :, pl.ds(2 * D + j * PAIR, PAIR)]
        k_aug = jnp.concatenate([k, away], axis=1)
        zero = jnp.zeros_like(q)
        weights, totals = [], []
        for h in range(2):
            s = nt(jnp.concatenate([jnp.where(masks[h], q, zero), here], axis=1), k_aug)
            e = jnp.exp(s - jnp.max(s, axis=1, keepdims=True))
            totals.append(jnp.sum(e, axis=1, keepdims=True))
            weights.append(e.astype(BF))
        values = jnp.concatenate([jnp.where(m, v, zero) for m in masks], axis=0)
        out = nn(jnp.concatenate(weights, axis=1), values) / jnp.where(masks[0], totals[0], totals[1])
        both_ref[:, pl.ds(D + j * PAIR, PAIR)] = out.astype(BF)
    branch = nn(both_ref[:, D:], w_out_ref[...]) + out_bias_ref[...]
    first_in_ref[...] = x.astype(F32) + branch


def attention_forward(lengths, pieces, w_in, bias, w_out, out_bias, rows, row, before, place=own_place):
    nblk = len(pieces)
    block = pieces[0].shape[1]
    length = block * nblk
    extra = list(before)
    return call(
        functools.partial(attention_kernel, nblk=nblk, place=place, row=row),
        "attention_forward",
        (1,),
        [SMEM] + [per_row(block, D)] * nblk + [whole((D, 3 * D)), whole((1, 3 * D)), whole((D, D)), whole((1, D))]
        + [ANY] * len(extra),
        [
            (pl.BlockSpec((length, 2 * D), lambda r: (row, 0)), (rows * length, 2 * D), BF),
            (pl.BlockSpec((1, length, 3 * D), lambda r: (row, 0, 0)), (rows, length, 3 * D), BF),
            (pl.BlockSpec((length, D), lambda r: (row, 0)), (rows * length, D), F32),
        ],
        aliases={nblk + 5 + n: n for n in range(len(extra))},
        flops=9e9,
    )(lengths, *pieces, w_in, bias, w_out, out_bias, *extra)


def gelu_both(x):
    cdf = 0.5 + 0.5 * lax.erf(x * (0.5**0.5))
    density = jnp.exp(x * x * -0.5) * 0.3989422804014327
    return x * cdf, cdf + x * density


def feed_kernel(lengths_ref, first_in_ref, pool_grad_ref, *refs, nblk, place):
    grad_pieces = refs[:nblk]
    (w_up_ref, up_bias_ref, w_down_ref, down_bias_ref, w_out_ref, g1_ref, b1_ref, g2_ref, b2_ref) = refs[nblk : nblk + 9]
    hidden = refs[nblk + 9 : 2 * nblk + 9]
    (active_own_ref, active_other_ref, inner_own_ref, other_ref, low_own_ref, grad_first_in_ref, grad_mixed_ref,
     branch_own_ref, vec_ref, up_sums_ref, slope_ref, branch_ref, pooled_ref) = refs[2 * nblk + 9 :]
    step = pl.program_id(0)
    r, part = step // 2, step % 2
    count = first_in_ref.shape[0]
    block = hidden[0].shape[1] - 2 * NSEG
    length = block * nblk
    some = nblk // 2
    half = FF // 2
    core, _, blk = place()
    chunks = [(flip, c) for flip in (1, 0) for c in range(half // CHUNK)]

    def units(flip, c):
        return pl.ds(pl.multiple_of((core ^ flip) * half + c * CHUNK, 128), CHUNK)


    unit1, inverse1 = norm_parts(first_in_ref[...])
    first = unit1 * g1_ref[...] + b1_ref[...]
    low = first.astype(BF)
    low_own_ref[...] = low
    other_ref[:, half : half + D] = low
    acc = first + down_bias_ref[...]
    for flip, c in chunks:
        cols, at = units(flip, c), pl.ds(c * CHUNK, CHUNK)
        inner = nn(low, w_up_ref[:, cols]) + up_bias_ref[:, cols]
        act, slope = gelu_both(inner)
        act = act.astype(BF)
        (active_other_ref if flip else active_own_ref)[:, at] = act
        slope_ref[flip, :, at] = slope.astype(BF)
        acc = acc + nn(act, w_down_ref[cols, :])
    unit, inverse = norm_parts(acc)
    result = unit * g2_ref[...] + b2_ref[...]
    high = result.astype(BF)
    here = jnp.where(segments(lengths_ref, r, length, count, nblk, blk, part * count), 1.0, 0.0).astype(BF)
    rest = (result - high.astype(F32)).astype(BF)
    sums = (tn(here, high) + tn(here, rest))[:NSEG]
    sub = lax.broadcasted_iota(jnp.int32, (NSEG, 1), 0)
    counts = jnp.zeros((NSEG, 1), F32)
    for c in range(NSEG):
        counts = jnp.where(sub == c, lengths_ref[r, c].astype(F32), counts)

    @pl.when(part == 0)
    def _():
        pooled_ref[...] = sums
        for i in range(some):
            hidden[i][0, :block, :] = high[i * block : (i + 1) * block]

    @pl.when(part == 1)
    def _():
        pooled = (pooled_ref[...] + sums) / counts
        pooled_high = pooled.astype(BF)
        both = jnp.concatenate([pooled_high.astype(F32), pooled - pooled_high.astype(F32)], axis=0).astype(BF)
        for i in range(some):
            hidden[some + i][0, :block, :] = high[i * block : (i + 1) * block]
        for i in range(nblk):
            hidden[i][0, block:, :] = both

    share = pool_grad_ref[0].astype(F32) / counts
    share_high = share.astype(BF)
    share_rest = (share - share_high.astype(F32)).astype(BF)
    pad = jnp.zeros((PAIR - NSEG, D), BF)
    spread = nn(here, jnp.concatenate([share_high, pad], axis=0)) + nn(here, jnp.concatenate([share_rest, pad], axis=0))
    given = jnp.where(
        part == 0,
        jnp.concatenate([g[0] for g in grad_pieces[:some]], axis=0).astype(F32),
        jnp.concatenate([g[0] for g in grad_pieces[some:]], axis=0).astype(F32),
    )
    grad = given + spread
    acc = norm_back(grad, g2_ref[...], unit, inverse)
    outer = acc.astype(BF)
    active_other_ref[:, half:] = outer
    sums2 = [col_sum(grad * unit), col_sum(grad), col_sum(outer.astype(F32))]
    @pl.when(step == 0)
    def _():
        up_sums_ref[...] = jnp.zeros_like(up_sums_ref)

    for flip, c in chunks:
        cols, at = units(flip, c), pl.ds(c * CHUNK, CHUNK)
        inner = (nt(outer, w_down_ref[cols, :]) * slope_ref[flip, :, at].astype(F32)).astype(BF)
        (other_ref if flip else inner_own_ref)[:, at] = inner
        up_sums_ref[:1, cols] += col_sum(inner.astype(F32))
        acc = acc + nt(inner, w_up_ref[:, cols])
    grad_first_in = norm_back(acc, g1_ref[...], unit1, inverse1)
    grad_first_in_ref[...] = grad_first_in
    branch = grad_first_in.astype(BF)
    branch_ref[...] = branch
    branch_own_ref[...] = branch_ref[:, pl.ds(pl.multiple_of(core * (D // 2), 128), D // 2)]
    other_ref[:, half + D :] = branch_ref[:, pl.ds(pl.multiple_of((core ^ 1) * (D // 2), 128), D // 2)]
    grad_mixed_ref[...] = nt(branch, w_out_ref[...]).astype(BF)
    sums1 = [col_sum(acc * unit1), col_sum(acc), col_sum(branch.astype(F32))]
    vec = jnp.concatenate(sums1 + sums2 + [jnp.zeros((2, D), F32)], axis=0)

    @pl.when(step == 0)
    def _():
        vec_ref[...] = vec

    @pl.when(step != 0)
    def _():
        vec_ref[...] += vec


def feed(lengths, first_in, pool_grad, grads, w_up, up_bias, w_down, down_bias, w_out, g1, b1, g2, b2, place=own_place):
    nblk = len(grads)
    rows, block, _ = grads[0].shape
    total = first_in.shape[0]
    tile = block * nblk // 2
    vec = whole((1, D))

    def row(*shape):
        return pl.BlockSpec((1,) + shape, lambda i: (i // 2,) + (0,) * len(shape))

    def out(cols, dtype=BF):
        return flat(tile, cols), (total, cols), dtype

    half = FF // 2
    return call(
        functools.partial(feed_kernel, nblk=nblk, place=place),
        "feed",
        (total // tile,),
        [SMEM, flat(tile, D), row(NSEG, D)] + [row(block, D)] * nblk
        + [whole((D, FF)), whole((1, FF)), whole((FF, D)), vec, whole((D, D)), vec, vec, vec, vec],
        [(row(block + 2 * NSEG, D), (rows, block + 2 * NSEG, D), BF)] * nblk
        + [out(half), out(half + D), out(half), out(half + D + D // 2), out(D), out(D, F32), out(D), out(D // 2),
           (whole((8, D)), (8, D), F32), (whole((8, FF)), (8, FF), F32)],
        scratch=[pltpu.VMEM((2, tile, half), BF), pltpu.VMEM((tile, D), BF), pltpu.VMEM((NSEG, D), F32)],
        flops=40e9,
    )(lengths, first_in, pool_grad, *grads, w_up, up_bias, w_down, down_bias, w_out, g1, b1, g2, b2)


def down_kernel(
    active_ref, outer_ref, came_active_ref, came_outer_ref, send_ref, keep_ref, slots_ref, sems, place, orders
):
    step = pl.program_id(0)
    core, here_block, _ = place()
    rows = slots_ref.shape[1]
    here = active_ref.shape[1] // rows
    tile = (tn(active_ref[...], outer_ref[...]) + tn(came_active_ref[...], came_outer_ref[...])).astype(BF)
    for i in range(here):
        slots_ref[slot_of(orders, core, step * here + i, here_block)] = tile[i * rows : (i + 1) * rows]

    @pl.when(step == pl.num_programs(0) - 1)
    def _():
        hand_out(slots_ref, send_ref, keep_ref, sems)


def down_gradient(active, mine, came, orders, place=own_place):
    total, half = active.shape
    outs, scratch = slots(half // BLOCKS, D)
    wide = 384
    part = pl.BlockSpec((total, wide), lambda j: (0, j))
    outer = pl.BlockSpec((total, D), lambda j: (0, half // D), pipeline_mode=pl.Buffered(1))
    return call(
        functools.partial(down_kernel, place=place, orders=orders),
        "down_gradient",
        (half // wide,),
        [part, outer, part, outer],
        outs,
        scratch=scratch,
        flops=6e9,
    )(active, mine, came, came)


def up_kernel(low_ref, inner_ref, came_low_ref, came_inner_ref, send_ref, keep_ref, slots_ref, sems, place, orders):
    step = pl.program_id(0)
    core, here_block, _ = place()
    rows = slots_ref.shape[1]
    wide = inner_ref.shape[1]
    tile = (tn(low_ref[...], inner_ref[...]) + tn(came_low_ref[...], came_inner_ref[...])).astype(BF)
    cols = pl.ds(pl.multiple_of(step * wide, 128), wide)
    for i in range(BLOCKS):
        slots_ref[slot_of(orders, core, i, here_block), :, cols] = tile[i * rows : (i + 1) * rows]

    @pl.when(step == pl.num_programs(0) - 1)
    def _():
        hand_out(slots_ref, send_ref, keep_ref, sems)


def up_gradient(low, inner, came, orders, place=own_place):
    total, half = inner.shape
    outs, scratch = slots(D // BLOCKS, half)
    wide = 512
    part = pl.BlockSpec((total, wide), lambda j: (0, j))
    came_low = pl.BlockSpec((total, D), lambda j: (0, half // D), pipeline_mode=pl.Buffered(1))
    return call(
        functools.partial(up_kernel, place=place, orders=orders),
        "up_gradient",
        (half // wide,),
        [whole((total, D)), part, came_low, part],
        outs,
        scratch=scratch,
        flops=6e9,
    )(low, inner, came, came)


def attention_back_kernel(lengths_ref, *refs, nblk, place):
    q_ref, k_ref, v_ref, gm_ref, grads_ref, other_ref, vec_ref = refs
    r = pl.program_id(0)
    core, _, blk = place()
    length = q_ref.shape[1]
    wide = 3 * PAIR
    hit = segments(lengths_ref, r, length, length, nblk, blk)
    here = jnp.where(hit, 1.0, 0.0).astype(BF)
    away = jnp.where(hit, 0.0, -BIG).astype(BF)
    masks = head_masks(length)
    scale = DH**-0.5
    for j in range(2):
        lanes = slice(j * PAIR, (j + 1) * PAIR)
        q = q_ref[0, :, lanes] * jnp.asarray(scale, BF)
        k = k_ref[0, :, lanes]
        v = v_ref[0, :, lanes]
        gm = gm_ref[:, lanes]
        k_aug = jnp.concatenate([k, away], axis=1)
        zero = jnp.zeros_like(q)
        probs, slopes, queries, keys, mixes = [], [], [], [], []
        for h in range(2):
            qh = jnp.where(masks[h], q, zero)
            kh = jnp.where(masks[h], k, zero)
            gmh = jnp.where(masks[h], gm, zero)
            s = nt(k_aug, jnp.concatenate([qh, here], axis=1))
            e = jnp.exp(s - jnp.max(s, axis=0, keepdims=True))
            p = e * (1.0 / jnp.sum(e, axis=0, keepdims=True))
            gp = nt(v, gmh)
            delta = jnp.sum(gp * p, axis=0, keepdims=True)
            slopes.append((p * (gp - delta)).astype(BF))
            probs.append(p.astype(BF))
            queries.append(qh)
            keys.append(kh)
            mixes.append(gmh)
        both = jnp.concatenate(slopes, axis=1)
        gv = nn(jnp.concatenate(probs, axis=1), jnp.concatenate(mixes, axis=0))
        gk = nn(both, jnp.concatenate(queries, axis=0))
        gq = nn(jnp.concatenate([x.T for x in keys], axis=1), jnp.concatenate(slopes, axis=0)).T
        grads = jnp.concatenate([(gq * scale).astype(BF), gk.astype(BF), gv.astype(BF)], axis=1)
        at = pl.ds(j * wide, wide)
        grads_ref[:, at] = grads
        sums = jnp.concatenate([col_sum(grads.astype(F32)), jnp.zeros((7, wide), F32)], axis=0)

        @pl.when(r == 0)
        def _():
            vec_ref[:, at] = sums

        @pl.when(r != 0)
        def _():
            vec_ref[:, at] += sums

    other_ref[...] = grads_ref[:, pl.ds(pl.multiple_of((core ^ 1) * wide, 128), wide)]


def attention_back(lengths, packed, grad_mixed, nblk, group, place=own_place):
    rows, length, _ = packed.shape
    total = rows * length

    def pairs(section):
        return pl.BlockSpec((1, length, 2 * PAIR), lambda r: (r, 0, section * (H // 4) + group))

    return call(
        functools.partial(attention_back_kernel, nblk=nblk, place=place),
        "attention_back",
        (rows,),
        [SMEM, pairs(0), pairs(1), pairs(2), pl.BlockSpec((length, 2 * PAIR), lambda r: (r, group))],
        [(flat(length, D), (total, D), BF), (flat(length, D // 2), (total, D // 2), BF), (whole((8, D)), (8, D), F32)],
        flops=12e9,
    )(lengths, packed, packed, packed, grad_mixed)


def head_gradient_kernel(
    both_ref, came_both_ref, branch_ref, came_rest_ref, *refs, groups, place, orders
):
    rights, came_rights = refs[:groups], refs[groups : 2 * groups]
    send_ref, keep_ref, held, right_held, slots_ref, sems, left_sems, right_sems = refs[2 * groups :]
    core, here_block, _ = place()
    wide = D // 2
    own = pl.ds(pl.multiple_of(core * wide, 128), wide)
    tokens, mixed, tail = pl.ds(0, D), pl.ds(D, D), pl.ds(came_rest_ref.shape[1] - wide, wide)
    pairs = [(branch_ref, came_rest_ref.at[:, tail])] + [(a.at[:, own], b) for a, b in zip(rights, came_rights)]
    left_loads = [
        pltpu.make_async_copy(ref.at[:, lanes], held.at[n], left_sems.at[n])
        for n, (ref, lanes) in enumerate(
            ((both_ref, mixed), (came_both_ref, mixed), (both_ref, tokens), (came_both_ref, tokens))
        )
    ]
    right_loads = [
        pltpu.make_async_copy(ref, right_held.at[n, side], right_sems.at[2 * n + side])
        for n, pair in enumerate(pairs)
        for side, ref in enumerate(pair)
    ]
    for load in left_loads[:2] + right_loads[:2] + left_loads[2:] + right_loads[2:]:
        load.start()
    rows = D // BLOCKS
    for n in range(groups + 1):
        for load in (left_loads[2 * n : 2 * n + 2] if n < 2 else []) + right_loads[2 * n : 2 * n + 2]:
            load.wait()
        at = 0 if n == 0 else 2
        tile = (tn(held[at], right_held[n, 0]) + tn(held[at + 1], right_held[n, 1])).astype(BF)
        for i in range(BLOCKS):
            slot = slot_of(orders, core, i, here_block)
            slots_ref[slot, :, n * wide : (n + 1) * wide] = tile[i * rows : (i + 1) * rows]
    hand_out(slots_ref, send_ref, keep_ref, sems)


def head_gradient(both, came_both, branch, came_rest, grads, came_grads, orders, place=own_place):
    total = both.shape[0]
    groups = len(grads)
    wide = D // 2
    outs, scratch = slots(D // BLOCKS, (groups + 1) * wide)
    return call(
        functools.partial(head_gradient_kernel, groups=groups, place=place, orders=orders),
        "head_gradient",
        (1,),
        [ANY] * (4 + 2 * groups),
        outs,
        scratch=[pltpu.VMEM((4, total, D), BF), pltpu.VMEM((groups + 1, 2, total, wide), BF)] + scratch
        + [pltpu.SemaphoreType.DMA((4,)), pltpu.SemaphoreType.DMA((2 * groups + 2,))],
        flops=6e9,
    )(both, came_both, branch, came_rest, *grads, *came_grads)


def tokens_grad_kernel(*refs, groups, nblk):
    grads = refs[:groups]
    grad_first_in_ref, w_in_ref = refs[groups : groups + 2]
    outs = refs[groups + 2 : groups + 2 + nblk]
    part = pl.program_id(0) % 2
    block = outs[0].shape[1]
    some = nblk // 2
    total = grad_first_in_ref[...]
    for g in range(groups):
        starts = [section * D + (2 * g + j) * PAIR for j in range(2) for section in range(3)]
        weight = jnp.concatenate([w_in_ref[:, at : at + PAIR] for at in starts], axis=1)
        total = total + nt(grads[g][...], weight)
    total = total.astype(BF)
    for half in range(2):

        @pl.when(part == half)
        def _():
            for i in range(some):
                outs[half * some + i][0] = total[i * block : (i + 1) * block]


def tokens_gradient(grads, grad_first_in, w_in, nblk, rows):
    total = grad_first_in.shape[0]
    block = total // rows // nblk
    tile = total // rows // 2
    return call(
        functools.partial(tokens_grad_kernel, groups=len(grads), nblk=nblk),
        "tokens_gradient",
        (2 * rows,),
        [flat(tile, D)] * len(grads) + [flat(tile, D), whole((D, 3 * D))],
        [(pl.BlockSpec((1, block, D), lambda i: (i // 2, 0, 0)), (rows, block, D), BF)] * nblk,
        flops=5e9,
    )(*grads, grad_first_in, w_in)


def place_hidden_kernel(*refs, nblk, rows, block, place):
    pieces, (hidden_ref, pooled_ref) = refs[:nblk], refs[nblk:]
    blk = place()[2]
    for i in range(nblk):
        for r in range(rows):
            at = (blk ^ i) * rows + r
            hidden_ref[pl.ds(at, 1)] = pieces[i][pl.ds(r, 1), :block, :]
            tail = pieces[i][r, block:, :].astype(F32)
            pooled_ref[pl.ds(at, 1)] = (tail[:NSEG] + tail[NSEG:]).reshape(1, NSEG, D)


def place_hidden(pieces, place=own_place):
    nblk = len(pieces)
    rows, block, _ = pieces[0].shape
    block -= 2 * NSEG
    return call(
        functools.partial(place_hidden_kernel, nblk=nblk, rows=rows, block=block, place=place),
        "place_hidden",
        (1,),
        [whole((rows, block + 2 * NSEG, D))] * nblk,
        [(whole((rows * nblk, block, D)), (rows * nblk, block, D), BF), (whole((rows * nblk, NSEG, D)), (rows * nblk, NSEG, D), F32)],
        flops=1e9,
    )(*pieces)


def place_tokens_kernel(*refs, nblk, rows, place):
    pieces, out_ref = refs[:nblk], refs[nblk]
    blk = place()[2]
    for i in range(nblk):
        for r in range(rows):
            out_ref[pl.ds((blk ^ i) * rows + r, 1)] = pieces[i][pl.ds(r, 1)].astype(F32)


def place_tokens(pieces, place=own_place):
    nblk = len(pieces)
    rows, block, _ = pieces[0].shape
    return call(
        functools.partial(place_tokens_kernel, nblk=nblk, rows=rows, place=place),
        "place_tokens",
        (1,),
        [whole((rows, block, D))] * nblk,
        [(whole((rows * nblk, block, D)), (rows * nblk, block, D), F32)],
        flops=1e9,
    )(*pieces)[0]


def unpack_kernel(half_ref, *refs, flip, place, orders):
    out_ref = refs[-1]
    core, here_block, _ = place()
    rows = half_ref.shape[1]
    count = out_ref.shape[0] // rows
    for i in range(count):
        slot = slot_of(orders, core ^ flip, pl.program_id(0) * count + i, here_block)
        out_ref[i * rows : (i + 1) * rows, :] = half_ref[slot].astype(F32)


def unpack_feed(half, by_rows, flip, before, orders, place=own_place):
    _, rows, cols = half.shape
    parts = 4
    core = lambda: place()[0] ^ flip
    tall = rows * BLOCKS
    shape, index = (
        ((2 * tall, cols), lambda q: (core() * parts + q, 0)) if by_rows else ((tall, 2 * cols), lambda q: (q, core()))
    )
    extra = [] if before is None else [before]
    return call(
        functools.partial(unpack_kernel, flip=flip, place=place, orders=orders),
        "unpack_feed",
        (parts,),
        [whole(half.shape)] + [ANY] * len(extra),
        [(pl.BlockSpec((tall // parts, cols), index), shape, F32)],
        aliases={1: 0} if extra else None,
        flops=2e9,
    )(half, *extra)[0]


def unpack_heads_kernel(half_ref, *refs, flip, place, orders):
    output_ref, input_ref, full_ref, sems = refs[-4:]
    core, here_block, _ = place()
    rows = D // BLOCKS
    wide = 3 * PAIR
    to = core ^ flip
    copies = []
    for n in range(full_ref.shape[0]):
        for i in range(BLOCKS):
            slot = slot_of(orders, to, i, here_block)
            full_ref[n, i * rows : (i + 1) * rows, :] = half_ref[slot, :, n * wide : (n + 1) * wide].astype(F32)
        if n == 0:
            lanes = pl.ds(pl.multiple_of(to * wide, 128), wide)
            copies.append(pltpu.make_async_copy(full_ref.at[0], output_ref.at[:, lanes], sems.at[0]))
            copies[-1].start()
            continue
        for section in range(3):
            lanes = pl.ds(pl.multiple_of(section * D + (2 * (n - 1) + to) * PAIR, 128), PAIR)
            part = full_ref.at[n, :, pl.ds(section * PAIR, PAIR)]
            copies.append(pltpu.make_async_copy(part, input_ref.at[:, lanes], sems.at[3 * n + section - 2]))
            copies[-1].start()
    for copy in copies:
        copy.wait()


def unpack_heads(half, flip, before, orders, place=own_place):
    extra = [] if before is None else list(before)
    count = half.shape[2] // (3 * PAIR)
    return call(
        functools.partial(unpack_heads_kernel, flip=flip, place=place, orders=orders),
        "unpack_heads",
        (1,),
        [whole(half.shape)] + [ANY] * len(extra),
        [(ANY, (D, D), F32), (ANY, (D, 3 * D), F32)],
        scratch=[pltpu.VMEM((count, D, 3 * PAIR), F32), pltpu.SemaphoreType.DMA((3 * count - 2,))],
        aliases={1: 0, 2: 1} if extra else None,
        flops=2e9,
    )(half, *extra)


def exchange(array, bits):
    nblk, nrows = lax.axis_size("blk"), lax.axis_size("rows")
    moves = {"c": (0, 1), "y": (0, 2), "x": (1, 0), "a": (2, 0), "b": (4, 0)}
    pairs = []
    for i in range(nblk * nrows):
        row, blk = divmod(i, nblk)
        bit = bits[blk & 1]
        by_row, by_blk = moves[bit] if isinstance(bit, str) else (bit, 0)
        pairs.append((i, (row ^ by_row) * nblk + (blk ^ by_blk)))
    return lax.ppermute(array, ("rows", "blk"), pairs)


def added(left, right):
    return (left.astype(F32) + right.astype(F32)).astype(BF)


class Sum:
    def __init__(self, send, keep, orders):
        self.keep = keep
        extra = []
        bit = 8
        while bit < lax.axis_size("rows"):
            extra.append(bit)
            bit *= 2
        bits = [(orders[0][t], orders[1][t]) for t in range(4)]
        halves, wholes = bits[: orders[2]], bits[orders[2] :]
        self.plan = [("half", h) for h in halves] + [("all", w) for w in wholes] + [("all", (e, e)) for e in extra]
        self.plan += [("join", h) for h in reversed(halves)] + [("end", ("c", "c"))]
        self.moving = exchange(send, self.plan[0][1])
        self.stage = 0

    def busy(self):
        return self.stage < len(self.plan)

    def step(self, marks=()):
        if not self.busy():
            return []
        kind = self.plan[self.stage][0]
        (came,) = after([self.moving], marks)
        self.stage += 1
        if kind == "end":
            self.other = came
            return [self.other]
        if kind == "half":
            if self.plan[self.stage][0] == "half":
                n = self.keep.shape[0] // 2
                send, self.keep = added(self.keep[n:], came[n:]), added(self.keep[:n], came[:n])
            else:
                send = self.now = added(self.keep, came)
        elif kind == "all":
            send = self.now = added(self.now, came)
        else:
            send = self.now = jnp.concatenate([self.now, came], axis=0)
        self.moving = exchange(send, self.plan[self.stage][1])
        return [send]

    def last(self):
        return self.stage == len(self.plan) - 1


class Vectors:
    def __init__(self, value):
        self.value = value
        bit = 8
        self.left = ["c", "y", "x", "a", "b"]
        while bit < lax.axis_size("rows"):
            self.left.append(bit)
            bit *= 2
        self.moving = None

    def step(self, marks=()):
        if self.moving is not None:
            (came,) = after([self.moving], marks)
            self.value = self.value + came
            self.moving = None
        elif marks:
            (self.value,) = after([self.value], marks)
        if self.left:
            bit = self.left.pop(0)
            self.moving = exchange(self.value, (bit, bit))
        return [self.value]

    def finish(self):
        while self.left or self.moving is not None:
            self.step()
        return self.value


def after(arrays, *marks):
    marks = [m for mark in marks for m in mark]
    return list(lax.optimization_barrier(tuple(arrays) + tuple(marks))[: len(arrays)])


def pieces_of(array, me, nblk, first=0, count=None):
    rows = array.shape[0] // nblk
    return [lax.dynamic_slice_in_dim(array, (me ^ k) * rows + first, count or rows, axis=0) for k in range(nblk)]


def swap(pieces):
    nblk = len(pieces)
    return [pieces[0]] + [
        lax.ppermute(pieces[k], "blk", [(i, i ^ k) for i in range(nblk)]) for k in range(1, nblk)
    ]


def on_device(
    tokens,
    lengths,
    input_weight,
    query_bias,
    value_bias,
    output_weight,
    output_bias,
    first_gain,
    first_shift,
    up_weight,
    up_bias,
    down_weight,
    down_bias,
    second_gain,
    second_shift,
    out_grad,
    pool_grad,
):
    nblk = lax.axis_size("blk")
    me = lax.axis_index("blk")
    rows = tokens.shape[0] // nblk
    row = lambda v: v.reshape(1, -1)
    g1, b1 = row(first_gain), row(first_shift)
    bias = row(jnp.concatenate([query_bias, jnp.zeros_like(query_bias), value_bias]))
    own_lengths = lax.dynamic_slice_in_dim(lengths, me * rows, rows, axis=0)
    own_pool = lax.dynamic_slice_in_dim(pool_grad, me * rows, rows, axis=0)
    pieces = []
    for r in range(rows):
        pieces.append(swap(after(pieces_of(tokens, me, nblk, r, 1), pieces[-1] if pieces else [])))
    grads = swap(after(pieces_of(out_grad, me, nblk), pieces[0]))
    twin = lambda a: exchange(a, ("c", "c"))
    made = ()
    for r in range(rows):
        made = attention_forward(
            own_lengths, pieces[r], input_weight, bias, output_weight, row(output_bias), rows, r, made
        )
    both, packed, first_in = made
    *hidden, active, active_outer, inner, inner_rest, low, grad_first_in, grad_mixed, branch, vec1, ups = feed(
        own_lengths, first_in, own_pool, grads, up_weight, row(up_bias), down_weight, row(down_bias), output_weight,
        g1, b1, row(second_gain), row(second_shift),
    )
    came_active, came_rest = twin(active_outer), twin(inner_rest)
    hidden = swap(hidden)

    def attention(group, marks):
        grad_packed, other, sums = attention_back(own_lengths, packed, after([grad_mixed], marks)[0], nblk, group)
        return grad_packed, other, sums[0].reshape(2, 3, PAIR)

    gp0, other0, vec_a = attention(0, [])
    active, came_active = after([active, came_active], [gp0])
    send, keep = down_gradient(active, active_outer, came_active, DOWN_ORDER)
    down = Sum(send, keep, DOWN_ORDER)
    (inner,) = after([inner], [keep] + hidden)
    send, keep = up_gradient(low, inner, came_rest, UP_ORDER)
    up = Sum(send, keep, UP_ORDER)
    came_both, came0 = [twin(a) for a in after([both, other0], [keep])]
    gp1, other1, vec_b = attention(1, [keep] + hidden)
    m = down.step([gp1])
    came1 = twin(other1)
    gp2, other2, vec_c = attention(2, m)
    came2 = twin(other2)
    m = up.step(down.step([gp2]))
    (both,) = after([both], m)
    send, keep = head_gradient(
        both, came_both, branch, came_rest, [gp0, gp1, gp2], [came0, came1, came2], HEAD_ORDER
    )
    heads = Sum(send, keep, HEAD_ORDER)
    m = up.step(down.step([keep]))
    sections = jnp.concatenate([vec_a, vec_b, vec_c], axis=0)
    vecs = Vectors(
        jnp.concatenate(
            [sections[:, 0].reshape(1, D), sections[:, 2].reshape(1, D), vec1[:6], ups[0].reshape(-1, D)], axis=0
        )
    )
    gp0, gp1, gp2, vecs.value = after([gp0, gp1, gp2, vecs.value], m)
    tokens_pieces = tokens_gradient([gp0, gp1, gp2], grad_first_in, input_weight, nblk, rows)
    m = tokens_pieces[:1]
    sums = {"d": down, "u": up, "r": heads, "v": vecs}
    held = {"down": None, "up": None, "heads": None}
    for action in TAIL:
        if action in sums:
            m = sums[action].step(m)
        elif action == "h":
            hidden_out, pooled = place_hidden(after(hidden, m))
            m = [hidden_out]
        elif action == "s":
            tokens_grad = after(tokens_pieces, m)
            halfway = twin(jnp.concatenate([tokens_grad[1], tokens_grad[3]], axis=0))
        elif action == "w":
            (halfway,) = after([halfway], m)
            far = jnp.concatenate([tokens_grad[2], halfway[rows:]], axis=0)
            m = [far]
            far = lax.ppermute(far, "blk", [(i, i ^ 2) for i in range(nblk)])
            tokens_grad = [tokens_grad[0], halfway[:rows], far[:rows], far[rows:]]
        elif action == "t":
            tokens_out = place_tokens(after(tokens_grad, m))
            m = [tokens_out]
        else:
            which, flip = divmod(int(action) - 1, 2)
            total = (down, up, heads)[which]
            while not total.last() and total.busy() or (flip and total.busy()):
                m = total.step(m)
            (half,) = after([total.other if flip else total.now], m)
            if which == 0:
                held["down"] = unpack_feed(half, True, flip, held["down"], DOWN_ORDER)
                m = [held["down"]]
            elif which == 1:
                held["up"] = unpack_feed(half, False, flip, held["up"], UP_ORDER)
                m = [held["up"]]
            else:
                held["heads"] = unpack_heads(half, flip, held["heads"], HEAD_ORDER)
                m = held["heads"]
    down_grad, up_grad, (output_grad, input_grad) = held["down"], held["up"], held["heads"]
    vecs = vecs.finish()
    return (
        hidden_out,
        pooled,
        tokens_out,
        input_grad,
        vecs[0],
        vecs[1],
        output_grad,
        vecs[4],
        vecs[2],
        vecs[3],
        up_grad,
        vecs[8:12].reshape(-1),
        down_grad,
        vecs[7],
        vecs[5],
        vecs[6],
    )


def solution(mesh):
    whole_rows = P("rows", "blk", None)
    rest = (P(),) * 13
    return jax.shard_map(
        on_device,
        mesh=mesh,
        in_specs=(whole_rows, P("rows", None)) + rest + (whole_rows, P("rows", None, None)),
        out_specs=(whole_rows, P("rows", None, None), whole_rows) + rest,
        check_vma=False,
    )
```

```python
import functools
import jax
import jax.numpy as jnp
from jax import lax
from jax.experimental import pallas as pl
from jax.experimental.pallas import tpu as pltpu
from jax.sharding import PartitionSpec as P

D = 768
H = 12
DH = 64
FF = 3072
NSEG = 8
PAIR = 2 * DH
NORM_EPS = 1e-12
BIG = 1e9
BF = jnp.bfloat16
F32 = jnp.float32
CHUNK = 768
VMEM_LIMIT = 60 * 1024 * 1024


def nn(a, b):
    return lax.dot_general(a, b, (((1,), (0,)), ((), ())), preferred_element_type=F32)


def nt(a, b):
    return lax.dot_general(a, b, (((1,), (1,)), ((), ())), preferred_element_type=F32)


def tn(a, b):
    return lax.dot_general(a, b, (((0,), (0,)), ((), ())), preferred_element_type=F32)


def col_sum(a):
    return jnp.sum(a, axis=0, keepdims=True)


def norm_parts(hidden):
    center = hidden - jnp.mean(hidden, axis=-1, keepdims=True)
    spread = jnp.mean(center * center, axis=-1, keepdims=True)
    inverse = lax.rsqrt(spread + NORM_EPS)
    return center * inverse, inverse


def norm_back(grad, gain, unit, inverse):
    scaled = grad * gain
    along = jnp.mean(scaled * unit, axis=-1, keepdims=True)
    return inverse * (scaled - jnp.mean(scaled, axis=-1, keepdims=True) - unit * along)


def segments(lengths_ref, row, length, count, nblk, me, first=0):
    shape = (count, PAIR)
    local = lax.broadcasted_iota(jnp.int32, shape, 0) + first
    block = length // nblk
    places = ((local // block) ^ me) * block + local % block
    end = jnp.int32(0)
    labels = jnp.zeros(shape, jnp.int32)
    for c in range(NSEG):
        end = end + lengths_ref[row, c]
        labels = labels + (places >= end).astype(jnp.int32)
    return labels == lax.broadcasted_iota(jnp.int32, shape, 1)


def head_masks(length):
    lane = lax.broadcasted_iota(jnp.int32, (length, PAIR), 1)
    return lane < DH, lane >= DH


PLACE = {"y": 0, "x": 1, "a": 2, "b": 3}
BLOCKS = 16
DOWN_ORDER = ("xyab", "yxab", 3)
UP_ORDER = ("xyab", "yxab", 3)
HEAD_ORDER = ("xyab", "yxab", 3)
TAIL = "duhrsdurwvudvrutvrvdrv1durv2u34vr5r6"


def own_place():
    blk = lax.axis_index("blk")
    rows = lax.axis_index("rows")
    return blk & 1, ((rows & 7) << 1) | ((blk >> 1) & 1), blk


def slot_in(order, halved, block, here):
    slot = 0
    for t, bit in enumerate(order):
        at = block ^ here if t < halved else block
        slot = slot | (((at >> PLACE[bit]) & 1) << (3 - t))
    return slot


def slot_of(orders, core, block, here):
    return jnp.where(
        core == 0, slot_in(orders[0], orders[2], block, here), slot_in(orders[1], orders[2], block, here)
    )


def hand_out(slots_ref, send_ref, keep_ref, sems):
    half = BLOCKS // 2
    copies = [
        pltpu.make_async_copy(slots_ref.at[pl.ds(half, half)], send_ref, sems.at[0]),
        pltpu.make_async_copy(slots_ref.at[pl.ds(0, half)], keep_ref, sems.at[1]),
    ]
    for c in copies:
        c.start()
    for c in copies:
        c.wait()


def whole(shape):
    return pl.BlockSpec(shape, lambda *_: (0,) * len(shape), pipeline_mode=pl.Buffered(1))


def per_row(*shape):
    return pl.BlockSpec((1,) + shape, lambda r: (r,) + (0,) * len(shape))


def flat(*shape):
    return pl.BlockSpec(shape, lambda r: (r,) + (0,) * (len(shape) - 1))


SMEM = pl.BlockSpec(memory_space=pltpu.SMEM)
ANY = pl.BlockSpec(memory_space=pl.ANY)


def slots(rows, cols):
    half = (ANY, (BLOCKS // 2, rows, cols), BF)
    return [half, half], [pltpu.VMEM((BLOCKS, rows, cols), BF), pltpu.SemaphoreType.DMA((2,))]


def shape_of(shape, dtype):
    return jax.ShapeDtypeStruct(shape, dtype)


def call(kernel, name, grid, in_specs, outs, scratch=(), flops=0, nbytes=0, aliases=None):
    return pl.pallas_call(
        kernel,
        grid=grid,
        in_specs=in_specs,
        out_specs=[o[0] for o in outs],
        out_shape=[shape_of(o[1], o[2]) for o in outs],
        scratch_shapes=scratch,
        input_output_aliases=aliases or {},
        compiler_params=pltpu.CompilerParams(vmem_limit_bytes=VMEM_LIMIT),
        cost_estimate=pl.CostEstimate(flops=int(flops), bytes_accessed=int(nbytes), transcendentals=0),
        name=name,
    )


def attention_kernel(lengths_ref, *refs, nblk, place, row):
    pieces = refs[:nblk]
    w_in_ref, bias_ref, w_out_ref, out_bias_ref = refs[nblk : nblk + 4]
    both_ref, packed_ref, first_in_ref = refs[-3:]
    block = pieces[0].shape[1]
    length = block * nblk
    for i in range(nblk):
        both_ref[pl.ds(i * block, block), :D] = pieces[i][0]
    x = both_ref[:, :D]
    for c in range(3):
        cols = pl.ds(c * D, D)
        packed_ref[0, :, cols] = (nn(x, w_in_ref[:, cols]) + bias_ref[:, cols]).astype(BF)
    hit = segments(lengths_ref, row, length, length, nblk, place()[2])
    here = jnp.where(hit, 1.0, 0.0).astype(BF)
    away = jnp.where(hit, 0.0, -BIG).astype(BF)
    masks = head_masks(length)
    for j in range(H // 2):
        q = packed_ref[0, :, pl.ds(j * PAIR, PAIR)] * jnp.asarray(DH**-0.5, BF)
        k = packed_ref[0, :, pl.ds(D + j * PAIR, PAIR)]
        v = packed_ref[0, :, pl.ds(2 * D + j * PAIR, PAIR)]
        k_aug = jnp.concatenate([k, away], axis=1)
        zero = jnp.zeros_like(q)
        weights, totals = [], []
        for h in range(2):
            s = nt(jnp.concatenate([jnp.where(masks[h], q, zero), here], axis=1), k_aug)
            e = jnp.exp(s - jnp.max(s, axis=1, keepdims=True))
            totals.append(jnp.sum(e, axis=1, keepdims=True))
            weights.append(e.astype(BF))
        values = jnp.concatenate([jnp.where(m, v, zero) for m in masks], axis=0)
        out = nn(jnp.concatenate(weights, axis=1), values) / jnp.where(masks[0], totals[0], totals[1])
        both_ref[:, pl.ds(D + j * PAIR, PAIR)] = out.astype(BF)
    branch = nn(both_ref[:, D:], w_out_ref[...]) + out_bias_ref[...]
    first_in_ref[...] = x.astype(F32) + branch


def attention_forward(lengths, pieces, w_in, bias, w_out, out_bias, rows, row, before, place=own_place):
    nblk = len(pieces)
    block = pieces[0].shape[1]
    length = block * nblk
    extra = list(before)
    return call(
        functools.partial(attention_kernel, nblk=nblk, place=place, row=row),
        "attention_forward",
        (1,),
        [SMEM] + [per_row(block, D)] * nblk + [whole((D, 3 * D)), whole((1, 3 * D)), whole((D, D)), whole((1, D))]
        + [ANY] * len(extra),
        [
            (pl.BlockSpec((length, 2 * D), lambda r: (row, 0)), (rows * length, 2 * D), BF),
            (pl.BlockSpec((1, length, 3 * D), lambda r: (row, 0, 0)), (rows, length, 3 * D), BF),
            (pl.BlockSpec((length, D), lambda r: (row, 0)), (rows * length, D), F32),
        ],
        aliases={nblk + 5 + n: n for n in range(len(extra))},
        flops=9e9,
    )(lengths, *pieces, w_in, bias, w_out, out_bias, *extra)


def gelu_both(x):
    cdf = 0.5 + 0.5 * lax.erf(x * (0.5**0.5))
    density = jnp.exp(x * x * -0.5) * 0.3989422804014327
    return x * cdf, cdf + x * density


def feed_kernel(lengths_ref, first_in_ref, pool_grad_ref, *refs, nblk, place):
    grad_pieces = refs[:nblk]
    (w_up_ref, up_bias_ref, w_down_ref, down_bias_ref, w_out_ref, g1_ref, b1_ref, g2_ref, b2_ref) = refs[nblk : nblk + 9]
    hidden = refs[nblk + 9 : 2 * nblk + 9]
    (active_own_ref, active_other_ref, inner_own_ref, other_ref, low_own_ref, grad_first_in_ref, grad_mixed_ref,
     branch_own_ref, vec_ref, up_sums_ref, slope_ref, branch_ref, pooled_ref) = refs[2 * nblk + 9 :]
    step = pl.program_id(0)
    r, part = step // 2, step % 2
    count = first_in_ref.shape[0]
    block = hidden[0].shape[1] - 2 * NSEG
    length = block * nblk
    some = nblk // 2
    half = FF // 2
    core, _, blk = place()
    chunks = [(flip, c) for flip in (1, 0) for c in range(half // CHUNK)]

    def units(flip, c):
        return pl.ds(pl.multiple_of((core ^ flip) * half + c * CHUNK, 128), CHUNK)


    unit1, inverse1 = norm_parts(first_in_ref[...])
    first = unit1 * g1_ref[...] + b1_ref[...]
    low = first.astype(BF)
    low_own_ref[...] = low
    other_ref[:, half : half + D] = low
    acc = first + down_bias_ref[...]
    for flip, c in chunks:
        cols, at = units(flip, c), pl.ds(c * CHUNK, CHUNK)
        inner = nn(low, w_up_ref[:, cols]) + up_bias_ref[:, cols]
        act, slope = gelu_both(inner)
        act = act.astype(BF)
        (active_other_ref if flip else active_own_ref)[:, at] = act
        slope_ref[flip, :, at] = slope.astype(BF)
        acc = acc + nn(act, w_down_ref[cols, :])
    unit, inverse = norm_parts(acc)
    result = unit * g2_ref[...] + b2_ref[...]
    high = result.astype(BF)
    here = jnp.where(segments(lengths_ref, r, length, count, nblk, blk, part * count), 1.0, 0.0).astype(BF)
    rest = (result - high.astype(F32)).astype(BF)
    sums = (tn(here, high) + tn(here, rest))[:NSEG]
    sub = lax.broadcasted_iota(jnp.int32, (NSEG, 1), 0)
    counts = jnp.zeros((NSEG, 1), F32)
    for c in range(NSEG):
        counts = jnp.where(sub == c, lengths_ref[r, c].astype(F32), counts)

    @pl.when(part == 0)
    def _():
        pooled_ref[...] = sums
        for i in range(some):
            hidden[i][0, :block, :] = high[i * block : (i + 1) * block]

    @pl.when(part == 1)
    def _():
        pooled = (pooled_ref[...] + sums) / counts
        pooled_high = pooled.astype(BF)
        both = jnp.concatenate([pooled_high.astype(F32), pooled - pooled_high.astype(F32)], axis=0).astype(BF)
        for i in range(some):
            hidden[some + i][0, :block, :] = high[i * block : (i + 1) * block]
        for i in range(nblk):
            hidden[i][0, block:, :] = both

    share = pool_grad_ref[0].astype(F32) / counts
    share_high = share.astype(BF)
    share_rest = (share - share_high.astype(F32)).astype(BF)
    pad = jnp.zeros((PAIR - NSEG, D), BF)
    spread = nn(here, jnp.concatenate([share_high, pad], axis=0)) + nn(here, jnp.concatenate([share_rest, pad], axis=0))
    given = jnp.where(
        part == 0,
        jnp.concatenate([g[0] for g in grad_pieces[:some]], axis=0).astype(F32),
        jnp.concatenate([g[0] for g in grad_pieces[some:]], axis=0).astype(F32),
    )
    grad = given + spread
    acc = norm_back(grad, g2_ref[...], unit, inverse)
    outer = acc.astype(BF)
    active_other_ref[:, half:] = outer
    sums2 = [col_sum(grad * unit), col_sum(grad), col_sum(outer.astype(F32))]
    @pl.when(step == 0)
    def _():
        up_sums_ref[...] = jnp.zeros_like(up_sums_ref)

    for flip, c in chunks:
        cols, at = units(flip, c), pl.ds(c * CHUNK, CHUNK)
        inner = (nt(outer, w_down_ref[cols, :]) * slope_ref[flip, :, at].astype(F32)).astype(BF)
        (other_ref if flip else inner_own_ref)[:, at] = inner
        up_sums_ref[:1, cols] += col_sum(inner.astype(F32))
        acc = acc + nt(inner, w_up_ref[:, cols])
    grad_first_in = norm_back(acc, g1_ref[...], unit1, inverse1)
    grad_first_in_ref[...] = grad_first_in
    branch = grad_first_in.astype(BF)
    branch_ref[...] = branch
    branch_own_ref[...] = branch_ref[:, pl.ds(pl.multiple_of(core * (D // 2), 128), D // 2)]
    other_ref[:, half + D :] = branch_ref[:, pl.ds(pl.multiple_of((core ^ 1) * (D // 2), 128), D // 2)]
    grad_mixed_ref[...] = nt(branch, w_out_ref[...]).astype(BF)
    sums1 = [col_sum(acc * unit1), col_sum(acc), col_sum(branch.astype(F32))]
    vec = jnp.concatenate(sums1 + sums2 + [jnp.zeros((2, D), F32)], axis=0)

    @pl.when(step == 0)
    def _():
        vec_ref[...] = vec

    @pl.when(step != 0)
    def _():
        vec_ref[...] += vec


def feed(lengths, first_in, pool_grad, grads, w_up, up_bias, w_down, down_bias, w_out, g1, b1, g2, b2, place=own_place):
    nblk = len(grads)
    rows, block, _ = grads[0].shape
    total = first_in.shape[0]
    tile = block * nblk // 2
    vec = whole((1, D))

    def row(*shape):
        return pl.BlockSpec((1,) + shape, lambda i: (i // 2,) + (0,) * len(shape))

    def out(cols, dtype=BF):
        return flat(tile, cols), (total, cols), dtype

    half = FF // 2
    return call(
        functools.partial(feed_kernel, nblk=nblk, place=place),
        "feed",
        (total // tile,),
        [SMEM, flat(tile, D), row(NSEG, D)] + [row(block, D)] * nblk
        + [whole((D, FF)), whole((1, FF)), whole((FF, D)), vec, whole((D, D)), vec, vec, vec, vec],
        [(row(block + 2 * NSEG, D), (rows, block + 2 * NSEG, D), BF)] * nblk
        + [out(half), out(half + D), out(half), out(half + D + D // 2), out(D), out(D, F32), out(D), out(D // 2),
           (whole((8, D)), (8, D), F32), (whole((8, FF)), (8, FF), F32)],
        scratch=[pltpu.VMEM((2, tile, half), BF), pltpu.VMEM((tile, D), BF), pltpu.VMEM((NSEG, D), F32)],
        flops=40e9,
    )(lengths, first_in, pool_grad, *grads, w_up, up_bias, w_down, down_bias, w_out, g1, b1, g2, b2)


def down_kernel(
    active_ref, outer_ref, came_active_ref, came_outer_ref, send_ref, keep_ref, slots_ref, sems, place, orders
):
    step = pl.program_id(0)
    core, here_block, _ = place()
    rows = slots_ref.shape[1]
    here = active_ref.shape[1] // rows
    tile = (tn(active_ref[...], outer_ref[...]) + tn(came_active_ref[...], came_outer_ref[...])).astype(BF)
    for i in range(here):
        slots_ref[slot_of(orders, core, step * here + i, here_block)] = tile[i * rows : (i + 1) * rows]

    @pl.when(step == pl.num_programs(0) - 1)
    def _():
        hand_out(slots_ref, send_ref, keep_ref, sems)


def down_gradient(active, mine, came, orders, place=own_place):
    total, half = active.shape
    outs, scratch = slots(half // BLOCKS, D)
    wide = 384
    part = pl.BlockSpec((total, wide), lambda j: (0, j))
    outer = pl.BlockSpec((total, D), lambda j: (0, half // D), pipeline_mode=pl.Buffered(1))
    return call(
        functools.partial(down_kernel, place=place, orders=orders),
        "down_gradient",
        (half // wide,),
        [part, outer, part, outer],
        outs,
        scratch=scratch,
        flops=6e9,
    )(active, mine, came, came)


def up_kernel(low_ref, inner_ref, came_low_ref, came_inner_ref, send_ref, keep_ref, slots_ref, sems, place, orders):
    step = pl.program_id(0)
    core, here_block, _ = place()
    rows = slots_ref.shape[1]
    wide = inner_ref.shape[1]
    tile = (tn(low_ref[...], inner_ref[...]) + tn(came_low_ref[...], came_inner_ref[...])).astype(BF)
    cols = pl.ds(pl.multiple_of(step * wide, 128), wide)
    for i in range(BLOCKS):
        slots_ref[slot_of(orders, core, i, here_block), :, cols] = tile[i * rows : (i + 1) * rows]

    @pl.when(step == pl.num_programs(0) - 1)
    def _():
        hand_out(slots_ref, send_ref, keep_ref, sems)


def up_gradient(low, inner, came, orders, place=own_place):
    total, half = inner.shape
    outs, scratch = slots(D // BLOCKS, half)
    wide = 512
    part = pl.BlockSpec((total, wide), lambda j: (0, j))
    came_low = pl.BlockSpec((total, D), lambda j: (0, half // D), pipeline_mode=pl.Buffered(1))
    return call(
        functools.partial(up_kernel, place=place, orders=orders),
        "up_gradient",
        (half // wide,),
        [whole((total, D)), part, came_low, part],
        outs,
        scratch=scratch,
        flops=6e9,
    )(low, inner, came, came)


def attention_back_kernel(lengths_ref, *refs, nblk, place):
    q_ref, k_ref, v_ref, gm_ref, grads_ref, other_ref, vec_ref = refs
    r = pl.program_id(0)
    core, _, blk = place()
    length = q_ref.shape[1]
    wide = 3 * PAIR
    hit = segments(lengths_ref, r, length, length, nblk, blk)
    here = jnp.where(hit, 1.0, 0.0).astype(BF)
    away = jnp.where(hit, 0.0, -BIG).astype(BF)
    masks = head_masks(length)
    scale = DH**-0.5
    for j in range(2):
        lanes = slice(j * PAIR, (j + 1) * PAIR)
        q = q_ref[0, :, lanes] * jnp.asarray(scale, BF)
        k = k_ref[0, :, lanes]
        v = v_ref[0, :, lanes]
        gm = gm_ref[:, lanes]
        k_aug = jnp.concatenate([k, away], axis=1)
        zero = jnp.zeros_like(q)
        probs, slopes, queries, keys, mixes = [], [], [], [], []
        for h in range(2):
            qh = jnp.where(masks[h], q, zero)
            kh = jnp.where(masks[h], k, zero)
            gmh = jnp.where(masks[h], gm, zero)
            s = nt(k_aug, jnp.concatenate([qh, here], axis=1))
            e = jnp.exp(s - jnp.max(s, axis=0, keepdims=True))
            p = e * (1.0 / jnp.sum(e, axis=0, keepdims=True))
            gp = nt(v, gmh)
            delta = jnp.sum(gp * p, axis=0, keepdims=True)
            slopes.append((p * (gp - delta)).astype(BF))
            probs.append(p.astype(BF))
            queries.append(qh)
            keys.append(kh)
            mixes.append(gmh)
        both = jnp.concatenate(slopes, axis=1)
        gv = nn(jnp.concatenate(probs, axis=1), jnp.concatenate(mixes, axis=0))
        gk = nn(both, jnp.concatenate(queries, axis=0))
        gq = nn(jnp.concatenate([x.T for x in keys], axis=1), jnp.concatenate(slopes, axis=0)).T
        grads = jnp.concatenate([(gq * scale).astype(BF), gk.astype(BF), gv.astype(BF)], axis=1)
        at = pl.ds(j * wide, wide)
        grads_ref[:, at] = grads
        sums = jnp.concatenate([col_sum(grads.astype(F32)), jnp.zeros((7, wide), F32)], axis=0)

        @pl.when(r == 0)
        def _():
            vec_ref[:, at] = sums

        @pl.when(r != 0)
        def _():
            vec_ref[:, at] += sums

    other_ref[...] = grads_ref[:, pl.ds(pl.multiple_of((core ^ 1) * wide, 128), wide)]


def attention_back(lengths, packed, grad_mixed, nblk, group, place=own_place):
    rows, length, _ = packed.shape
    total = rows * length

    def pairs(section):
        return pl.BlockSpec((1, length, 2 * PAIR), lambda r: (r, 0, section * (H // 4) + group))

    return call(
        functools.partial(attention_back_kernel, nblk=nblk, place=place),
        "attention_back",
        (rows,),
        [SMEM, pairs(0), pairs(1), pairs(2), pl.BlockSpec((length, 2 * PAIR), lambda r: (r, group))],
        [(flat(length, D), (total, D), BF), (flat(length, D // 2), (total, D // 2), BF), (whole((8, D)), (8, D), F32)],
        flops=12e9,
    )(lengths, packed, packed, packed, grad_mixed)


def head_gradient_kernel(
    both_ref, came_both_ref, branch_ref, came_rest_ref, *refs, groups, place, orders
):
    rights, came_rights = refs[:groups], refs[groups : 2 * groups]
    send_ref, keep_ref, held, right_held, slots_ref, sems, left_sems, right_sems = refs[2 * groups :]
    core, here_block, _ = place()
    wide = D // 2
    own = pl.ds(pl.multiple_of(core * wide, 128), wide)
    tokens, mixed, tail = pl.ds(0, D), pl.ds(D, D), pl.ds(came_rest_ref.shape[1] - wide, wide)
    pairs = [(branch_ref, came_rest_ref.at[:, tail])] + [(a.at[:, own], b) for a, b in zip(rights, came_rights)]
    left_loads = [
        pltpu.make_async_copy(ref.at[:, lanes], held.at[n], left_sems.at[n])
        for n, (ref, lanes) in enumerate(
            ((both_ref, mixed), (came_both_ref, mixed), (both_ref, tokens), (came_both_ref, tokens))
        )
    ]
    right_loads = [
        pltpu.make_async_copy(ref, right_held.at[n, side], right_sems.at[2 * n + side])
        for n, pair in enumerate(pairs)
        for side, ref in enumerate(pair)
    ]
    for load in left_loads[:2] + right_loads[:2] + left_loads[2:] + right_loads[2:]:
        load.start()
    rows = D // BLOCKS
    for n in range(groups + 1):
        for load in (left_loads[2 * n : 2 * n + 2] if n < 2 else []) + right_loads[2 * n : 2 * n + 2]:
            load.wait()
        at = 0 if n == 0 else 2
        tile = (tn(held[at], right_held[n, 0]) + tn(held[at + 1], right_held[n, 1])).astype(BF)
        for i in range(BLOCKS):
            slot = slot_of(orders, core, i, here_block)
            slots_ref[slot, :, n * wide : (n + 1) * wide] = tile[i * rows : (i + 1) * rows]
    hand_out(slots_ref, send_ref, keep_ref, sems)


def head_gradient(both, came_both, branch, came_rest, grads, came_grads, orders, place=own_place):
    total = both.shape[0]
    groups = len(grads)
    wide = D // 2
    outs, scratch = slots(D // BLOCKS, (groups + 1) * wide)
    return call(
        functools.partial(head_gradient_kernel, groups=groups, place=place, orders=orders),
        "head_gradient",
        (1,),
        [ANY] * (4 + 2 * groups),
        outs,
        scratch=[pltpu.VMEM((4, total, D), BF), pltpu.VMEM((groups + 1, 2, total, wide), BF)] + scratch
        + [pltpu.SemaphoreType.DMA((4,)), pltpu.SemaphoreType.DMA((2 * groups + 2,))],
        flops=6e9,
    )(both, came_both, branch, came_rest, *grads, *came_grads)


def tokens_grad_kernel(*refs, groups, nblk):
    grads = refs[:groups]
    grad_first_in_ref, w_in_ref = refs[groups : groups + 2]
    outs = refs[groups + 2 : groups + 2 + nblk]
    part = pl.program_id(0) % 2
    block = outs[0].shape[1]
    some = nblk // 2
    total = grad_first_in_ref[...]
    for g in range(groups):
        starts = [section * D + (2 * g + j) * PAIR for j in range(2) for section in range(3)]
        weight = jnp.concatenate([w_in_ref[:, at : at + PAIR] for at in starts], axis=1)
        total = total + nt(grads[g][...], weight)
    total = total.astype(BF)
    for half in range(2):

        @pl.when(part == half)
        def _():
            for i in range(some):
                outs[half * some + i][0] = total[i * block : (i + 1) * block]


def tokens_gradient(grads, grad_first_in, w_in, nblk, rows):
    total = grad_first_in.shape[0]
    block = total // rows // nblk
    tile = total // rows // 2
    return call(
        functools.partial(tokens_grad_kernel, groups=len(grads), nblk=nblk),
        "tokens_gradient",
        (2 * rows,),
        [flat(tile, D)] * len(grads) + [flat(tile, D), whole((D, 3 * D))],
        [(pl.BlockSpec((1, block, D), lambda i: (i // 2, 0, 0)), (rows, block, D), BF)] * nblk,
        flops=5e9,
    )(*grads, grad_first_in, w_in)


def place_hidden_kernel(*refs, nblk, rows, block, place):
    pieces, (hidden_ref, pooled_ref) = refs[:nblk], refs[nblk:]
    blk = place()[2]
    for i in range(nblk):
        for r in range(rows):
            at = (blk ^ i) * rows + r
            hidden_ref[pl.ds(at, 1)] = pieces[i][pl.ds(r, 1), :block, :]
            tail = pieces[i][r, block:, :].astype(F32)
            pooled_ref[pl.ds(at, 1)] = (tail[:NSEG] + tail[NSEG:]).reshape(1, NSEG, D)


def place_hidden(pieces, place=own_place):
    nblk = len(pieces)
    rows, block, _ = pieces[0].shape
    block -= 2 * NSEG
    return call(
        functools.partial(place_hidden_kernel, nblk=nblk, rows=rows, block=block, place=place),
        "place_hidden",
        (1,),
        [whole((rows, block + 2 * NSEG, D))] * nblk,
        [(whole((rows * nblk, block, D)), (rows * nblk, block, D), BF), (whole((rows * nblk, NSEG, D)), (rows * nblk, NSEG, D), F32)],
        flops=1e9,
    )(*pieces)


def place_tokens_kernel(*refs, nblk, rows, place):
    pieces, out_ref = refs[:nblk], refs[nblk]
    blk = place()[2]
    for i in range(nblk):
        for r in range(rows):
            out_ref[pl.ds((blk ^ i) * rows + r, 1)] = pieces[i][pl.ds(r, 1)].astype(F32)


def place_tokens(pieces, place=own_place):
    nblk = len(pieces)
    rows, block, _ = pieces[0].shape
    return call(
        functools.partial(place_tokens_kernel, nblk=nblk, rows=rows, place=place),
        "place_tokens",
        (1,),
        [whole((rows, block, D))] * nblk,
        [(whole((rows * nblk, block, D)), (rows * nblk, block, D), F32)],
        flops=1e9,
    )(*pieces)[0]


def unpack_kernel(half_ref, *refs, flip, place, orders):
    out_ref = refs[-1]
    core, here_block, _ = place()
    rows = half_ref.shape[1]
    count = out_ref.shape[0] // rows
    for i in range(count):
        slot = slot_of(orders, core ^ flip, pl.program_id(0) * count + i, here_block)
        out_ref[i * rows : (i + 1) * rows, :] = half_ref[slot].astype(F32)


def unpack_feed(half, by_rows, flip, before, orders, place=own_place):
    _, rows, cols = half.shape
    parts = 4
    core = lambda: place()[0] ^ flip
    tall = rows * BLOCKS
    shape, index = (
        ((2 * tall, cols), lambda q: (core() * parts + q, 0)) if by_rows else ((tall, 2 * cols), lambda q: (q, core()))
    )
    extra = [] if before is None else [before]
    return call(
        functools.partial(unpack_kernel, flip=flip, place=place, orders=orders),
        "unpack_feed",
        (parts,),
        [whole(half.shape)] + [ANY] * len(extra),
        [(pl.BlockSpec((tall // parts, cols), index), shape, F32)],
        aliases={1: 0} if extra else None,
        flops=2e9,
    )(half, *extra)[0]


def unpack_heads_kernel(half_ref, *refs, flip, place, orders):
    output_ref, input_ref, full_ref, sems = refs[-4:]
    core, here_block, _ = place()
    rows = D // BLOCKS
    wide = 3 * PAIR
    to = core ^ flip
    copies = []
    for n in range(full_ref.shape[0]):
        for i in range(BLOCKS):
            slot = slot_of(orders, to, i, here_block)
            full_ref[n, i * rows : (i + 1) * rows, :] = half_ref[slot, :, n * wide : (n + 1) * wide].astype(F32)
        if n == 0:
            lanes = pl.ds(pl.multiple_of(to * wide, 128), wide)
            copies.append(pltpu.make_async_copy(full_ref.at[0], output_ref.at[:, lanes], sems.at[0]))
            copies[-1].start()
            continue
        for section in range(3):
            lanes = pl.ds(pl.multiple_of(section * D + (2 * (n - 1) + to) * PAIR, 128), PAIR)
            part = full_ref.at[n, :, pl.ds(section * PAIR, PAIR)]
            copies.append(pltpu.make_async_copy(part, input_ref.at[:, lanes], sems.at[3 * n + section - 2]))
            copies[-1].start()
    for copy in copies:
        copy.wait()


def unpack_heads(half, flip, before, orders, place=own_place):
    extra = [] if before is None else list(before)
    count = half.shape[2] // (3 * PAIR)
    return call(
        functools.partial(unpack_heads_kernel, flip=flip, place=place, orders=orders),
        "unpack_heads",
        (1,),
        [whole(half.shape)] + [ANY] * len(extra),
        [(ANY, (D, D), F32), (ANY, (D, 3 * D), F32)],
        scratch=[pltpu.VMEM((count, D, 3 * PAIR), F32), pltpu.SemaphoreType.DMA((3 * count - 2,))],
        aliases={1: 0, 2: 1} if extra else None,
        flops=2e9,
    )(half, *extra)


def exchange(array, bits):
    nblk, nrows = lax.axis_size("blk"), lax.axis_size("rows")
    moves = {"c": (0, 1), "y": (0, 2), "x": (1, 0), "a": (2, 0), "b": (4, 0)}
    pairs = []
    for i in range(nblk * nrows):
        row, blk = divmod(i, nblk)
        bit = bits[blk & 1]
        by_row, by_blk = moves[bit] if isinstance(bit, str) else (bit, 0)
        pairs.append((i, (row ^ by_row) * nblk + (blk ^ by_blk)))
    return lax.ppermute(array, ("rows", "blk"), pairs)


def added(left, right):
    return (left.astype(F32) + right.astype(F32)).astype(BF)


class Sum:
    def __init__(self, send, keep, orders):
        self.keep = keep
        extra = []
        bit = 8
        while bit < lax.axis_size("rows"):
            extra.append(bit)
            bit *= 2
        bits = [(orders[0][t], orders[1][t]) for t in range(4)]
        halves, wholes = bits[: orders[2]], bits[orders[2] :]
        self.plan = [("half", h) for h in halves] + [("all", w) for w in wholes] + [("all", (e, e)) for e in extra]
        self.plan += [("join", h) for h in reversed(halves)] + [("end", ("c", "c"))]
        self.moving = exchange(send, self.plan[0][1])
        self.stage = 0

    def busy(self):
        return self.stage < len(self.plan)

    def step(self, marks=()):
        if not self.busy():
            return []
        kind = self.plan[self.stage][0]
        (came,) = after([self.moving], marks)
        self.stage += 1
        if kind == "end":
            self.other = came
            return [self.other]
        if kind == "half":
            if self.plan[self.stage][0] == "half":
                n = self.keep.shape[0] // 2
                send, self.keep = added(self.keep[n:], came[n:]), added(self.keep[:n], came[:n])
            else:
                send = self.now = added(self.keep, came)
        elif kind == "all":
            send = self.now = added(self.now, came)
        else:
            send = self.now = jnp.concatenate([self.now, came], axis=0)
        self.moving = exchange(send, self.plan[self.stage][1])
        return [send]

    def last(self):
        return self.stage == len(self.plan) - 1


class Vectors:
    def __init__(self, value):
        self.value = value
        bit = 8
        self.left = ["x", "a", "y", "b", "c"]
        while bit < lax.axis_size("rows"):
            self.left.append(bit)
            bit *= 2
        self.moving = None

    def step(self, marks=()):
        if self.moving is not None:
            (came,) = after([self.moving], marks)
            self.value = self.value + came
            self.moving = None
        elif marks:
            (self.value,) = after([self.value], marks)
        if self.left:
            bit = self.left.pop(0)
            self.moving = exchange(self.value, (bit, bit))
        return [self.value]

    def finish(self):
        while self.left or self.moving is not None:
            self.step()
        return self.value


def after(arrays, *marks):
    marks = [m for mark in marks for m in mark]
    return list(lax.optimization_barrier(tuple(arrays) + tuple(marks))[: len(arrays)])


def pieces_of(array, me, nblk, first=0, count=None):
    rows = array.shape[0] // nblk
    return [lax.dynamic_slice_in_dim(array, (me ^ k) * rows + first, count or rows, axis=0) for k in range(nblk)]


def swap(pieces):
    nblk = len(pieces)
    return [pieces[0]] + [
        lax.ppermute(pieces[k], "blk", [(i, i ^ k) for i in range(nblk)]) for k in range(1, nblk)
    ]


def on_device(
    tokens,
    lengths,
    input_weight,
    query_bias,
    value_bias,
    output_weight,
    output_bias,
    first_gain,
    first_shift,
    up_weight,
    up_bias,
    down_weight,
    down_bias,
    second_gain,
    second_shift,
    out_grad,
    pool_grad,
):
    nblk = lax.axis_size("blk")
    me = lax.axis_index("blk")
    rows = tokens.shape[0] // nblk
    row = lambda v: v.reshape(1, -1)
    g1, b1 = row(first_gain), row(first_shift)
    bias = row(jnp.concatenate([query_bias, jnp.zeros_like(query_bias), value_bias]))
    own_lengths = lax.dynamic_slice_in_dim(lengths, me * rows, rows, axis=0)
    own_pool = lax.dynamic_slice_in_dim(pool_grad, me * rows, rows, axis=0)
    pieces = []
    for r in range(rows):
        pieces.append(swap(after(pieces_of(tokens, me, nblk, r, 1), pieces[-1] if pieces else [])))
    grads = swap(after(pieces_of(out_grad, me, nblk), pieces[0]))
    twin = lambda a: exchange(a, ("c", "c"))
    made = ()
    for r in range(rows):
        made = attention_forward(
            own_lengths, pieces[r], input_weight, bias, output_weight, row(output_bias), rows, r, made
        )
    both, packed, first_in = made
    *hidden, active, active_outer, inner, inner_rest, low, grad_first_in, grad_mixed, branch, vec1, ups = feed(
        own_lengths, first_in, own_pool, grads, up_weight, row(up_bias), down_weight, row(down_bias), output_weight,
        g1, b1, row(second_gain), row(second_shift),
    )
    came_active, came_rest = twin(active_outer), twin(inner_rest)
    hidden = swap(hidden)

    def attention(group, marks):
        grad_packed, other, sums = attention_back(own_lengths, packed, after([grad_mixed], marks)[0], nblk, group)
        return grad_packed, other, sums[0].reshape(2, 3, PAIR)

    gp0, other0, vec_a = attention(0, [])
    active, came_active = after([active, came_active], [gp0])
    send, keep = down_gradient(active, active_outer, came_active, DOWN_ORDER)
    down = Sum(send, keep, DOWN_ORDER)
    (inner,) = after([inner], [keep] + hidden)
    send, keep = up_gradient(low, inner, came_rest, UP_ORDER)
    up = Sum(send, keep, UP_ORDER)
    came_both, came0 = [twin(a) for a in after([both, other0], [keep])]
    gp1, other1, vec_b = attention(1, [keep] + hidden)
    m = down.step([gp1])
    came1 = twin(other1)
    gp2, other2, vec_c = attention(2, m)
    came2 = twin(other2)
    m = up.step(down.step([gp2]))
    (both,) = after([both], m)
    send, keep = head_gradient(
        both, came_both, branch, came_rest, [gp0, gp1, gp2], [came0, came1, came2], HEAD_ORDER
    )
    heads = Sum(send, keep, HEAD_ORDER)
    m = up.step(down.step([keep]))
    sections = jnp.concatenate([vec_a, vec_b, vec_c], axis=0)
    vecs = Vectors(
        jnp.concatenate(
            [sections[:, 0].reshape(1, D), sections[:, 2].reshape(1, D), vec1[:6], ups[0].reshape(-1, D)], axis=0
        )
    )
    gp0, gp1, gp2, vecs.value = after([gp0, gp1, gp2, vecs.value], m)
    tokens_pieces = tokens_gradient([gp0, gp1, gp2], grad_first_in, input_weight, nblk, rows)
    m = tokens_pieces[:1]
    sums = {"d": down, "u": up, "r": heads, "v": vecs}
    held = {"down": None, "up": None, "heads": None}
    for action in TAIL:
        if action in sums:
            m = sums[action].step(m)
        elif action == "h":
            hidden_out, pooled = place_hidden(after(hidden, m))
            m = [hidden_out]
        elif action == "s":
            tokens_grad = after(tokens_pieces, m)
            halfway = twin(jnp.concatenate([tokens_grad[1], tokens_grad[3]], axis=0))
        elif action == "w":
            (halfway,) = after([halfway], m)
            far = jnp.concatenate([tokens_grad[2], halfway[rows:]], axis=0)
            m = [far]
            far = lax.ppermute(far, "blk", [(i, i ^ 2) for i in range(nblk)])
            tokens_grad = [tokens_grad[0], halfway[:rows], far[:rows], far[rows:]]
        elif action == "t":
            tokens_out = place_tokens(after(tokens_grad, m))
            m = [tokens_out]
        else:
            which, flip = divmod(int(action) - 1, 2)
            total = (down, up, heads)[which]
            while not total.last() and total.busy() or (flip and total.busy()):
                m = total.step(m)
            (half,) = after([total.other if flip else total.now], m)
            if which == 0:
                held["down"] = unpack_feed(half, True, flip, held["down"], DOWN_ORDER)
                m = [held["down"]]
            elif which == 1:
                held["up"] = unpack_feed(half, False, flip, held["up"], UP_ORDER)
                m = [held["up"]]
            else:
                held["heads"] = unpack_heads(half, flip, held["heads"], HEAD_ORDER)
                m = held["heads"]
    down_grad, up_grad, (output_grad, input_grad) = held["down"], held["up"], held["heads"]
    vecs = vecs.finish()
    return (
        hidden_out,
        pooled,
        tokens_out,
        input_grad,
        vecs[0],
        vecs[1],
        output_grad,
        vecs[4],
        vecs[2],
        vecs[3],
        up_grad,
        vecs[8:12].reshape(-1),
        down_grad,
        vecs[7],
        vecs[5],
        vecs[6],
    )


def solution(mesh):
    whole_rows = P("rows", "blk", None)
    rest = (P(),) * 13
    return jax.shard_map(
        on_device,
        mesh=mesh,
        in_specs=(whole_rows, P("rows", None)) + rest + (whole_rows, P("rows", None, None)),
        out_specs=(whole_rows, P("rows", None, None), whole_rows) + rest,
        check_vma=False,
    )
```

```python
import functools
import jax
import jax.numpy as jnp
from jax import lax
from jax.experimental import pallas as pl
from jax.experimental.pallas import tpu as pltpu
from jax.sharding import PartitionSpec as P

D = 768
H = 12
DH = 64
FF = 3072
NSEG = 8
PAIR = 2 * DH
NORM_EPS = 1e-12
BIG = 1e9
BF = jnp.bfloat16
F32 = jnp.float32
CHUNK = 768
VMEM_LIMIT = 60 * 1024 * 1024


def nn(a, b):
    return lax.dot_general(a, b, (((1,), (0,)), ((), ())), preferred_element_type=F32)


def nt(a, b):
    return lax.dot_general(a, b, (((1,), (1,)), ((), ())), preferred_element_type=F32)


def tn(a, b):
    return lax.dot_general(a, b, (((0,), (0,)), ((), ())), preferred_element_type=F32)


def col_sum(a):
    return jnp.sum(a, axis=0, keepdims=True)


def norm_parts(hidden):
    center = hidden - jnp.mean(hidden, axis=-1, keepdims=True)
    spread = jnp.mean(center * center, axis=-1, keepdims=True)
    inverse = lax.rsqrt(spread + NORM_EPS)
    return center * inverse, inverse


def norm_back(grad, gain, unit, inverse):
    scaled = grad * gain
    along = jnp.mean(scaled * unit, axis=-1, keepdims=True)
    return inverse * (scaled - jnp.mean(scaled, axis=-1, keepdims=True) - unit * along)


def segments(lengths_ref, row, length, count, nblk, me, first=0):
    shape = (count, PAIR)
    local = lax.broadcasted_iota(jnp.int32, shape, 0) + first
    block = length // nblk
    places = ((local // block) ^ me) * block + local % block
    end = jnp.int32(0)
    labels = jnp.zeros(shape, jnp.int32)
    for c in range(NSEG):
        end = end + lengths_ref[row, c]
        labels = labels + (places >= end).astype(jnp.int32)
    return labels == lax.broadcasted_iota(jnp.int32, shape, 1)


def head_masks(length):
    lane = lax.broadcasted_iota(jnp.int32, (length, PAIR), 1)
    return lane < DH, lane >= DH


PLACE = {"y": 0, "x": 1, "a": 2, "b": 3}
BLOCKS = 16
DOWN_ORDER = ("xyab", "yxab", 3)
UP_ORDER = ("xyab", "yxab", 3)
HEAD_ORDER = ("xyab", "yxab", 3)
TAIL = "duhrsdurwvudvrutvrvdrv1durv2u34vr5r6"


def own_place():
    blk = lax.axis_index("blk")
    rows = lax.axis_index("rows")
    return blk & 1, ((rows & 7) << 1) | ((blk >> 1) & 1), blk


def slot_in(order, halved, block, here):
    slot = 0
    for t, bit in enumerate(order):
        at = block ^ here if t < halved else block
        slot = slot | (((at >> PLACE[bit]) & 1) << (3 - t))
    return slot


def slot_of(orders, core, block, here):
    return jnp.where(
        core == 0, slot_in(orders[0], orders[2], block, here), slot_in(orders[1], orders[2], block, here)
    )


def hand_out(slots_ref, send_ref, keep_ref, sems):
    half = BLOCKS // 2
    copies = [
        pltpu.make_async_copy(slots_ref.at[pl.ds(half, half)], send_ref, sems.at[0]),
        pltpu.make_async_copy(slots_ref.at[pl.ds(0, half)], keep_ref, sems.at[1]),
    ]
    for c in copies:
        c.start()
    for c in copies:
        c.wait()


def whole(shape):
    return pl.BlockSpec(shape, lambda *_: (0,) * len(shape), pipeline_mode=pl.Buffered(1))


def per_row(*shape):
    return pl.BlockSpec((1,) + shape, lambda r: (r,) + (0,) * len(shape))


def flat(*shape):
    return pl.BlockSpec(shape, lambda r: (r,) + (0,) * (len(shape) - 1))


SMEM = pl.BlockSpec(memory_space=pltpu.SMEM)
ANY = pl.BlockSpec(memory_space=pl.ANY)


def slots(rows, cols):
    half = (ANY, (BLOCKS // 2, rows, cols), BF)
    return [half, half], [pltpu.VMEM((BLOCKS, rows, cols), BF), pltpu.SemaphoreType.DMA((2,))]


def shape_of(shape, dtype):
    return jax.ShapeDtypeStruct(shape, dtype)


def call(kernel, name, grid, in_specs, outs, scratch=(), flops=0, nbytes=0, aliases=None):
    return pl.pallas_call(
        kernel,
        grid=grid,
        in_specs=in_specs,
        out_specs=[o[0] for o in outs],
        out_shape=[shape_of(o[1], o[2]) for o in outs],
        scratch_shapes=scratch,
        input_output_aliases=aliases or {},
        compiler_params=pltpu.CompilerParams(vmem_limit_bytes=VMEM_LIMIT),
        cost_estimate=pl.CostEstimate(flops=int(flops), bytes_accessed=int(nbytes), transcendentals=0),
        name=name,
    )


def attention_kernel(lengths_ref, *refs, nblk, place, row):
    pieces = refs[:nblk]
    w_in_ref, bias_ref, w_out_ref, out_bias_ref = refs[nblk : nblk + 4]
    both_ref, packed_ref, first_in_ref = refs[-3:]
    block = pieces[0].shape[1]
    length = block * nblk
    for i in range(nblk):
        both_ref[pl.ds(i * block, block), :D] = pieces[i][0]
    x = both_ref[:, :D]
    for c in range(3):
        cols = pl.ds(c * D, D)
        packed_ref[0, :, cols] = (nn(x, w_in_ref[:, cols]) + bias_ref[:, cols]).astype(BF)
    hit = segments(lengths_ref, row, length, length, nblk, place()[2])
    here = jnp.where(hit, 1.0, 0.0).astype(BF)
    away = jnp.where(hit, 0.0, -BIG).astype(BF)
    masks = head_masks(length)
    for j in range(H // 2):
        q = packed_ref[0, :, pl.ds(j * PAIR, PAIR)] * jnp.asarray(DH**-0.5, BF)
        k = packed_ref[0, :, pl.ds(D + j * PAIR, PAIR)]
        v = packed_ref[0, :, pl.ds(2 * D + j * PAIR, PAIR)]
        k_aug = jnp.concatenate([k, away], axis=1)
        zero = jnp.zeros_like(q)
        weights, totals = [], []
        for h in range(2):
            s = nt(jnp.concatenate([jnp.where(masks[h], q, zero), here], axis=1), k_aug)
            e = jnp.exp(s - jnp.max(s, axis=1, keepdims=True))
            totals.append(jnp.sum(e, axis=1, keepdims=True))
            weights.append(e.astype(BF))
        values = jnp.concatenate([jnp.where(m, v, zero) for m in masks], axis=0)
        out = nn(jnp.concatenate(weights, axis=1), values) / jnp.where(masks[0], totals[0], totals[1])
        both_ref[:, pl.ds(D + j * PAIR, PAIR)] = out.astype(BF)
    branch = nn(both_ref[:, D:], w_out_ref[...]) + out_bias_ref[...]
    first_in_ref[...] = x.astype(F32) + branch


def attention_forward(lengths, pieces, w_in, bias, w_out, out_bias, rows, row, before, place=own_place):
    nblk = len(pieces)
    block = pieces[0].shape[1]
    length = block * nblk
    extra = list(before)
    return call(
        functools.partial(attention_kernel, nblk=nblk, place=place, row=row),
        "attention_forward",
        (1,),
        [SMEM] + [per_row(block, D)] * nblk + [whole((D, 3 * D)), whole((1, 3 * D)), whole((D, D)), whole((1, D))]
        + [ANY] * len(extra),
        [
            (pl.BlockSpec((length, 2 * D), lambda r: (row, 0)), (rows * length, 2 * D), BF),
            (pl.BlockSpec((1, length, 3 * D), lambda r: (row, 0, 0)), (rows, length, 3 * D), BF),
            (pl.BlockSpec((length, D), lambda r: (row, 0)), (rows * length, D), F32),
        ],
        aliases={nblk + 5 + n: n for n in range(len(extra))},
        flops=9e9,
    )(lengths, *pieces, w_in, bias, w_out, out_bias, *extra)


def gelu_both(x):
    cdf = 0.5 + 0.5 * lax.erf(x * (0.5**0.5))
    density = jnp.exp(x * x * -0.5) * 0.3989422804014327
    return x * cdf, cdf + x * density


def feed_kernel(lengths_ref, first_in_ref, pool_grad_ref, *refs, nblk, place):
    grad_pieces = refs[:nblk]
    (w_up_ref, up_bias_ref, w_down_ref, down_bias_ref, w_out_ref, g1_ref, b1_ref, g2_ref, b2_ref) = refs[nblk : nblk + 9]
    hidden = refs[nblk + 9 : 2 * nblk + 9]
    (active_own_ref, active_other_ref, inner_own_ref, other_ref, low_own_ref, grad_first_in_ref, grad_mixed_ref,
     branch_own_ref, vec_ref, up_sums_ref, slope_ref, branch_ref, pooled_ref) = refs[2 * nblk + 9 :]
    step = pl.program_id(0)
    r, part = step // 2, step % 2
    count = first_in_ref.shape[0]
    block = hidden[0].shape[1] - 2 * NSEG
    length = block * nblk
    some = nblk // 2
    half = FF // 2
    core, _, blk = place()
    chunks = [(flip, c) for flip in (1, 0) for c in range(half // CHUNK)]

    def units(flip, c):
        return pl.ds(pl.multiple_of((core ^ flip) * half + c * CHUNK, 128), CHUNK)


    unit1, inverse1 = norm_parts(first_in_ref[...])
    first = unit1 * g1_ref[...] + b1_ref[...]
    low = first.astype(BF)
    low_own_ref[...] = low
    other_ref[:, half : half + D] = low
    acc = first + down_bias_ref[...]
    for flip, c in chunks:
        cols, at = units(flip, c), pl.ds(c * CHUNK, CHUNK)
        inner = nn(low, w_up_ref[:, cols]) + up_bias_ref[:, cols]
        act, slope = gelu_both(inner)
        act = act.astype(BF)
        (active_other_ref if flip else active_own_ref)[:, at] = act
        slope_ref[flip, :, at] = slope.astype(BF)
        acc = acc + nn(act, w_down_ref[cols, :])
    unit, inverse = norm_parts(acc)
    result = unit * g2_ref[...] + b2_ref[...]
    high = result.astype(BF)
    here = jnp.where(segments(lengths_ref, r, length, count, nblk, blk, part * count), 1.0, 0.0).astype(BF)
    rest = (result - high.astype(F32)).astype(BF)
    sums = (tn(here, high) + tn(here, rest))[:NSEG]
    sub = lax.broadcasted_iota(jnp.int32, (NSEG, 1), 0)
    counts = jnp.zeros((NSEG, 1), F32)
    for c in range(NSEG):
        counts = jnp.where(sub == c, lengths_ref[r, c].astype(F32), counts)

    @pl.when(part == 0)
    def _():
        pooled_ref[...] = sums
        for i in range(some):
            hidden[i][0, :block, :] = high[i * block : (i + 1) * block]

    @pl.when(part == 1)
    def _():
        pooled = (pooled_ref[...] + sums) / counts
        pooled_high = pooled.astype(BF)
        both = jnp.concatenate([pooled_high.astype(F32), pooled - pooled_high.astype(F32)], axis=0).astype(BF)
        for i in range(some):
            hidden[some + i][0, :block, :] = high[i * block : (i + 1) * block]
        for i in range(nblk):
            hidden[i][0, block:, :] = both

    share = pool_grad_ref[0].astype(F32) / counts
    share_high = share.astype(BF)
    share_rest = (share - share_high.astype(F32)).astype(BF)
    pad = jnp.zeros((PAIR - NSEG, D), BF)
    spread = nn(here, jnp.concatenate([share_high, pad], axis=0)) + nn(here, jnp.concatenate([share_rest, pad], axis=0))
    given = jnp.where(
        part == 0,
        jnp.concatenate([g[0] for g in grad_pieces[:some]], axis=0).astype(F32),
        jnp.concatenate([g[0] for g in grad_pieces[some:]], axis=0).astype(F32),
    )
    grad = given + spread
    acc = norm_back(grad, g2_ref[...], unit, inverse)
    outer = acc.astype(BF)
    active_other_ref[:, half:] = outer
    sums2 = [col_sum(grad * unit), col_sum(grad), col_sum(outer.astype(F32))]
    @pl.when(step == 0)
    def _():
        up_sums_ref[...] = jnp.zeros_like(up_sums_ref)

    for flip, c in chunks:
        cols, at = units(flip, c), pl.ds(c * CHUNK, CHUNK)
        inner = (nt(outer, w_down_ref[cols, :]) * slope_ref[flip, :, at].astype(F32)).astype(BF)
        (other_ref if flip else inner_own_ref)[:, at] = inner
        up_sums_ref[:1, cols] += col_sum(inner.astype(F32))
        acc = acc + nt(inner, w_up_ref[:, cols])
    grad_first_in = norm_back(acc, g1_ref[...], unit1, inverse1)
    grad_first_in_ref[...] = grad_first_in
    branch = grad_first_in.astype(BF)
    branch_ref[...] = branch
    branch_own_ref[...] = branch_ref[:, pl.ds(pl.multiple_of(core * (D // 2), 128), D // 2)]
    other_ref[:, half + D :] = branch_ref[:, pl.ds(pl.multiple_of((core ^ 1) * (D // 2), 128), D // 2)]
    grad_mixed_ref[...] = nt(branch, w_out_ref[...]).astype(BF)
    sums1 = [col_sum(acc * unit1), col_sum(acc), col_sum(branch.astype(F32))]
    vec = jnp.concatenate(sums1 + sums2 + [jnp.zeros((2, D), F32)], axis=0)

    @pl.when(step == 0)
    def _():
        vec_ref[...] = vec

    @pl.when(step != 0)
    def _():
        vec_ref[...] += vec


def feed(lengths, first_in, pool_grad, grads, w_up, up_bias, w_down, down_bias, w_out, g1, b1, g2, b2, place=own_place):
    nblk = len(grads)
    rows, block, _ = grads[0].shape
    total = first_in.shape[0]
    tile = block * nblk // 2
    vec = whole((1, D))

    def row(*shape):
        return pl.BlockSpec((1,) + shape, lambda i: (i // 2,) + (0,) * len(shape))

    def out(cols, dtype=BF):
        return flat(tile, cols), (total, cols), dtype

    half = FF // 2
    return call(
        functools.partial(feed_kernel, nblk=nblk, place=place),
        "feed",
        (total // tile,),
        [SMEM, flat(tile, D), row(NSEG, D)] + [row(block, D)] * nblk
        + [whole((D, FF)), whole((1, FF)), whole((FF, D)), vec, whole((D, D)), vec, vec, vec, vec],
        [(row(block + 2 * NSEG, D), (rows, block + 2 * NSEG, D), BF)] * nblk
        + [out(half), out(half + D), out(half), out(half + D + D // 2), out(D), out(D, F32), out(D), out(D // 2),
           (whole((8, D)), (8, D), F32), (whole((8, FF)), (8, FF), F32)],
        scratch=[pltpu.VMEM((2, tile, half), BF), pltpu.VMEM((tile, D), BF), pltpu.VMEM((NSEG, D), F32)],
        flops=40e9,
    )(lengths, first_in, pool_grad, *grads, w_up, up_bias, w_down, down_bias, w_out, g1, b1, g2, b2)


def down_kernel(
    active_ref, outer_ref, came_active_ref, came_outer_ref, send_ref, keep_ref, slots_ref, sems, place, orders
):
    step = pl.program_id(0)
    core, here_block, _ = place()
    rows = slots_ref.shape[1]
    here = active_ref.shape[1] // rows
    tile = (tn(active_ref[...], outer_ref[...]) + tn(came_active_ref[...], came_outer_ref[...])).astype(BF)
    for i in range(here):
        slots_ref[slot_of(orders, core, step * here + i, here_block)] = tile[i * rows : (i + 1) * rows]

    @pl.when(step == pl.num_programs(0) - 1)
    def _():
        hand_out(slots_ref, send_ref, keep_ref, sems)


def down_gradient(active, mine, came, orders, place=own_place):
    total, half = active.shape
    outs, scratch = slots(half // BLOCKS, D)
    wide = 384
    part = pl.BlockSpec((total, wide), lambda j: (0, j))
    outer = pl.BlockSpec((total, D), lambda j: (0, half // D), pipeline_mode=pl.Buffered(1))
    return call(
        functools.partial(down_kernel, place=place, orders=orders),
        "down_gradient",
        (half // wide,),
        [part, outer, part, outer],
        outs,
        scratch=scratch,
        flops=6e9,
    )(active, mine, came, came)


def up_kernel(low_ref, inner_ref, came_low_ref, came_inner_ref, send_ref, keep_ref, slots_ref, sems, place, orders):
    step = pl.program_id(0)
    core, here_block, _ = place()
    rows = slots_ref.shape[1]
    wide = inner_ref.shape[1]
    tile = (tn(low_ref[...], inner_ref[...]) + tn(came_low_ref[...], came_inner_ref[...])).astype(BF)
    cols = pl.ds(pl.multiple_of(step * wide, 128), wide)
    for i in range(BLOCKS):
        slots_ref[slot_of(orders, core, i, here_block), :, cols] = tile[i * rows : (i + 1) * rows]

    @pl.when(step == pl.num_programs(0) - 1)
    def _():
        hand_out(slots_ref, send_ref, keep_ref, sems)


def up_gradient(low, inner, came, orders, place=own_place):
    total, half = inner.shape
    outs, scratch = slots(D // BLOCKS, half)
    wide = 512
    part = pl.BlockSpec((total, wide), lambda j: (0, j))
    came_low = pl.BlockSpec((total, D), lambda j: (0, half // D), pipeline_mode=pl.Buffered(1))
    return call(
        functools.partial(up_kernel, place=place, orders=orders),
        "up_gradient",
        (half // wide,),
        [whole((total, D)), part, came_low, part],
        outs,
        scratch=scratch,
        flops=6e9,
    )(low, inner, came, came)


def attention_back_kernel(lengths_ref, *refs, nblk, place):
    q_ref, k_ref, v_ref, gm_ref, grads_ref, other_ref, vec_ref = refs
    r = pl.program_id(0)
    core, _, blk = place()
    length = q_ref.shape[1]
    wide = 3 * PAIR
    hit = segments(lengths_ref, r, length, length, nblk, blk)
    here = jnp.where(hit, 1.0, 0.0).astype(BF)
    away = jnp.where(hit, 0.0, -BIG).astype(BF)
    masks = head_masks(length)
    scale = DH**-0.5
    for j in range(2):
        lanes = slice(j * PAIR, (j + 1) * PAIR)
        q = q_ref[0, :, lanes] * jnp.asarray(scale, BF)
        k = k_ref[0, :, lanes]
        v = v_ref[0, :, lanes]
        gm = gm_ref[:, lanes]
        k_aug = jnp.concatenate([k, away], axis=1)
        zero = jnp.zeros_like(q)
        probs, slopes, queries, keys, mixes = [], [], [], [], []
        for h in range(2):
            qh = jnp.where(masks[h], q, zero)
            kh = jnp.where(masks[h], k, zero)
            gmh = jnp.where(masks[h], gm, zero)
            s = nt(k_aug, jnp.concatenate([qh, here], axis=1))
            e = jnp.exp(s - jnp.max(s, axis=0, keepdims=True))
            p = e * (1.0 / jnp.sum(e, axis=0, keepdims=True))
            gp = nt(v, gmh)
            delta = jnp.sum(gp * p, axis=0, keepdims=True)
            slopes.append((p * (gp - delta)).astype(BF))
            probs.append(p.astype(BF))
            queries.append(qh)
            keys.append(kh)
            mixes.append(gmh)
        both = jnp.concatenate(slopes, axis=1)
        gv = nn(jnp.concatenate(probs, axis=1), jnp.concatenate(mixes, axis=0))
        gk = nn(both, jnp.concatenate(queries, axis=0))
        gq = nn(jnp.concatenate([x.T for x in keys], axis=1), jnp.concatenate(slopes, axis=0)).T
        grads = jnp.concatenate([(gq * scale).astype(BF), gk.astype(BF), gv.astype(BF)], axis=1)
        at = pl.ds(j * wide, wide)
        grads_ref[:, at] = grads
        sums = jnp.concatenate([col_sum(grads.astype(F32)), jnp.zeros((7, wide), F32)], axis=0)

        @pl.when(r == 0)
        def _():
            vec_ref[:, at] = sums

        @pl.when(r != 0)
        def _():
            vec_ref[:, at] += sums

    other_ref[...] = grads_ref[:, pl.ds(pl.multiple_of((core ^ 1) * wide, 128), wide)]


def attention_back(lengths, packed, grad_mixed, nblk, group, place=own_place):
    rows, length, _ = packed.shape
    total = rows * length

    def pairs(section):
        return pl.BlockSpec((1, length, 2 * PAIR), lambda r: (r, 0, section * (H // 4) + group))

    return call(
        functools.partial(attention_back_kernel, nblk=nblk, place=place),
        "attention_back",
        (rows,),
        [SMEM, pairs(0), pairs(1), pairs(2), pl.BlockSpec((length, 2 * PAIR), lambda r: (r, group))],
        [(flat(length, D), (total, D), BF), (flat(length, D // 2), (total, D // 2), BF), (whole((8, D)), (8, D), F32)],
        flops=12e9,
    )(lengths, packed, packed, packed, grad_mixed)


def head_gradient_kernel(
    both_ref, came_both_ref, branch_ref, came_rest_ref, *refs, groups, place, orders
):
    rights, came_rights = refs[:groups], refs[groups : 2 * groups]
    send_ref, keep_ref, held, right_held, slots_ref, sems, left_sems, right_sems = refs[2 * groups :]
    core, here_block, _ = place()
    wide = D // 2
    own = pl.ds(pl.multiple_of(core * wide, 128), wide)
    tokens, mixed, tail = pl.ds(0, D), pl.ds(D, D), pl.ds(came_rest_ref.shape[1] - wide, wide)
    pairs = [(branch_ref, came_rest_ref.at[:, tail])] + [(a.at[:, own], b) for a, b in zip(rights, came_rights)]
    left_loads = [
        pltpu.make_async_copy(ref.at[:, lanes], held.at[n], left_sems.at[n])
        for n, (ref, lanes) in enumerate(
            ((both_ref, mixed), (came_both_ref, mixed), (both_ref, tokens), (came_both_ref, tokens))
        )
    ]
    right_loads = [
        pltpu.make_async_copy(ref, right_held.at[n, side], right_sems.at[2 * n + side])
        for n, pair in enumerate(pairs)
        for side, ref in enumerate(pair)
    ]
    for load in left_loads[:2] + right_loads[:2] + left_loads[2:] + right_loads[2:]:
        load.start()
    rows = D // BLOCKS
    for first, last, at in ((0, 1, 0), (1, groups + 1, 2)):
        for load in left_loads[at : at + 2] + right_loads[2 * first : 2 * last]:
            load.wait()
        here, there = [jnp.concatenate([right_held[n, side] for n in range(first, last)], axis=1) for side in range(2)]
        tile = (tn(held[at], here) + tn(held[at + 1], there)).astype(BF)
        for i in range(BLOCKS):
            slot = slot_of(orders, core, i, here_block)
            slots_ref[slot, :, first * wide : last * wide] = tile[i * rows : (i + 1) * rows]
    hand_out(slots_ref, send_ref, keep_ref, sems)


def head_gradient(both, came_both, branch, came_rest, grads, came_grads, orders, place=own_place):
    total = both.shape[0]
    groups = len(grads)
    wide = D // 2
    outs, scratch = slots(D // BLOCKS, (groups + 1) * wide)
    return call(
        functools.partial(head_gradient_kernel, groups=groups, place=place, orders=orders),
        "head_gradient",
        (1,),
        [ANY] * (4 + 2 * groups),
        outs,
        scratch=[pltpu.VMEM((4, total, D), BF), pltpu.VMEM((groups + 1, 2, total, wide), BF)] + scratch
        + [pltpu.SemaphoreType.DMA((4,)), pltpu.SemaphoreType.DMA((2 * groups + 2,))],
        flops=6e9,
    )(both, came_both, branch, came_rest, *grads, *came_grads)


def tokens_grad_kernel(*refs, groups, nblk):
    grads = refs[:groups]
    grad_first_in_ref, w_in_ref = refs[groups : groups + 2]
    outs = refs[groups + 2 : groups + 2 + nblk]
    part = pl.program_id(0) % 2
    block = outs[0].shape[1]
    some = nblk // 2
    total = grad_first_in_ref[...]
    for g in range(groups):
        starts = [section * D + (2 * g + j) * PAIR for j in range(2) for section in range(3)]
        weight = jnp.concatenate([w_in_ref[:, at : at + PAIR] for at in starts], axis=1)
        total = total + nt(grads[g][...], weight)
    total = total.astype(BF)
    for half in range(2):

        @pl.when(part == half)
        def _():
            for i in range(some):
                outs[half * some + i][0] = total[i * block : (i + 1) * block]


def tokens_gradient(grads, grad_first_in, w_in, nblk, rows):
    total = grad_first_in.shape[0]
    block = total // rows // nblk
    tile = total // rows // 2
    return call(
        functools.partial(tokens_grad_kernel, groups=len(grads), nblk=nblk),
        "tokens_gradient",
        (2 * rows,),
        [flat(tile, D)] * len(grads) + [flat(tile, D), whole((D, 3 * D))],
        [(pl.BlockSpec((1, block, D), lambda i: (i // 2, 0, 0)), (rows, block, D), BF)] * nblk,
        flops=5e9,
    )(*grads, grad_first_in, w_in)


def place_hidden_kernel(*refs, nblk, rows, block, place):
    pieces, (hidden_ref, pooled_ref) = refs[:nblk], refs[nblk:]
    blk = place()[2]
    for i in range(nblk):
        for r in range(rows):
            at = (blk ^ i) * rows + r
            hidden_ref[pl.ds(at, 1)] = pieces[i][pl.ds(r, 1), :block, :]
            tail = pieces[i][r, block:, :].astype(F32)
            pooled_ref[pl.ds(at, 1)] = (tail[:NSEG] + tail[NSEG:]).reshape(1, NSEG, D)


def place_hidden(pieces, place=own_place):
    nblk = len(pieces)
    rows, block, _ = pieces[0].shape
    block -= 2 * NSEG
    return call(
        functools.partial(place_hidden_kernel, nblk=nblk, rows=rows, block=block, place=place),
        "place_hidden",
        (1,),
        [whole((rows, block + 2 * NSEG, D))] * nblk,
        [(whole((rows * nblk, block, D)), (rows * nblk, block, D), BF), (whole((rows * nblk, NSEG, D)), (rows * nblk, NSEG, D), F32)],
        flops=1e9,
    )(*pieces)


def place_tokens_kernel(*refs, nblk, rows, place):
    pieces, out_ref = refs[:nblk], refs[nblk]
    blk = place()[2]
    for i in range(nblk):
        for r in range(rows):
            out_ref[pl.ds((blk ^ i) * rows + r, 1)] = pieces[i][pl.ds(r, 1)].astype(F32)


def place_tokens(pieces, place=own_place):
    nblk = len(pieces)
    rows, block, _ = pieces[0].shape
    return call(
        functools.partial(place_tokens_kernel, nblk=nblk, rows=rows, place=place),
        "place_tokens",
        (1,),
        [whole((rows, block, D))] * nblk,
        [(whole((rows * nblk, block, D)), (rows * nblk, block, D), F32)],
        flops=1e9,
    )(*pieces)[0]


def unpack_kernel(half_ref, *refs, flip, place, orders):
    out_ref = refs[-1]
    core, here_block, _ = place()
    rows = half_ref.shape[1]
    count = out_ref.shape[0] // rows
    for i in range(count):
        slot = slot_of(orders, core ^ flip, pl.program_id(0) * count + i, here_block)
        out_ref[i * rows : (i + 1) * rows, :] = half_ref[slot].astype(F32)


def unpack_feed(half, by_rows, flip, before, orders, place=own_place):
    _, rows, cols = half.shape
    parts = 4
    core = lambda: place()[0] ^ flip
    tall = rows * BLOCKS
    shape, index = (
        ((2 * tall, cols), lambda q: (core() * parts + q, 0)) if by_rows else ((tall, 2 * cols), lambda q: (q, core()))
    )
    extra = [] if before is None else [before]
    return call(
        functools.partial(unpack_kernel, flip=flip, place=place, orders=orders),
        "unpack_feed",
        (parts,),
        [whole(half.shape)] + [ANY] * len(extra),
        [(pl.BlockSpec((tall // parts, cols), index), shape, F32)],
        aliases={1: 0} if extra else None,
        flops=2e9,
    )(half, *extra)[0]


def unpack_heads_kernel(half_ref, *refs, flip, place, orders):
    output_ref, input_ref, full_ref, sems = refs[-4:]
    core, here_block, _ = place()
    rows = D // BLOCKS
    wide = 3 * PAIR
    to = core ^ flip
    copies = []
    for n in range(full_ref.shape[0]):
        for i in range(BLOCKS):
            slot = slot_of(orders, to, i, here_block)
            full_ref[n, i * rows : (i + 1) * rows, :] = half_ref[slot, :, n * wide : (n + 1) * wide].astype(F32)
        if n == 0:
            lanes = pl.ds(pl.multiple_of(to * wide, 128), wide)
            copies.append(pltpu.make_async_copy(full_ref.at[0], output_ref.at[:, lanes], sems.at[0]))
            copies[-1].start()
            continue
        for section in range(3):
            lanes = pl.ds(pl.multiple_of(section * D + (2 * (n - 1) + to) * PAIR, 128), PAIR)
            part = full_ref.at[n, :, pl.ds(section * PAIR, PAIR)]
            copies.append(pltpu.make_async_copy(part, input_ref.at[:, lanes], sems.at[3 * n + section - 2]))
            copies[-1].start()
    for copy in copies:
        copy.wait()


def unpack_heads(half, flip, before, orders, place=own_place):
    extra = [] if before is None else list(before)
    count = half.shape[2] // (3 * PAIR)
    return call(
        functools.partial(unpack_heads_kernel, flip=flip, place=place, orders=orders),
        "unpack_heads",
        (1,),
        [whole(half.shape)] + [ANY] * len(extra),
        [(ANY, (D, D), F32), (ANY, (D, 3 * D), F32)],
        scratch=[pltpu.VMEM((count, D, 3 * PAIR), F32), pltpu.SemaphoreType.DMA((3 * count - 2,))],
        aliases={1: 0, 2: 1} if extra else None,
        flops=2e9,
    )(half, *extra)


def exchange(array, bits):
    nblk, nrows = lax.axis_size("blk"), lax.axis_size("rows")
    moves = {"c": (0, 1), "y": (0, 2), "x": (1, 0), "a": (2, 0), "b": (4, 0)}
    pairs = []
    for i in range(nblk * nrows):
        row, blk = divmod(i, nblk)
        bit = bits[blk & 1]
        by_row, by_blk = moves[bit] if isinstance(bit, str) else (bit, 0)
        pairs.append((i, (row ^ by_row) * nblk + (blk ^ by_blk)))
    return lax.ppermute(array, ("rows", "blk"), pairs)


def added(left, right):
    return (left.astype(F32) + right.astype(F32)).astype(BF)


class Sum:
    def __init__(self, send, keep, orders):
        self.keep = keep
        extra = []
        bit = 8
        while bit < lax.axis_size("rows"):
            extra.append(bit)
            bit *= 2
        bits = [(orders[0][t], orders[1][t]) for t in range(4)]
        halves, wholes = bits[: orders[2]], bits[orders[2] :]
        self.plan = [("half", h) for h in halves] + [("all", w) for w in wholes] + [("all", (e, e)) for e in extra]
        self.plan += [("join", h) for h in reversed(halves)] + [("end", ("c", "c"))]
        self.moving = exchange(send, self.plan[0][1])
        self.stage = 0

    def busy(self):
        return self.stage < len(self.plan)

    def step(self, marks=()):
        if not self.busy():
            return []
        kind = self.plan[self.stage][0]
        (came,) = after([self.moving], marks)
        self.stage += 1
        if kind == "end":
            self.other = came
            return [self.other]
        if kind == "half":
            if self.plan[self.stage][0] == "half":
                n = self.keep.shape[0] // 2
                send, self.keep = added(self.keep[n:], came[n:]), added(self.keep[:n], came[:n])
            else:
                send = self.now = added(self.keep, came)
        elif kind == "all":
            send = self.now = added(self.now, came)
        else:
            send = self.now = jnp.concatenate([self.now, came], axis=0)
        self.moving = exchange(send, self.plan[self.stage][1])
        return [send]

    def last(self):
        return self.stage == len(self.plan) - 1


class Vectors:
    def __init__(self, value):
        self.value = value
        bit = 8
        self.left = ["x", "a", "y", "b", "c"]
        while bit < lax.axis_size("rows"):
            self.left.append(bit)
            bit *= 2
        self.moving = None

    def step(self, marks=()):
        if self.moving is not None:
            (came,) = after([self.moving], marks)
            self.value = self.value + came
            self.moving = None
        elif marks:
            (self.value,) = after([self.value], marks)
        if self.left:
            bit = self.left.pop(0)
            self.moving = exchange(self.value, (bit, bit))
        return [self.value]

    def finish(self):
        while self.left or self.moving is not None:
            self.step()
        return self.value


def after(arrays, *marks):
    marks = [m for mark in marks for m in mark]
    return list(lax.optimization_barrier(tuple(arrays) + tuple(marks))[: len(arrays)])


def pieces_of(array, me, nblk, first=0, count=None):
    rows = array.shape[0] // nblk
    return [lax.dynamic_slice_in_dim(array, (me ^ k) * rows + first, count or rows, axis=0) for k in range(nblk)]


def swap(pieces):
    nblk = len(pieces)
    return [pieces[0]] + [
        lax.ppermute(pieces[k], "blk", [(i, i ^ k) for i in range(nblk)]) for k in range(1, nblk)
    ]


def on_device(
    tokens,
    lengths,
    input_weight,
    query_bias,
    value_bias,
    output_weight,
    output_bias,
    first_gain,
    first_shift,
    up_weight,
    up_bias,
    down_weight,
    down_bias,
    second_gain,
    second_shift,
    out_grad,
    pool_grad,
):
    nblk = lax.axis_size("blk")
    me = lax.axis_index("blk")
    rows = tokens.shape[0] // nblk
    row = lambda v: v.reshape(1, -1)
    g1, b1 = row(first_gain), row(first_shift)
    bias = row(jnp.concatenate([query_bias, jnp.zeros_like(query_bias), value_bias]))
    own_lengths = lax.dynamic_slice_in_dim(lengths, me * rows, rows, axis=0)
    own_pool = lax.dynamic_slice_in_dim(pool_grad, me * rows, rows, axis=0)
    pieces = []
    for r in range(rows):
        pieces.append(swap(after(pieces_of(tokens, me, nblk, r, 1), pieces[-1] if pieces else [])))
    grads = swap(after(pieces_of(out_grad, me, nblk), pieces[0]))
    twin = lambda a: exchange(a, ("c", "c"))
    made = ()
    for r in range(rows):
        made = attention_forward(
            own_lengths, pieces[r], input_weight, bias, output_weight, row(output_bias), rows, r, made
        )
    both, packed, first_in = made
    *hidden, active, active_outer, inner, inner_rest, low, grad_first_in, grad_mixed, branch, vec1, ups = feed(
        own_lengths, first_in, own_pool, grads, up_weight, row(up_bias), down_weight, row(down_bias), output_weight,
        g1, b1, row(second_gain), row(second_shift),
    )
    came_active, came_rest = twin(active_outer), twin(inner_rest)
    hidden = swap(hidden)

    def attention(group, marks):
        grad_packed, other, sums = attention_back(own_lengths, packed, after([grad_mixed], marks)[0], nblk, group)
        return grad_packed, other, sums[0].reshape(2, 3, PAIR)

    gp0, other0, vec_a = attention(0, [])
    active, came_active = after([active, came_active], [gp0])
    send, keep = down_gradient(active, active_outer, came_active, DOWN_ORDER)
    down = Sum(send, keep, DOWN_ORDER)
    (inner,) = after([inner], [keep] + hidden)
    send, keep = up_gradient(low, inner, came_rest, UP_ORDER)
    up = Sum(send, keep, UP_ORDER)
    came_both, came0 = [twin(a) for a in after([both, other0], [keep])]
    gp1, other1, vec_b = attention(1, [keep] + hidden)
    m = down.step([gp1])
    came1 = twin(other1)
    gp2, other2, vec_c = attention(2, m)
    came2 = twin(other2)
    m = up.step(down.step([gp2]))
    (both,) = after([both], m)
    send, keep = head_gradient(
        both, came_both, branch, came_rest, [gp0, gp1, gp2], [came0, came1, came2], HEAD_ORDER
    )
    heads = Sum(send, keep, HEAD_ORDER)
    m = up.step(down.step([keep]))
    sections = jnp.concatenate([vec_a, vec_b, vec_c], axis=0)
    vecs = Vectors(
        jnp.concatenate(
            [sections[:, 0].reshape(1, D), sections[:, 2].reshape(1, D), vec1[:6], ups[0].reshape(-1, D)], axis=0
        )
    )
    gp0, gp1, gp2, vecs.value = after([gp0, gp1, gp2, vecs.value], m)
    tokens_pieces = tokens_gradient([gp0, gp1, gp2], grad_first_in, input_weight, nblk, rows)
    m = tokens_pieces[:1]
    sums = {"d": down, "u": up, "r": heads, "v": vecs}
    held = {"down": None, "up": None, "heads": None}
    for action in TAIL:
        if action in sums:
            m = sums[action].step(m)
        elif action == "h":
            hidden_out, pooled = place_hidden(after(hidden, m))
            m = [hidden_out]
        elif action == "s":
            tokens_grad = after(tokens_pieces, m)
            halfway = twin(jnp.concatenate([tokens_grad[1], tokens_grad[3]], axis=0))
        elif action == "w":
            (halfway,) = after([halfway], m)
            far = jnp.concatenate([tokens_grad[2], halfway[rows:]], axis=0)
            m = [far]
            far = lax.ppermute(far, "blk", [(i, i ^ 2) for i in range(nblk)])
            tokens_grad = [tokens_grad[0], halfway[:rows], far[:rows], far[rows:]]
        elif action == "t":
            tokens_out = place_tokens(after(tokens_grad, m))
            m = [tokens_out]
        else:
            which, flip = divmod(int(action) - 1, 2)
            total = (down, up, heads)[which]
            while not total.last() and total.busy() or (flip and total.busy()):
                m = total.step(m)
            (half,) = after([total.other if flip else total.now], m)
            if which == 0:
                held["down"] = unpack_feed(half, True, flip, held["down"], DOWN_ORDER)
                m = [held["down"]]
            elif which == 1:
                held["up"] = unpack_feed(half, False, flip, held["up"], UP_ORDER)
                m = [held["up"]]
            else:
                held["heads"] = unpack_heads(half, flip, held["heads"], HEAD_ORDER)
                m = held["heads"]
    down_grad, up_grad, (output_grad, input_grad) = held["down"], held["up"], held["heads"]
    vecs = vecs.finish()
    return (
        hidden_out,
        pooled,
        tokens_out,
        input_grad,
        vecs[0],
        vecs[1],
        output_grad,
        vecs[4],
        vecs[2],
        vecs[3],
        up_grad,
        vecs[8:12].reshape(-1),
        down_grad,
        vecs[7],
        vecs[5],
        vecs[6],
    )


def solution(mesh):
    whole_rows = P("rows", "blk", None)
    rest = (P(),) * 13
    return jax.shard_map(
        on_device,
        mesh=mesh,
        in_specs=(whole_rows, P("rows", None)) + rest + (whole_rows, P("rows", None, None)),
        out_specs=(whole_rows, P("rows", None, None), whole_rows) + rest,
        check_vma=False,
    )
```
